32 devices in a mesh: dp: 16 (over z, y, x), mlp: 2 (over core).
Axes of the slice: x: 2, y: 2, z: 4, core: 2. Of those that a mesh axis runs over, the one named last changes fastest.
Arguments:
- tokens: bfloat16 [64, 197, 768], P(('dp', 'mlp')), may hold values from -6 to 6
- cotangent: bfloat16 [64, 197, 768], P(('dp', 'mlp')), may hold values from -6 to 6
- prompts: float32 [2, 50, 768], P(None, None, 'mlp'), may hold values from -6 to 6
- first_moment: float32 [2, 50, 768], P(None, None, 'mlp'), may hold values from -0.005859375 to 0.005859375
- second_moment: float32 [2, 50, 768], P(None, None, 'mlp'), may hold values from 1.3020833e-08 to 5.2083333e-08
- norm_params: float32 [2, 4, 768], replicated, may hold values from -1.2 to 1.9, as said below
- bias_rows: float32 [2, 4, 768], replicated, may hold values from -1.5 to 1.5
- qkv_weight: bfloat16 [2, 768, 2304], replicated, may hold values from -0.21875 to 0.21875
- out_weight: bfloat16 [2, 768, 768], replicated, may hold values from -0.625 to 0.625
- up_weight: bfloat16 [2, 768, 3072], P(None, None, 'mlp'), may hold values from -0.21875 to 0.21875
- up_bias: float32 [2, 3072], P(None, 'mlp'), may hold values from -1.5 to 1.5
- down_weight: bfloat16 [2, 3072, 768], P(None, 'mlp'), may hold values from -0.109375 to 0.109375
Outputs:
- activations: bfloat16 [64, 197, 768], P(('dp', 'mlp'))
- input_grad: float32 [64, 197, 768], P(('dp', 'mlp'))
- prompt_grad: float32 [2, 50, 768], P(None, None, 'mlp')
- grad_norm: float32 [], replicated
- new_first: float32 [2, 50, 768], P(None, None, 'mlp')
- new_second: float32 [2, 50, 768], P(None, None, 'mlp')
- new_prompts: float32 [2, 50, 768], P(None, None, 'mlp')
The draws below stay inside these ranges and needn't reach their ends.
Inputs may be any that keep to these rules, and one draw needn't show every extreme that they name: `norm_params`: gains in rows 0 and 2 of the middle dimension are positive.
All inputs are finite; a program needn't handle non-finite values.
Results may differ from the reference program's by a relative error of at most 0.025.
Values may be sent and summed in bfloat16 or wider, within the bound.
A program may use at most 128 MiB of HBM per device.

```python
import math
import jax
import jax.numpy as jnp
from jax import lax

D = 768
HEADS = 12
HEAD_DIM = 64
FF = 3072
PROMPTS = 50
IMG_TOK = 197
LAYERS = 2
STEP = 10
IMAGES = 64


def draw_norm_params(key, part):
    key = jax.random.fold_in(key, 11)
    keys = jax.random.split(key, 4)
    ramp = jnp.arange(D, dtype=jnp.float32) / (D - 1)
    rising = 0.5 + ramp
    rough = jax.random.uniform(keys[0], (LAYERS, D), jnp.float32, 0.8, 1.25)
    gain_one = rising * rough
    shift_one = jnp.clip(0.3 * jax.random.normal(keys[1], (LAYERS, D), jnp.float32), -1.2, 1.2)
    gain_two = jax.random.uniform(keys[2], (LAYERS, D), jnp.float32, 0.6, 1.4)
    shift_two = jnp.clip(0.3 * jax.random.normal(keys[3], (LAYERS, D), jnp.float32), -1.2, 1.2)
    return jnp.stack([gain_one, shift_one, gain_two, shift_two], axis=1).astype(jnp.float32)


def block_scale(key, shape, cuts, low, top_value):
    level, own = 1.0, jax.random.fold_in(key, 6)
    for position, parts in cuts:
        steps = jnp.exp(jax.random.uniform(jax.random.fold_in(own, position), (parts,), jnp.float32, low / len(cuts), top_value / len(cuts)))
        level = level * jnp.repeat(steps, shape[position] // parts).reshape([-1 if axis == position else 1 for axis in range(len(shape))])
    return level


def bell_draw(own_key, dims, scale, reach, cuts=(), held_as=jnp.bfloat16):
    values = jax.random.normal(own_key, dims, jnp.float32) * scale
    if len(cuts) > 0:
        values = block_scale(own_key, dims, cuts, -0.22, 0.18) * values
    return jnp.clip(values, min=-reach, max=reach).astype(held_as)


def setup_inputs(seed: int = 0) -> dict:
    splits = jax.random.split(jax.random.key(seed), 13)
    return {
        "tokens": bell_draw(splits[0], (IMAGES, IMG_TOK, D), 1.0, 6.0, ((0, 32),)),
        "cotangent": bell_draw(splits[1], (IMAGES, IMG_TOK, D), 1.0, 6.0, ((0, 32),)),
        "prompts": bell_draw(splits[2], (LAYERS, PROMPTS, D), 1.0, 6.0, ((2, 2),), jnp.float32),
        "first_moment": bell_draw(splits[3], (LAYERS, PROMPTS, D), (0.11 * (LAYERS * PROMPTS * D) ** -0.5), 0.005859375, ((2, 2),), jnp.float32),
        "second_moment": jnp.clip(jnp.exp(math.log(5.208333320183556e-08) - 1.3862944 * jax.random.uniform(splits[4], (LAYERS, PROMPTS, D), jnp.float32) ** block_scale(splits[4], (LAYERS, PROMPTS, D), ((2, 2),), -0.2, 0.2)), 1.302083330045889e-08, 5.208333320183556e-08),
        "norm_params": draw_norm_params(jax.random.fold_in(splits[12], 71), 0),
        "bias_rows": bell_draw(splits[6], (LAYERS, 4, D), 0.3, 1.5, (), jnp.float32),
        "qkv_weight": bell_draw(splits[7], (LAYERS, D, 3 * D), D ** -0.5, 0.21875),
        "out_weight": bell_draw(splits[8], (LAYERS, D, D), (D // 8) ** -0.5, 0.625),
        "up_weight": bell_draw(splits[9], (LAYERS, D, FF), D ** -0.5, 0.21875, ((2, 2),)),
        "up_bias": bell_draw(splits[10], (LAYERS, FF), 0.3, 1.5, ((1, 2),), jnp.float32),
        "down_weight": bell_draw(splits[11], (LAYERS, FF, D), FF ** -0.5, 0.109375, ((1, 2),)),
    }


@jax.custom_vjp
def low(v):
    return lax.optimization_barrier(v.astype(jnp.bfloat16)).astype(jnp.float32)

@jax.custom_vjp
def low_back(v):
    return v

def low_keep(v):
    return (low(v), None)

def low_pass(kept, grad):
    return (grad,)

def back_keep(v):
    return (v, None)

def back_low(kept, grad):
    return (low(grad),)
low.defvjp(low_keep, low_pass)
low_back.defvjp(back_keep, back_low)
norm_eps = 1e-06
clip_limit = 1.0
beta_one = 0.9
beta_two = 0.999
learn_rate = 1.5
weight_decay = 0.05
adam_eps = 1e-08

def matmul_hi(form, left, right):
    return jnp.einsum(form, left, right, precision=lax.Precision.HIGHEST)

def layer_norm(values, gain, shift):
    centre = values - lax.optimization_barrier(jnp.mean(values, axis=-1, keepdims=True))
    spread = lax.optimization_barrier(jnp.mean(centre * centre, axis=-1, keepdims=True))
    return centre * lax.rsqrt(spread + norm_eps) * gain + shift

def block_forward(stream, prompt, norm_rows, bias_set, qkv_w, out_w, up_w, up_b, down_w):
    images = stream.shape[0]
    sequence = jnp.concatenate([jnp.broadcast_to(prompt, (images, PROMPTS, D)), stream], axis=1)
    normed = low(layer_norm(sequence, norm_rows[0], norm_rows[1]))
    queries = low(low_back(matmul_hi('bsd,de->bse', normed[:, PROMPTS:], qkv_w[:, :D]) + bias_set[0]))
    keyval = matmul_hi('btd,de->bte', normed, qkv_w[:, D:])
    key_rows = low(low_back(keyval[..., :D]))
    value_rows = low(low_back(keyval[..., D:] + bias_set[1]))
    total_len = PROMPTS + IMG_TOK
    query_heads = queries.reshape(images, IMG_TOK, HEADS, HEAD_DIM)
    key_heads = key_rows.reshape(images, total_len, HEADS, HEAD_DIM)
    value_heads = value_rows.reshape(images, total_len, HEADS, HEAD_DIM)
    scores = low_back(matmul_hi('bshe,bthe->bhst', query_heads, key_heads) * HEAD_DIM ** (-0.5))
    probs = low(jnp.exp(scores - jax.nn.logsumexp(scores, axis=-1, keepdims=True)))
    mixed = low(low_back(matmul_hi('bhst,bthe->bshe', probs, value_heads).reshape(images, IMG_TOK, D)))
    branch = low_back(matmul_hi('bsd,de->bse', mixed, out_w) + bias_set[2])
    hidden = stream + branch
    normed_two = low(layer_norm(hidden, norm_rows[2], norm_rows[3]))
    pre_act = low_back(matmul_hi('bsd,df->bsf', normed_two, up_w) + up_b)
    activated = low(jax.nn.gelu(pre_act, approximate=False))
    mlp_part = low_back(matmul_hi('bsf,fd->bsd', activated, down_w) + bias_set[3])
    return hidden + mlp_part

def reference(tokens, cotangent, prompts, first_moment, second_moment, norm_params, bias_rows, qkv_weight, out_weight, up_weight, up_bias, down_weight):
    qkv_f = qkv_weight.astype(jnp.float32)
    out_f = out_weight.astype(jnp.float32)
    up_f = up_weight.astype(jnp.float32)
    down_f = down_weight.astype(jnp.float32)
    group_size = math.gcd(IMAGES, 16)
    groups = IMAGES // group_size
    token_groups = tokens.astype(jnp.float32).reshape(groups, group_size, IMG_TOK, D)
    cot_groups = cotangent.astype(jnp.float32).reshape(groups, group_size, IMG_TOK, D)

    def stack_forward(prompt_set, stream):
        for depth in range(LAYERS):
            stream = block_forward(stream, prompt_set[depth], norm_params[depth], bias_rows[depth], qkv_f[depth], out_f[depth], up_f[depth], up_bias[depth], down_f[depth])
        return stream

    def scan_step(grad_total, batch_pair):
        stream, cot_rows = batch_pair
        result, pullback = jax.vjp(stack_forward, prompts, stream)
        grad_prompt, grad_stream = pullback(cot_rows)
        return (grad_total + grad_prompt, (result.astype(jnp.bfloat16), grad_stream))
    prompt_grad, (outputs, input_rows) = lax.scan(scan_step, jnp.zeros(prompts.shape, jnp.float32), (token_groups, cot_groups))
    activations = outputs.reshape(IMAGES, IMG_TOK, D)
    input_grad = input_rows.reshape(IMAGES, IMG_TOK, D)
    grad_norm = jnp.sqrt(jnp.sum(prompt_grad * prompt_grad))
    factor = jnp.minimum(1.0, clip_limit / (grad_norm + 1e-06))
    clipped = prompt_grad * factor
    new_first = beta_one * first_moment + (1.0 - beta_one) * clipped
    new_second = beta_two * second_moment + (1.0 - beta_two) * clipped * clipped
    fix_first = 1.0 - beta_one ** STEP
    fix_second = 1.0 - beta_two ** STEP
    new_prompts = prompts - learn_rate * (new_first / fix_first / (jnp.sqrt(new_second / fix_second) + adam_eps) + weight_decay * prompts)
    return (activations, input_grad, prompt_grad, grad_norm, new_first, new_second, new_prompts)
```

```python
import functools

import jax
import jax.numpy as jnp
from jax import lax
from jax.experimental import pallas as pl
from jax.experimental.pallas import tpu as pltpu
from jax.sharding import PartitionSpec as P

HEADS = 12
STEP = 10
MESH = pl.DeviceIdType.MESH
VMEM = pltpu.VMEM
DMA = pltpu.SemaphoreType.DMA
BF16 = jnp.bfloat16
F32 = jnp.float32

norm_eps = 1e-06
clip_limit = 1.0
beta_one = 0.9
beta_two = 0.999
learn_rate = 1.5
weight_decay = 0.05
adam_eps = 1e-08
LOG2E = 1.4426950408889634


def up_to(value, step):
    return -(-value // step) * step


def mm(left, right):
    return jnp.dot(left, right, preferred_element_type=F32)


def mm_nt(left, right):
    return lax.dot_general(left, right, (((1,), (1,)), ((), ())), preferred_element_type=F32)


def mm_tn(left, right):
    return lax.dot_general(left, right, (((0,), (0,)), ((), ())), preferred_element_type=F32)


def rows_loop(count, step, body, unroll=1):
    def one(i, carry):
        body(pl.multiple_of(i * step, step))
        return carry

    lax.fori_loop(0, count // step, one, 0, unroll=unroll)


def main_kernel(
    dims,
    tok_hbm,
    cot_hbm,
    prompts_hbm,
    norms_hbm,
    bias_hbm,
    qkv_hbm,
    out_hbm,
    up_hbm,
    ub_hbm,
    dn_hbm,
    act_ref,
    igrad_ref,
    pgrad_ref,
    tok,
    cot,
    prom,
    norms,
    bias,
    w_qkv,
    w_out,
    w_up,
    ub,
    w_dn,
    seq,
    hid,
    acc,
    wide,
    x16,
    xh1,
    r1,
    xh2,
    r2,
    q_s,
    k_s,
    v_s,
    e_s,
    ri_s,
    o_s,
    gp_s,
    local_sem,
    send_sem,
    recv_sem,
):
    B, T, D, L, PN, TK, PP, S, TQ, FH = dims
    H = HEADS
    HD = D // H
    C = 768
    me = lax.axis_index("mlp")
    other = 1 - me
    half = D // 2

    barrier = pltpu.get_barrier_semaphore()
    pl.semaphore_signal(barrier, inc=1, device_id={"mlp": other}, device_id_type=MESH)

    local = {}

    def fetch(name, src, dst):
        copy = pltpu.make_async_copy(src, dst, local_sem.at[len(local)])
        copy.start()
        local[name] = copy

    mine = pl.ds(pl.multiple_of(me * half, 128), half)
    fetch("tok", tok_hbm, tok)
    fetch("norms", norms_hbm, norms)
    fetch("bias", bias_hbm, bias)
    fetch("prom", prompts_hbm, prom.at[:, :, mine])
    fetch("qkv0", qkv_hbm.at[0], w_qkv.at[0])
    fetch("out0", out_hbm.at[0], w_out.at[0])
    fetch("ub", ub_hbm, ub.at[0])
    for l in range(L):
        if l:
            fetch(f"qkv{l}", qkv_hbm.at[l], w_qkv.at[l])
            fetch(f"out{l}", out_hbm.at[l], w_out.at[l])
        fetch(f"up{l}", up_hbm.at[l], w_up.at[l, 0])
        fetch(f"dn{l}", dn_hbm.at[l], w_dn.at[l, 0])
    fetch("cot", cot_hbm, cot)

    pl.semaphore_wait(barrier, 1)
    remote = {}

    def push(name, src, dst):
        i = len(remote)
        copy = pltpu.make_async_remote_copy(
            src_ref=src,
            dst_ref=dst,
            send_sem=send_sem.at[i],
            recv_sem=recv_sem.at[i],
            device_id={"mlp": other},
            device_id_type=MESH,
        )
        copy.start()
        remote[name] = copy

    push("prom", prompts_hbm, prom.at[:, :, mine])
    push("ub", ub_hbm, ub.at[1])
    for l in range(L):
        push(f"up{l}", up_hbm.at[l], w_up.at[l, 1])
        push(f"dn{l}", dn_hbm.at[l], w_dn.at[l, 1])

    lane = lax.broadcasted_iota(jnp.int32, (1, S), 1)
    valid = (lane < T) | ((lane >= TK) & (lane < TK + PN))
    key_bias = jnp.where(valid, 0.0, -1e30).astype(F32)
    even_q = lax.broadcasted_iota(jnp.int32, (TQ, 2 * HD), 1) < HD
    even_k = lax.broadcasted_iota(jnp.int32, (S, 2 * HD), 1) < HD
    scale = HD**-0.5

    for b in range(B):
        seq[b, TK - 8 :, :] = jnp.zeros((S - TK + 8, D), F32)
    local["tok"].wait()
    for b in range(B):
        seq[b, 0:T, :] = tok[b].astype(F32)
    local["norms"].wait()
    local["bias"].wait()
    local["prom"].wait()
    remote["prom"].wait()

    def norm_rows(x):
        mean = jnp.mean(x, axis=-1, keepdims=True)
        centre = x - mean
        spread = jnp.mean(centre * centre, axis=-1, keepdims=True)
        inv = lax.rsqrt(spread + norm_eps)
        return centre * inv, inv

    def attend_forward(l):
        def pair(i, carry):
            b = i // (H // 2)
            hp = i % (H // 2)
            sl = pl.ds(pl.multiple_of(hp * 2 * HD, 2 * HD), 2 * HD)
            qr = pl.ds(pl.multiple_of(b * TQ, 16), TQ)
            kr = pl.ds(pl.multiple_of(b * S, 16), S)
            q = q_s[l, qr, sl]
            k = k_s[l, kr, sl]
            v = v_s[l, kr, sl]
            sums = []
            for h in range(2):
                here = even_k if h == 0 else jnp.logical_not(even_k)
                s = mm_nt(q, jnp.where(here, k, jnp.zeros_like(k))) + key_bias
                top = jnp.max(s, axis=1, keepdims=True)
                e = jnp.exp2((s - top) * (LOG2E * scale)).astype(BF16)
                e_s[l, b, hp * 2 + h] = e
                sums.append(mm(e, jnp.where(here, v, jnp.ones_like(v))))
            top_part = jnp.where(even_q, sums[0], sums[1])
            total = jnp.where(even_q, sums[1], sums[0])
            inv = pltpu.roll(1.0 / total, HD, 1)
            ri_s[l, b, :, sl] = inv
            o_s[l, qr, sl] = (top_part * inv).astype(BF16)
            return carry

        lax.fori_loop(0, B * H // 2, pair, 0, unroll=3)

    def attend_backward(l):
        def pair(i, carry):
            b = i // (H // 2)
            hp = i % (H // 2)
            at = pl.multiple_of(hp * 2 * HD, 2 * HD)
            sl = pl.ds(at, 2 * HD)
            qr = pl.ds(pl.multiple_of(b * TQ, 16), TQ)
            kr = pl.ds(pl.multiple_of(b * S, 16), S)
            q = q_s[l, qr, sl]
            k = k_s[l, kr, sl]
            v = v_s[l, kr, sl]
            do = x16[qr, sl].astype(F32) * ri_s[l, b, :, sl]
            prod = do * o_s[l, qr, sl].astype(F32)
            do16 = do.astype(BF16)
            dq = None
            dks, dvs = [], []
            for h in range(2):
                here_q = even_q if h == 0 else jnp.logical_not(even_q)
                here = even_k if h == 0 else jnp.logical_not(even_k)
                delta = jnp.sum(jnp.where(here_q, prod, 0.0), axis=1, keepdims=True)
                dp = mm_nt(do16, jnp.where(here, v, jnp.zeros_like(v)))
                e = e_s[l, b, hp * 2 + h]
                ds = (e.astype(F32) * (dp - delta)).astype(BF16)
                part = mm(ds, jnp.where(here, k, jnp.zeros_like(k)))
                dq = part if dq is None else dq + part
                dks.append(mm_tn(ds, q))
                dvs.append(mm_tn(e, do16))
            qrow = pl.ds(pl.multiple_of(b * S, 16), TQ)
            wide[qrow, sl] = (dq * scale).astype(BF16)
            wide[kr, pl.ds(pl.multiple_of(D + at, 128), 2 * HD)] = (
                jnp.where(even_k, dks[0], dks[1]) * scale
            ).astype(BF16)
            wide[kr, pl.ds(pl.multiple_of(2 * D + at, 128), 2 * HD)] = jnp.where(
                even_k, dvs[0], dvs[1]
            ).astype(BF16)
            return carry

        lax.fori_loop(0, B * H // 2, pair, 0, unroll=3)

    for l in range(L):
        for b in range(B):
            seq[b, TK : TK + PN, :] = prom[l]
        gain, shift = norms[l, 0:1, :], norms[l, 1:2, :]
        for b in range(B):

            def ln_one(r, b=b):
                xh, inv = norm_rows(seq[b, pl.ds(r, 32), :])
                at = pl.ds(pl.multiple_of(b * S + r, 32), 32)
                xh1[l, at, :] = xh.astype(BF16)
                r1[l, at, :] = inv
                wide[at, 0:D] = (xh * gain + shift).astype(BF16)

            rows_loop(S, 32, ln_one, unroll=2)
        local[f"qkv{l}"].wait()
        lhs = jnp.concatenate([wide[b * S : b * S + TQ, 0:D] for b in range(B)], axis=0)
        q_s[l] = (mm(lhs, w_qkv[l, :, 0:D]) + bias[l, 0:1, :]).astype(BF16)
        k_s[l] = mm(wide[:, 0:D], w_qkv[l, :, D : 2 * D]).astype(BF16)
        v_s[l] = (mm(wide[:, 0:D], w_qkv[l, :, 2 * D : 3 * D]) + bias[l, 1:2, :]).astype(BF16)
        attend_forward(l)
        local[f"out{l}"].wait()
        branch = mm(o_s[l], w_out[l]) + bias[l, 2:3, :]
        for b in range(B):
            hid[b * TQ : (b + 1) * TQ, :] = seq[b, 0:TQ, :] + branch[b * TQ : (b + 1) * TQ]
        gain2, shift2 = norms[l, 2:3, :], norms[l, 3:4, :]

        def ln_two(r):
            at = pl.ds(r, 32)
            xh, inv = norm_rows(hid[at, :])
            xh2[l, at, :] = xh.astype(BF16)
            r2[l, at, :] = inv
            x16[at, :] = (xh * gain2 + shift2).astype(BF16)

        rows_loop(B * TQ, 32, ln_two)
        if l == 0:
            local["ub"].wait()
            remote["ub"].wait()
        for part in range(2):
            kept = local if part == 0 else remote
            kept[f"up{l}"].wait()
            kept[f"dn{l}"].wait()
            for j in range(FH // C):
                cols = slice(j * C, (j + 1) * C)
                pre = mm(x16[...], w_up[l, part, :, cols]) + ub[part, l : l + 1, cols]
                cdf = 0.5 + 0.5 * lax.erf(pre * 0.7071067811865476)
                bell = jnp.exp2(pre * pre * (-0.5 * LOG2E)) * 0.3989422804014327
                at = slice((part * (FH // C) + j) * C, (part * (FH // C) + j + 1) * C)
                gp_s[l, :, at] = (cdf + pre * bell).astype(BF16)
                add = mm((pre * cdf).astype(BF16), w_dn[l, part, cols, :])
                if part == 0 and j == 0:
                    acc[...] = add
                else:
                    acc[...] += add
        for b in range(B):
            seq[b, 0:TQ, :] = (
                hid[b * TQ : (b + 1) * TQ, :] + acc[b * TQ : (b + 1) * TQ, :] + bias[l, 3:4, :]
            )

    for b in range(B):
        act_ref[b] = seq[b, 0:T, :].astype(BF16)

    local["cot"].wait()
    for b in range(B):
        hid[b * TQ + TK - 8 : (b + 1) * TQ, :] = jnp.zeros((TQ - TK + 8, D), F32)
        hid[b * TQ : b * TQ + T, :] = cot[b].astype(F32)
        wide[b * S + TQ : (b + 1) * S, 0:D] = jnp.zeros((S - TQ, D), BF16)
    for l in reversed(range(L)):
        x16[...] = hid[...].astype(BF16)
        for part in range(2):
            for j in range(FH // C):
                cols = slice(j * C, (j + 1) * C)
                at = slice((part * (FH // C) + j) * C, (part * (FH // C) + j + 1) * C)
                ga = mm_nt(x16[...], w_dn[l, part, cols, :])
                gpre = (gp_s[l, :, at].astype(F32) * ga).astype(BF16)
                add = mm_nt(gpre, w_up[l, part, :, cols])
                if part == 0 and j == 0:
                    acc[...] = add
                else:
                    acc[...] += add
        gain2 = norms[l, 2:3, :]

        def ln_two_back(r):
            at = pl.ds(r, 32)
            xh = xh2[l, at, :].astype(F32)
            gdy = acc[at, :] * gain2
            a = jnp.mean(gdy, axis=-1, keepdims=True)
            c = jnp.mean(gdy * xh, axis=-1, keepdims=True)
            new = hid[at, :] + r2[l, at, :] * (gdy - a - xh * c)
            hid[at, :] = new
            x16[at, :] = new.astype(BF16)

        rows_loop(B * TQ, 32, ln_two_back)
        x16[...] = mm_nt(x16[...], w_out[l]).astype(BF16)
        attend_backward(l)
        gain = norms[l, 0:1, :]
        gn = mm_nt(wide[...], w_qkv[l])
        for b in range(B):
            seq[b] = gn[b * S : (b + 1) * S]

        def ln_back(dy, xh, inv):
            gdy = dy * gain
            a = jnp.mean(gdy, axis=-1, keepdims=True)
            c = jnp.mean(gdy * xh, axis=-1, keepdims=True)
            return inv * (gdy - a - xh * c)

        dprom = seq[0, TK:S, :]
        for b in range(1, B):
            dprom = dprom + seq[b, TK:S, :]
        xh_p = xh1[l, TK - 8 : S, :].astype(F32)[8:]
        pgrad_ref[l] = ln_back(dprom, xh_p, r1[l, TK:S, :])
        for b in range(B):

            def ln_one_back(r, b=b):
                dx = ln_back(
                    seq[b, pl.ds(r, 16), :],
                    xh1[l, pl.ds(pl.multiple_of(b * S + r, 16), 16), :].astype(F32),
                    r1[l, pl.ds(pl.multiple_of(b * S + r, 16), 16), :],
                )
                at = pl.ds(pl.multiple_of(b * TQ + r, 16), 16)
                hid[at, :] = hid[at, :] + dx

            rows_loop(TK // 16 * 16, 16, ln_one_back, unroll=2)
            base = TK // 16 * 16
            dx = ln_back(
                seq[b, base:TK, :],
                xh1[l, b * S + base : b * S + base + 16, :].astype(F32)[: TK - base],
                r1[l, b * S + base : b * S + TK, :],
            )
            hid[b * TQ + base : b * TQ + TK, :] = hid[b * TQ + base : b * TQ + TK, :] + dx
    for b in range(B):
        igrad_ref[b] = hid[b * TQ : b * TQ + T, :]


def run_main(tokens, cotangent, prompts, norm_params, bias_rows, qkv, out, up, ub, dn):
    B, T, D = tokens.shape
    L, PN, _ = prompts.shape
    FH = dn.shape[1]
    TK, PP = up_to(T, 8), up_to(PN, 8)
    S = up_to(TK + PP, 128)
    TQ = up_to(T, 16)
    dims = (B, T, D, L, PN, TK, PP, S, TQ, FH)
    H = HEADS
    n_local, n_remote = 8 + 4 * L, 2 + 2 * L
    scratch = [
        VMEM((B, T, D), BF16),
        VMEM((B, T, D), BF16),
        VMEM((L, PN, D), F32),
        VMEM((L, 4, D), F32),
        VMEM((L, 4, D), F32),
        VMEM((L, D, 3 * D), BF16),
        VMEM((L, D, D), BF16),
        VMEM((L, 2, D, FH), BF16),
        VMEM((2, L, FH), F32),
        VMEM((L, 2, FH, D), BF16),
        VMEM((B, S, D), F32),
        VMEM((B * TQ, D), F32),
        VMEM((B * TQ, D), F32),
        VMEM((B * S, 3 * D), BF16),
        VMEM((B * TQ, D), BF16),
        VMEM((L, B * S, D), BF16),
        VMEM((L, B * S, 1), F32),
        VMEM((L, B * TQ, D), BF16),
        VMEM((L, B * TQ, 1), F32),
        VMEM((L, B * TQ, D), BF16),
        VMEM((L, B * S, D), BF16),
        VMEM((L, B * S, D), BF16),
        VMEM((L, B, H, TQ, S), BF16),
        VMEM((L, B, TQ, D), F32),
        VMEM((L, B * TQ, D), BF16),
        VMEM((L, B * TQ, 2 * FH), BF16),
        DMA((n_local,)),
        DMA((n_remote,)),
        DMA((n_remote,)),
    ]
    any_spec = pl.BlockSpec(memory_space=pl.ANY)
    vmem_spec = pl.BlockSpec(memory_space=VMEM)
    return pl.pallas_call(
        functools.partial(main_kernel, dims),
        out_shape=(
            jax.ShapeDtypeStruct((B, T, D), BF16),
            jax.ShapeDtypeStruct((B, T, D), F32),
            jax.ShapeDtypeStruct((L, S - TK, D), F32),
        ),
        in_specs=[any_spec] * 10,
        out_specs=(vmem_spec,) * 3,
        scratch_shapes=scratch,
        compiler_params=pltpu.CompilerParams(
            collective_id=0, has_side_effects=True, vmem_limit_bytes=64 * 2**20
        ),
    )(tokens, cotangent, prompts, norm_params, bias_rows, qkv, out, up, ub, dn)


def tail_kernel(
    ndp, pn, pg_ref, prompt_ref, first_ref, second_ref,
    grad_ref, norm_ref, new_first_ref, new_second_ref, new_prompt_ref,
    sent, got, got0, sq, send_sem, recv_sem, half_sem, sq_sem,
):
    me = lax.axis_index("dp")
    core = lax.axis_index("mlp")
    other = 1 - core
    L, rows, D = pg_ref.shape
    half = D // 2
    steps = []
    stride = 1
    while stride < ndp:
        low = lax.rem(me, stride)
        bit = lax.rem(me // stride, 2)
        high = me // (2 * stride)
        steps.append(high * 2 * stride + (1 - bit) * stride + low)
        stride *= 2
    barrier = pltpu.get_barrier_semaphore()
    pl.semaphore_signal(barrier, inc=1, device_id={"mlp": other}, device_id_type=MESH)
    for peer in steps:
        pl.semaphore_signal(barrier, inc=1, device_id={"dp": peer}, device_id_type=MESH)
    pl.semaphore_wait(barrier, 1 + len(steps))

    def swap(src, dst, sems, device):
        copy = pltpu.make_async_remote_copy(
            src_ref=src, dst_ref=dst, send_sem=sems[0], recv_sem=sems[1],
            device_id=device, device_id_type=MESH,
        )
        copy.start()
        copy.wait()

    theirs = pl.ds(pl.multiple_of(other * half, 128), half)
    ours = pl.ds(pl.multiple_of(core * half, 128), half)
    swap(pg_ref.at[:, :, theirs], got0, (half_sem.at[0], half_sem.at[1]), {"mlp": other})
    total = pg_ref[:, :, ours] + got0[...]
    for i, peer in enumerate(steps):
        sent[i] = total
        swap(sent.at[i], got.at[i], (send_sem.at[i], recv_sem.at[i]), {"dp": peer})
        total = sent[i] + got[i]
    total = total[:, :pn]
    grad_ref[...] = total
    sq[0] = jnp.broadcast_to(jnp.sum(total * total).reshape(1, 1), (8, 128))
    swap(sq.at[0], sq.at[1], (sq_sem.at[0], sq_sem.at[1]), {"mlp": other})
    squares = sq[0, 0:1, 0:1] + sq[1, 0:1, 0:1]
    grad_norm = jnp.sqrt(squares)
    norm_ref[...] = grad_norm
    factor = jnp.minimum(1.0, clip_limit / (grad_norm + 1e-06))
    clipped = total * factor
    new_first = beta_one * first_ref[...] + (1.0 - beta_one) * clipped
    new_second = beta_two * second_ref[...] + (1.0 - beta_two) * clipped * clipped
    fix_first = 1.0 - beta_one**STEP
    fix_second = 1.0 - beta_two**STEP
    new_first_ref[...] = new_first
    new_second_ref[...] = new_second
    new_prompt_ref[...] = prompt_ref[...] - learn_rate * (
        new_first / fix_first / (jnp.sqrt(new_second / fix_second) + adam_eps)
        + weight_decay * prompt_ref[...]
    )


def run_tail(ndp, pgrad, prompts, first, second):
    L, rows, D = pgrad.shape
    n = max(1, (ndp - 1).bit_length())
    spec = pl.BlockSpec(memory_space=VMEM)
    small = jax.ShapeDtypeStruct(prompts.shape, F32)
    return pl.pallas_call(
        functools.partial(tail_kernel, ndp, prompts.shape[1]),
        out_shape=(small, jax.ShapeDtypeStruct((1, 1), F32), small, small, small),
        in_specs=[spec] * 4,
        out_specs=(spec,) * 5,
        scratch_shapes=[
            VMEM((n, L, rows, D // 2), F32),
            VMEM((n, L, rows, D // 2), F32),
            VMEM((L, rows, D // 2), F32),
            VMEM((2, 8, 128), F32),
            DMA((n,)),
            DMA((n,)),
            DMA((2,)),
            DMA((2,)),
        ],
        compiler_params=pltpu.CompilerParams(collective_id=1, has_side_effects=True),
    )(pgrad, prompts, first, second)


def local(
    ndp, tokens, cotangent, prompts, first_moment, second_moment, norm_params, bias_rows,
    qkv_weight, out_weight, up_weight, up_bias, down_weight,
):
    act, igrad, pgrad = run_main(
        tokens, cotangent, prompts, norm_params, bias_rows,
        qkv_weight, out_weight, up_weight, up_bias, down_weight,
    )
    grad, norm, new_first, new_second, new_prompts = run_tail(
        ndp, pgrad, prompts, first_moment, second_moment
    )
    return act, igrad, grad, norm.reshape(()), new_first, new_second, new_prompts


def solution(mesh):
    ndp = mesh.shape["dp"]
    return jax.shard_map(
        functools.partial(local, ndp),
        mesh=mesh,
        in_specs=(
            P(("dp", "mlp"), None, None),
            P(("dp", "mlp"), None, None),
            P(None, None, "mlp"),
            P(None, None, "mlp"),
            P(None, None, "mlp"),
            P(),
            P(),
            P(),
            P(),
            P(None, None, "mlp"),
            P(None, "mlp"),
            P(None, "mlp", None),
        ),
        out_specs=(
            P(("dp", "mlp"), None, None),
            P(("dp", "mlp"), None, None),
            P(None, None, "mlp"),
            P(),
            P(None, None, "mlp"),
            P(None, None, "mlp"),
            P(None, None, "mlp"),
        ),
        check_vma=False,
    )
```

```python
import functools

import jax
import jax.numpy as jnp
from jax import lax
from jax.experimental import pallas as pl
from jax.experimental.pallas import tpu as pltpu
from jax.sharding import PartitionSpec as P

HEADS = 12
STEP = 10
MESH = pl.DeviceIdType.MESH
VMEM = pltpu.VMEM
DMA = pltpu.SemaphoreType.DMA
BF16 = jnp.bfloat16
F32 = jnp.float32

norm_eps = 1e-06
clip_limit = 1.0
beta_one = 0.9
beta_two = 0.999
learn_rate = 1.5
weight_decay = 0.05
adam_eps = 1e-08
LOG2E = 1.4426950408889634


def up_to(value, step):
    return -(-value // step) * step


def mm(left, right):
    return jnp.dot(left, right, preferred_element_type=F32)


def mm_nt(left, right):
    return lax.dot_general(left, right, (((1,), (1,)), ((), ())), preferred_element_type=F32)


def mm_tn(left, right):
    return lax.dot_general(left, right, (((0,), (0,)), ((), ())), preferred_element_type=F32)


def rows_loop(count, step, body, unroll=1):
    def one(i, carry):
        body(pl.multiple_of(i * step, step))
        return carry

    lax.fori_loop(0, count // step, one, 0, unroll=unroll)


def main_kernel(
    dims,
    tok_hbm,
    cot_hbm,
    prompts_hbm,
    first_hbm,
    second_hbm,
    norms_hbm,
    bias_hbm,
    qkv_hbm,
    out_hbm,
    up_hbm,
    ub_hbm,
    dn_hbm,
    act_hbm,
    igrad_hbm,
    pgrad_hbm,
    norm_hbm,
    new_first_hbm,
    new_second_hbm,
    new_prompt_hbm,
    tok_nat,
    cot_nat,
    stage_nat,
    prom_nat,
    adam_nat,
    norms,
    bias,
    w_qkv,
    w_out,
    w_up,
    ub,
    w_dn,
    seq,
    hid,
    acc,
    wide,
    x16,
    xh1,
    r1,
    xh2,
    r2,
    q_s,
    k_s,
    v_s,
    e_s,
    ri_s,
    o_s,
    gp_s,
    part_f,
    part_h,
    got_a,
    sum_b,
    sum_h,
    slot_b,
    slot_c,
    fin,
    sq,
    norm_s,
    local_sem,
    out_sem,
    send_sem,
    recv_sem,
    sem_a,
    send_b,
    recv_b,
    send_c,
    recv_c,
    send_d,
    recv_d,
    sem_sq,
):
    B, T, D, L, PN, TK, S, TQ, FH, G, R = dims
    H = HEADS
    HD = D // H
    C = 768
    NJ = D // 128
    HJ = NJ // 2
    PB = 16
    core = lax.axis_index("mlp")
    other = 1 - core
    me = lax.axis_index("dp")
    g, r = lax.rem(me, G), me // G
    half = D // 2

    def member(k):
        return lax.rem(g + k, G)

    def rank(k):
        return lax.rem(r + k, R)

    barrier = pltpu.get_barrier_semaphore()
    pl.semaphore_signal(barrier, inc=1, device_id={"mlp": other}, device_id_type=MESH)
    for k in range(1, G):
        pl.semaphore_signal(
            barrier, inc=1, device_id={"dp": r * G + member(k)}, device_id_type=MESH
        )

    def greet(k, carry):
        pl.semaphore_signal(
            barrier, inc=1, device_id={"dp": rank(k) * G + g}, device_id_type=MESH
        )
        return carry

    lax.fori_loop(1, R, greet, 0)

    local = {}

    def fetch(name, src, dst):
        copy = pltpu.make_async_copy(src, dst, local_sem.at[len(local)])
        copy.start()
        local[name] = copy

    def fetch_native(name, src, dst, base, count):
        for j in range(count):
            fetch(f"{name}{j}", src.at[:, :, 128 * j : 128 * (j + 1)], dst.at[base + j])

    fetch_native("tok", tok_hbm, tok_nat, 0, NJ)
    fetch_native("prom", prompts_hbm, prom_nat, core * HJ, HJ)
    fetch("norms", norms_hbm, norms)
    fetch("bias", bias_hbm, bias)
    fetch("qkv0", qkv_hbm.at[0], w_qkv.at[0])

    remote = {}

    def push(name, src, dst):
        i = len(remote)
        copy = pltpu.make_async_remote_copy(
            src_ref=src,
            dst_ref=dst,
            send_sem=send_sem.at[i],
            recv_sem=recv_sem.at[i],
            device_id={"mlp": other},
            device_id_type=MESH,
        )
        copy.start()
        remote[name] = copy

    pl.semaphore_wait(barrier, G + R - 1)
    for j in range(HJ):
        push(
            f"prom{j}",
            prompts_hbm.at[:, :, 128 * j : 128 * (j + 1)],
            prom_nat.at[core * HJ + j],
        )

    tok_v = tok_nat.reshape(NJ, T * B, 128)
    cot_v = cot_nat.reshape(NJ, T * B, 128)
    stage_v = stage_nat.reshape(NJ, T * B, 128)
    prom_v = prom_nat.reshape(NJ, PN * L, 128)

    lane = lax.broadcasted_iota(jnp.int32, (1, S), 1)
    valid = (lane < T) | ((lane >= TK) & (lane < TK + PN))
    key_bias = jnp.where(valid, 0.0, -1e30).astype(F32)
    even_q = lax.broadcasted_iota(jnp.int32, (TQ, 2 * HD), 1) < HD
    even_k = lax.broadcasted_iota(jnp.int32, (S, 2 * HD), 1) < HD
    SH = S // 2
    even_h = lax.broadcasted_iota(jnp.int32, (SH, 2 * HD), 1) < HD
    low_lane = lax.broadcasted_iota(jnp.int32, (TQ, S), 1) < SH
    scale = HD**-0.5

    def spread(src_v, store):
        for j in range(NJ):
            stage_v[j] = src_v[j].astype(F32)
        for b in range(B):
            for j in range(NJ):
                store(b, slice(128 * j, 128 * (j + 1)), stage_v[j, pl.ds(b, T, stride=B), :])

    for b in range(B):
        seq[b, TK - 8 :, :] = jnp.zeros((S - TK + 8, D), F32)
    for j in range(NJ):
        local[f"tok{j}"].wait()

    def store_tok(b, cols, rows):
        seq[b, 0:T, cols] = rows

    spread(tok_v, store_tok)
    local["norms"].wait()
    local["bias"].wait()
    for j in range(HJ):
        local[f"prom{j}"].wait()
        remote[f"prom{j}"].wait()

    def norm_rows(x):
        mean = jnp.mean(x, axis=-1, keepdims=True)
        centre = x - mean
        spread_ = jnp.mean(centre * centre, axis=-1, keepdims=True)
        inv = lax.rsqrt(spread_ + norm_eps)
        return centre * inv, inv

    def attend_forward(l):
        def pair(i, carry):
            b = i // (H // 2)
            hp = i % (H // 2)
            sl = pl.ds(pl.multiple_of(hp * 2 * HD, 2 * HD), 2 * HD)
            qr = pl.ds(pl.multiple_of(b * TQ, 16), TQ)
            kr = pl.ds(pl.multiple_of(b * S, 16), S)
            q = q_s[l, qr, sl]
            k = k_s[l, kr, sl]
            v = v_s[l, kr, sl]
            sums = []
            for h in range(2):
                here = even_k if h == 0 else jnp.logical_not(even_k)
                s = mm_nt(q, jnp.where(here, k, jnp.zeros_like(k))) + key_bias
                top = jnp.max(s, axis=1, keepdims=True)
                e = jnp.exp2((s - top) * (LOG2E * scale)).astype(BF16)
                e_s[l, b, hp * 2 + h] = e
                sums.append(mm(e, jnp.where(here, v, jnp.ones_like(v))))
            top_part = jnp.where(even_q, sums[0], sums[1])
            total = jnp.where(even_q, sums[1], sums[0])
            inv = pltpu.roll(1.0 / total, HD, 1)
            ri_s[l, b, :, sl] = inv
            o_s[l, qr, sl] = (top_part * inv).astype(BF16)
            return carry

        lax.fori_loop(0, B * H // 2, pair, 0, unroll=3)

    def back_half(l, b, hp, part, first):
        at = pl.multiple_of(hp * 2 * HD, 2 * HD)
        sl = pl.ds(at, 2 * HD)
        qr = pl.ds(pl.multiple_of(b * TQ, 16), TQ)
        kr = pl.ds(pl.multiple_of(b * S + part * SH, 16), SH)
        q = q_s[l, qr, sl]
        v = v_s[l, kr, sl]
        if first:
            do = x16[qr, sl].astype(F32) * ri_s[l, b, :, sl]
            prod = do * o_s[l, qr, sl].astype(F32)
            d0 = jnp.sum(jnp.where(even_q, prod, 0.0), axis=1, keepdims=True)
            d1 = jnp.sum(jnp.where(even_q, 0.0, prod), axis=1, keepdims=True)
            do16 = do.astype(BF16)
            x16[qr, sl] = do16
            ri_s[l, b, :, sl] = jnp.where(even_q, d0, d1)
        else:
            do16 = x16[qr, sl]
            both = ri_s[l, b, :, sl]
            d0, d1 = both[:, 0:1], both[:, HD : HD + 1]
        zero = jnp.zeros_like(v)
        stacked = jnp.concatenate([jnp.where(even_h, v, zero), jnp.where(even_h, zero, v)], axis=0)
        dp = mm_nt(do16, stacked)
        keys = slice(part * SH, (part + 1) * SH)
        e = jnp.concatenate([e_s[l, b, hp * 2, :, keys], e_s[l, b, hp * 2 + 1, :, keys]], axis=1)
        ds = (e.astype(F32) * (dp - jnp.where(low_lane, d0, d1))).astype(BF16)
        dk = mm_tn(ds, q)
        dv = mm_tn(e, do16)
        wide[kr, pl.ds(pl.multiple_of(D + at, 128), 2 * HD)] = (
            jnp.where(even_h, dk[:SH], dk[SH:]) * scale
        ).astype(BF16)
        wide[kr, pl.ds(pl.multiple_of(2 * D + at, 128), 2 * HD)] = jnp.where(
            even_h, dv[:SH], dv[SH:]
        ).astype(BF16)
        return ds

    def back_queries(l, b, hp, low, high):
        at = pl.multiple_of(hp * 2 * HD, 2 * HD)
        sl = pl.ds(at, 2 * HD)
        kr = pl.ds(pl.multiple_of(b * S, 16), S)
        k = k_s[l, kr, sl]
        zero = jnp.zeros_like(k)
        dq = mm(jnp.concatenate([low[:, :SH], high[0]], axis=1), jnp.where(even_k, k, zero))
        dq += mm(jnp.concatenate([low[:, SH:], high[1]], axis=1), jnp.where(even_k, zero, k))
        wide[pl.ds(pl.multiple_of(b * S, 16), TQ), sl] = (dq * scale).astype(BF16)

    def pairs_loop(body, lo, hi):
        def one(i, carry):
            body(i // (H // 2), i % (H // 2))
            return carry

        lax.fori_loop(lo, hi, one, 0, unroll=3)

    pairs = B * H // 2

    def device_of(member_, rank_):
        return {"dp": rank_ * G + member_}

    def copy_a(l):
        return pltpu.make_async_remote_copy(
            src_ref=part_h.at[l, other],
            dst_ref=got_a.at[l],
            send_sem=sem_a.at[l, 0],
            recv_sem=sem_a.at[l, 1],
            device_id={"mlp": other},
            device_id_type=MESH,
        )

    def copy_b(l, k):
        peer = member(k)
        return pltpu.make_async_remote_copy(
            src_ref=sum_h.at[l, peer],
            dst_ref=slot_b.at[l, g],
            send_sem=send_b.at[l, peer],
            recv_sem=recv_b.at[l, g],
            device_id=device_of(peer, r),
            device_id_type=MESH,
        )

    def copy_c(l, k):
        peer = rank(k)
        return pltpu.make_async_remote_copy(
            src_ref=slot_c.at[l, r],
            dst_ref=slot_c.at[l, r],
            send_sem=send_c.at[l, peer],
            recv_sem=recv_c.at[l, r],
            device_id=device_of(g, peer),
            device_id_type=MESH,
        )

    def copy_d(l, k):
        peer = member(k)
        return pltpu.make_async_remote_copy(
            src_ref=fin.at[l, g],
            dst_ref=fin.at[l, g],
            send_sem=send_d.at[l, peer],
            recv_sem=recv_d.at[l, g],
            device_id=device_of(peer, r),
            device_id_type=MESH,
        )

    def await_from(l, slots, sems, index):
        pltpu.make_async_remote_copy(
            src_ref=slots.at[l, index],
            dst_ref=slots.at[l, index],
            send_sem=sems.at[l, index],
            recv_sem=sems.at[l, index],
            device_id={"mlp": other},
            device_id_type=MESH,
        ).wait_recv()

    def reduce_start(l, grad):
        rows = jnp.concatenate([grad, jnp.zeros((G * PB - grad.shape[0], D), F32)], axis=0)
        for j in range(NJ):
            for k in range(G):
                block = rows[k * PB : (k + 1) * PB, 128 * j : 128 * (j + 1)]
                part_f[l, j // HJ, k, j % HJ] = block
                part_h[l, j // HJ, k, j % HJ] = block.astype(BF16)
        copy_a(l).start()

    def reduce_pair(l):
        copy_a(l).wait()
        total = part_f[l, core] + got_a[l].astype(F32)
        sum_b[l] = total
        sum_h[l] = total.astype(BF16)
        for k in range(1, G):
            copy_b(l, k).start()

    def reduce_group(l):
        total = sum_b[l, g]
        for k in range(1, G):
            await_from(l, slot_b, recv_b, member(k))
            total = total + slot_b[l, member(k)].astype(F32)
        slot_c[l, r] = total.astype(BF16)

        def go(k, carry):
            copy_c(l, k).start()
            return carry

        lax.fori_loop(1, R, go, 0)
        for k in range(1, G):
            copy_b(l, k).wait_send()

    def reduce_ranks(l):
        def come(k, carry):
            await_from(l, slot_c, recv_c, rank(k))
            return carry

        lax.fori_loop(1, R, come, 0)

        def add(k, total):
            return total + slot_c[l, k].astype(F32)

        total = lax.fori_loop(0, R, add, jnp.zeros((HJ, PB, 128), F32))
        fin[l, g] = total.astype(BF16)
        for k in range(1, G):
            copy_d(l, k).start()

        def sent(k, carry):
            copy_c(l, k).wait_send()
            return carry

        lax.fori_loop(1, R, sent, 0)

    def reduce_end(l):
        for k in range(1, G):
            await_from(l, fin, recv_d, member(k))
        for k in range(1, G):
            copy_d(l, k).wait_send()

    for l in range(L):
        for b in range(B):
            for j in range(NJ):
                seq[b, TK : TK + PN, 128 * j : 128 * (j + 1)] = prom_v[
                    j, pl.ds(l, PN, stride=L), :
                ]
        gain, shift = norms[l, 0:1, :], norms[l, 1:2, :]
        for b in range(B):

            def ln_one(row, b=b):
                xh, inv = norm_rows(seq[b, pl.ds(row, 32), :])
                at = pl.ds(pl.multiple_of(b * S + row, 32), 32)
                xh1[l, at, :] = xh.astype(BF16)
                r1[l, at, :] = inv
                wide[at, 0:D] = (xh * gain + shift).astype(BF16)

            rows_loop(S, 32, ln_one, unroll=2)
        local[f"qkv{l}"].wait()
        if l == 0:
            fetch("out0", out_hbm.at[0], w_out.at[0])
            fetch("ub", ub_hbm, ub.at[0])
            push("ub", ub_hbm, ub.at[1])
            for i in range(L):
                push(f"up{i}", up_hbm.at[i], w_up.at[i, 1])
                push(f"dn{i}", dn_hbm.at[i], w_dn.at[i, 1])
            for i in range(L):
                if i:
                    fetch(f"qkv{i}", qkv_hbm.at[i], w_qkv.at[i])
                    fetch(f"out{i}", out_hbm.at[i], w_out.at[i])
                fetch(f"up{i}", up_hbm.at[i], w_up.at[i, 0])
                fetch(f"dn{i}", dn_hbm.at[i], w_dn.at[i, 0])
            fetch_native("cot", cot_hbm, cot_nat, 0, NJ)
            for j in range(HJ):
                cols = slice(128 * j, 128 * (j + 1))
                fetch(f"first{j}", first_hbm.at[:, :, cols], adam_nat.at[0, j, 0:PN])
                fetch(f"second{j}", second_hbm.at[:, :, cols], adam_nat.at[1, j, 0:PN])
        lhs = jnp.concatenate([wide[b * S : b * S + TQ, 0:D] for b in range(B)], axis=0)
        q_s[l] = (mm(lhs, w_qkv[l, :, 0:D]) + bias[l, 0:1, :]).astype(BF16)
        k_s[l] = mm(wide[:, 0:D], w_qkv[l, :, D : 2 * D]).astype(BF16)
        v_s[l] = (mm(wide[:, 0:D], w_qkv[l, :, 2 * D : 3 * D]) + bias[l, 1:2, :]).astype(BF16)
        attend_forward(l)
        local[f"out{l}"].wait()
        branch = mm(o_s[l], w_out[l]) + bias[l, 2:3, :]
        for b in range(B):
            hid[b * TQ : (b + 1) * TQ, :] = seq[b, 0:TQ, :] + branch[b * TQ : (b + 1) * TQ]
        gain2, shift2 = norms[l, 2:3, :], norms[l, 3:4, :]

        def ln_two(row):
            at = pl.ds(row, 32)
            xh, inv = norm_rows(hid[at, :])
            xh2[l, at, :] = xh.astype(BF16)
            r2[l, at, :] = inv
            x16[at, :] = (xh * gain2 + shift2).astype(BF16)

        rows_loop(B * TQ, 32, ln_two)
        if l == 0:
            local["ub"].wait()
            remote["ub"].wait()
        for part in range(2):
            kept = local if part == 0 else remote
            kept[f"up{l}"].wait()
            kept[f"dn{l}"].wait()
            for j in range(FH // C):
                cols = slice(j * C, (j + 1) * C)
                pre = mm(x16[...], w_up[l, part, :, cols]) + ub[part, l : l + 1, cols]
                cdf = 0.5 + 0.5 * lax.erf(pre * 0.7071067811865476)
                bell = jnp.exp2(pre * pre * (-0.5 * LOG2E)) * 0.3989422804014327
                at = slice((part * (FH // C) + j) * C, (part * (FH // C) + j + 1) * C)
                gp_s[l, :, at] = (cdf + pre * bell).astype(BF16)
                add = mm((pre * cdf).astype(BF16), w_dn[l, part, cols, :])
                if part == 0 and j == 0:
                    acc[...] = add
                else:
                    acc[...] += add
        for b in range(B):
            seq[b, 0:TQ, :] = (
                hid[b * TQ : (b + 1) * TQ, :] + acc[b * TQ : (b + 1) * TQ, :] + bias[l, 3:4, :]
            )

    for b in range(B):
        for j in range(NJ):
            stage_v[j, pl.ds(b, T, stride=B), :] = seq[b, 0:T, 128 * j : 128 * (j + 1)]
    leaving = []

    def leave(src, dst):
        copy = pltpu.make_async_copy(src, dst, out_sem.at[len(leaving)])
        copy.start()
        leaving.append(copy)

    for j in range(NJ):
        tok_v[j] = stage_v[j].astype(BF16)
        leave(tok_nat.at[j], act_hbm.at[:, :, 128 * j : 128 * (j + 1)])

    for j in range(NJ):
        local[f"cot{j}"].wait()
    for b in range(B):
        hid[b * TQ + TK - 8 : (b + 1) * TQ, :] = jnp.zeros((TQ - TK + 8, D), F32)
        wide[b * S + TQ : (b + 1) * S, 0:D] = jnp.zeros((S - TQ, D), BF16)

    def store_cot(b, cols, rows):
        hid[b * TQ : b * TQ + T, cols] = rows

    spread(cot_v, store_cot)

    for l in reversed(range(L)):
        last = l == 0
        above = l + 1
        x16[...] = hid[...].astype(BF16)
        for part in range(2):
            for j in range(FH // C):
                cols = slice(j * C, (j + 1) * C)
                at = slice((part * (FH // C) + j) * C, (part * (FH // C) + j + 1) * C)
                ga = mm_nt(x16[...], w_dn[l, part, cols, :])
                gpre = (gp_s[l, :, at].astype(F32) * ga).astype(BF16)
                add = mm_nt(gpre, w_up[l, part, :, cols])
                if part == 0 and j == 0:
                    acc[...] = add
                else:
                    acc[...] += add
            if above < L:
                (reduce_pair if part == 0 else reduce_group)(above)
        gain2 = norms[l, 2:3, :]

        def ln_two_back(row):
            at = pl.ds(row, 32)
            xh = xh2[l, at, :].astype(F32)
            gdy = acc[at, :] * gain2
            a = jnp.mean(gdy, axis=-1, keepdims=True)
            c = jnp.mean(gdy * xh, axis=-1, keepdims=True)
            new = hid[at, :] + r2[l, at, :] * (gdy - a - xh * c)
            hid[at, :] = new
            x16[at, :] = new.astype(BF16)

        rows_loop(B * TQ, 32, ln_two_back)
        x16[...] = mm_nt(x16[...], w_out[l]).astype(BF16)
        gain = norms[l, 0:1, :]

        def ln_back(dy, xh, inv):
            gdy = dy * gain
            a = jnp.mean(gdy, axis=-1, keepdims=True)
            c = jnp.mean(gdy * xh, axis=-1, keepdims=True)
            return inv * (gdy - a - xh * c)

        def high_keys(b, hp):
            ds = back_half(l, b, hp, 1, True)
            e_s[l, b, hp * 2, :, SH:] = ds[:, :SH]
            e_s[l, b, hp * 2 + 1, :, SH:] = ds[:, SH:]

        def low_keys(b, hp):
            ds = back_half(l, b, hp, 0, False)
            back_queries(
                l, b, hp, ds, (e_s[l, b, hp * 2, :, SH:], e_s[l, b, hp * 2 + 1, :, SH:])
            )

        def prompt_gradient():
            base = TK // 16 * 16
            lhs = jnp.concatenate(
                [wide[b * S + base : (b + 1) * S, D : 3 * D] for b in range(B)], axis=0
            )
            full = mm_nt(lhs, w_qkv[l, :, D : 3 * D])
            n = S - base
            dprom = full[TK - base : n]
            for b in range(1, B):
                dprom = dprom + full[b * n + TK - base : (b + 1) * n]
            xh_p = xh1[l, base:S, :].astype(F32)[TK - base :]
            return ln_back(dprom, xh_p, r1[l, TK:S, :])

        pairs_loop(high_keys, 0, pairs)
        if above < L:
            reduce_ranks(above)
        reduce_start(l, prompt_gradient())
        if last:
            pairs_loop(low_keys, 0, pairs // 4)
            reduce_pair(l)
            pairs_loop(low_keys, pairs // 4, pairs * 3 // 4)
            reduce_group(l)
            pairs_loop(low_keys, pairs * 3 // 4, pairs)
        else:
            pairs_loop(low_keys, 0, pairs)
        if above < L:
            reduce_end(above)
        lhs = jnp.concatenate([wide[b * S : b * S + TQ, :] for b in range(B)], axis=0)
        acc[...] = mm_nt(lhs, w_qkv[l])
        if last:
            reduce_ranks(l)
        for b in range(B):

            def ln_one_back(row, b=b):
                at = pl.ds(pl.multiple_of(b * TQ + row, 16), 16)
                dx = ln_back(
                    acc[at, :],
                    xh1[l, pl.ds(pl.multiple_of(b * S + row, 16), 16), :].astype(F32),
                    r1[l, pl.ds(pl.multiple_of(b * S + row, 16), 16), :],
                )
                hid[at, :] = hid[at, :] + dx

            rows_loop(TK // 16 * 16, 16, ln_one_back, unroll=2)
            base = TK // 16 * 16
            if base < TK:
                dx = ln_back(
                    acc[b * TQ + base : b * TQ + TK, :],
                    xh1[l, b * S + base : b * S + base + 16, :].astype(F32)[: TK - base],
                    r1[l, b * S + base : b * S + TK, :],
                )
                hid[b * TQ + base : b * TQ + TK, :] = hid[b * TQ + base : b * TQ + TK, :] + dx

    for j in range(NJ):
        for b in range(B):
            stage_v[j, pl.ds(b, T, stride=B), :] = hid[
                b * TQ : b * TQ + T, 128 * j : 128 * (j + 1)
            ]
        leave(stage_nat.at[j], igrad_hbm.at[:, :, 128 * j : 128 * (j + 1)])
    reduce_end(0)

    grad_v = adam_nat.at[2].reshape(HJ, G * PB * L, 128)
    for l in range(L):
        for k in range(G):
            for j in range(HJ):
                grad_v[j, pl.ds(k * PB * L + l, PB, stride=L), :] = fin[l, k, j].astype(F32)
    n = PN * L
    squares = jnp.zeros((1, 1), F32)
    for j in range(HJ):
        rows = grad_v[j, 0:n, :]
        squares += jnp.sum(rows * rows, axis=(0, 1), keepdims=True)
    sq[core] = jnp.broadcast_to(squares, (8, 128))
    copy = pltpu.make_async_remote_copy(
        src_ref=sq.at[core],
        dst_ref=sq.at[core],
        send_sem=sem_sq.at[0],
        recv_sem=sem_sq.at[1],
        device_id={"mlp": other},
        device_id_type=MESH,
    )
    copy.start()
    for j in range(HJ):
        leave(adam_nat.at[2, j, 0:PN], pgrad_hbm.at[:, :, 128 * j : 128 * (j + 1)])
    copy.wait()
    grad_norm = jnp.sqrt(sq[0] + sq[1])
    norm_s[...] = grad_norm[0:1, 0:1]
    leave(norm_s, norm_hbm)
    factor = jnp.minimum(1.0, clip_limit / (grad_norm[0:1, :] + 1e-06))
    fix_first = 1.0 - beta_one**STEP
    fix_second = 1.0 - beta_two**STEP
    for j in range(HJ):
        local[f"first{j}"].wait()
        local[f"second{j}"].wait()
        first_v = adam_nat.at[0].reshape(HJ, G * PB * L, 128)
        second_v = adam_nat.at[1].reshape(HJ, G * PB * L, 128)
        clipped = grad_v[j, 0:n, :] * factor
        new_first = beta_one * first_v[j, 0:n, :] + (1.0 - beta_one) * clipped
        new_second = beta_two * second_v[j, 0:n, :] + (1.0 - beta_two) * clipped * clipped
        first_v[j, 0:n, :] = new_first
        second_v[j, 0:n, :] = new_second
        old = prom_v[core * HJ + j]
        prom_v[core * HJ + j] = old - learn_rate * (
            new_first / fix_first / (jnp.sqrt(new_second / fix_second) + adam_eps)
            + weight_decay * old
        )
        cols = slice(128 * j, 128 * (j + 1))
        leave(adam_nat.at[0, j, 0:PN], new_first_hbm.at[:, :, cols])
        leave(adam_nat.at[1, j, 0:PN], new_second_hbm.at[:, :, cols])
        leave(prom_nat.at[core * HJ + j], new_prompt_hbm.at[:, :, cols])
    for copy in leaving:
        copy.wait()


def hand_on_kernel(parts, *refs):
    n = len(parts)
    sources, targets, held, sem_in, sem_out = (
        refs[:n], refs[n : 2 * n], refs[2 * n : 3 * n], refs[3 * n], refs[3 * n + 1]
    )
    come, go = [], []
    for src, dst, mid, count in zip(sources, targets, held, parts):
        rows = src.shape[0]
        for i in range(count):
            lo, hi = rows * i // count, rows * (i + 1) // count
            a, b, c = (src, mid, dst) if count == 1 else (r.at[lo:hi] for r in (src, mid, dst))
            come.append(pltpu.make_async_copy(a, b, sem_in.at[len(come)]))
            go.append(pltpu.make_async_copy(b, c, sem_out.at[len(go)]))
    for copy in come:
        copy.start()
    for first, second in zip(come, go):
        first.wait()
        second.start()
    for copy in go:
        copy.wait()


def hand_on(parts, arrays):
    any_spec = pl.BlockSpec(memory_space=pl.ANY)
    return pl.pallas_call(
        functools.partial(hand_on_kernel, parts),
        out_shape=tuple(jax.ShapeDtypeStruct(a.shape, a.dtype) for a in arrays),
        in_specs=[any_spec] * len(arrays),
        out_specs=(any_spec,) * len(arrays),
        scratch_shapes=[VMEM(a.shape, a.dtype) for a in arrays]
        + [DMA((sum(parts),)), DMA((sum(parts),))],
        compiler_params=pltpu.CompilerParams(vmem_limit_bytes=60 * 2**20),
    )(*arrays)


def native(x):
    return x.transpose(1, 0, 2)


def local(
    ndp, tokens, cotangent, prompts, first_moment, second_moment, norm_params, bias_rows,
    qkv_weight, out_weight, up_weight, up_bias, down_weight,
):
    B, T, D = tokens.shape
    L, PN, _ = prompts.shape
    FH = down_weight.shape[1]
    TK = up_to(T, 8)
    S = up_to(TK + up_to(PN, 8), 128)
    TQ = up_to(T, 16)
    G = 4
    R = ndp // G
    NJ, HJ, PB = D // 128, D // 256, 16
    dims = (B, T, D, L, PN, TK, S, TQ, FH, G, R)
    H = HEADS
    n_local = 2 * NJ + 3 * HJ + 3 + 4 * L
    n_remote = HJ + 1 + 2 * L
    n_out = 2 * NJ + 4 * HJ + 1
    scratch = [
        VMEM((NJ, T, B, 128), BF16),
        VMEM((NJ, T, B, 128), BF16),
        VMEM((NJ, T, B, 128), F32),
        VMEM((NJ, PN, L, 128), F32),
        VMEM((3, HJ, G * PB, L, 128), F32),
        VMEM((L, 4, D), F32),
        VMEM((L, 4, D), F32),
        VMEM((L, D, 3 * D), BF16),
        VMEM((L, D, D), BF16),
        VMEM((L, 2, D, FH), BF16),
        VMEM((2, L, FH), F32),
        VMEM((L, 2, FH, D), BF16),
        VMEM((B, S, D), F32),
        VMEM((B * TQ, D), F32),
        VMEM((B * TQ, D), F32),
        VMEM((B * S, 3 * D), BF16),
        VMEM((B * TQ, D), BF16),
        VMEM((L, B * S, D), BF16),
        VMEM((L, B * S, 1), F32),
        VMEM((L, B * TQ, D), BF16),
        VMEM((L, B * TQ, 1), F32),
        VMEM((L, B * TQ, D), BF16),
        VMEM((L, B * S, D), BF16),
        VMEM((L, B * S, D), BF16),
        VMEM((L, B, H, TQ, S), BF16),
        VMEM((L, B, TQ, D), F32),
        VMEM((L, B * TQ, D), BF16),
        VMEM((L, B * TQ, 2 * FH), BF16),
        VMEM((L, 2, G, HJ, PB, 128), F32),
        VMEM((L, 2, G, HJ, PB, 128), BF16),
        VMEM((L, G, HJ, PB, 128), BF16),
        VMEM((L, G, HJ, PB, 128), F32),
        VMEM((L, G, HJ, PB, 128), BF16),
        VMEM((L, G, HJ, PB, 128), BF16),
        VMEM((L, R, HJ, PB, 128), BF16),
        VMEM((L, G, HJ, PB, 128), BF16),
        VMEM((2, 8, 128), F32),
        VMEM((1, 1), F32),
        DMA((n_local,)),
        DMA((n_out,)),
        DMA((n_remote,)),
        DMA((n_remote,)),
        DMA((L, 2)),
        DMA((L, G)),
        DMA((L, G)),
        DMA((L, R)),
        DMA((L, R)),
        DMA((L, G)),
        DMA((L, G)),
        DMA((2,)),
    ]
    any_spec = pl.BlockSpec(memory_space=pl.ANY)
    small = jax.ShapeDtypeStruct((PN, L, D // 2), F32)
    results = pl.pallas_call(
        functools.partial(main_kernel, dims),
        out_shape=(
            jax.ShapeDtypeStruct((T, B, D), BF16),
            jax.ShapeDtypeStruct((T, B, D), F32),
            small,
            jax.ShapeDtypeStruct((1, 1), F32),
            small,
            small,
            small,
        ),
        in_specs=[any_spec] * 12,
        out_specs=(any_spec,) * 7,
        scratch_shapes=scratch,
        compiler_params=pltpu.CompilerParams(
            collective_id=0, has_side_effects=True, vmem_limit_bytes=64 * 2**20
        ),
    )(
        native(tokens), native(cotangent), native(prompts), native(first_moment),
        native(second_moment), norm_params, bias_rows, qkv_weight, out_weight,
        up_weight, up_bias, down_weight,
    )
    act, igrad, grad, norm, new_first, new_second, new_prompts = hand_on(
        (4, 8, 1, 1, 1, 1, 1), results
    )
    return (
        native(act), native(igrad), native(grad), norm.reshape(()),
        native(new_first), native(new_second), native(new_prompts),
    )


def solution(mesh):
    ndp = mesh.shape["dp"]
    return jax.shard_map(
        functools.partial(local, ndp),
        mesh=mesh,
        in_specs=(
            P(("dp", "mlp"), None, None),
            P(("dp", "mlp"), None, None),
            P(None, None, "mlp"),
            P(None, None, "mlp"),
            P(None, None, "mlp"),
            P(),
            P(),
            P(),
            P(),
            P(None, None, "mlp"),
            P(None, "mlp"),
            P(None, "mlp", None),
        ),
        out_specs=(
            P(("dp", "mlp"), None, None),
            P(("dp", "mlp"), None, None),
            P(None, None, "mlp"),
            P(),
            P(None, None, "mlp"),
            P(None, None, "mlp"),
            P(None, None, "mlp"),
        ),
        check_vma=False,
    )
```

```python
import functools

import jax
import jax.numpy as jnp
from jax import lax
from jax.experimental import pallas as pl
from jax.experimental.pallas import tpu as pltpu
from jax.sharding import PartitionSpec as P

HEADS = 12
STEP = 10
MESH = pl.DeviceIdType.MESH
VMEM = pltpu.VMEM
DMA = pltpu.SemaphoreType.DMA
BF16 = jnp.bfloat16
F32 = jnp.float32

norm_eps = 1e-06
clip_limit = 1.0
beta_one = 0.9
beta_two = 0.999
learn_rate = 1.5
weight_decay = 0.05
adam_eps = 1e-08
LOG2E = 1.4426950408889634


def up_to(value, step):
    return -(-value // step) * step


def mm(left, right):
    return jnp.dot(left, right, preferred_element_type=F32)


def mm_nt(left, right):
    return lax.dot_general(left, right, (((1,), (1,)), ((), ())), preferred_element_type=F32)


def mm_tn(left, right):
    return lax.dot_general(left, right, (((0,), (0,)), ((), ())), preferred_element_type=F32)


def rows_loop(count, step, body, unroll=1):
    def one(i, carry):
        body(pl.multiple_of(i * step, step))
        return carry

    lax.fori_loop(0, count // step, one, 0, unroll=unroll)


def main_kernel(
    dims,
    tok_hbm,
    cot_hbm,
    prompts_hbm,
    first_hbm,
    second_hbm,
    norms_hbm,
    bias_hbm,
    qkv_hbm,
    out_hbm,
    up_hbm,
    ub_hbm,
    dn_hbm,
    act_hbm,
    igrad_hbm,
    pgrad_hbm,
    norm_hbm,
    new_first_hbm,
    new_second_hbm,
    new_prompt_hbm,
    tok_nat,
    cot_nat,
    stage_nat,
    prom_nat,
    adam_nat,
    norms,
    bias,
    w_qkv,
    w_out,
    w_up,
    ub,
    w_dn,
    seq,
    hid,
    acc,
    wide,
    x16,
    xh1,
    r1,
    xh2,
    r2,
    q_s,
    k_s,
    v_s,
    e_s,
    ri_s,
    o_s,
    gp_s,
    part_h,
    slot_b,
    slot_c,
    fin,
    sq_out,
    sq_in,
    norm_s,
    local_sem,
    out_sem,
    send_sem,
    recv_sem,
    sem_b,
    sem_c,
    sem_d,
    sem_e,
):
    B, T, D, L, PN, TK, S, TQ, FH, G, R = dims
    H = HEADS
    HD = D // H
    C = 768
    NJ = D // 128
    HJ = NJ // 2
    PB = 16
    core = lax.axis_index("mlp")
    other = 1 - core
    me = lax.axis_index("dp")
    g, r = lax.rem(me, G), me // G
    half = D // 2

    def member(k):
        return lax.rem(g + k, G)

    def rank(k):
        return lax.rem(r + k, R)

    around = [(k, c) for k in range(G) for c in range(2)][1:]

    def neighbour(k, c):
        return {"dp": r * G + member(k), "mlp": lax.rem(core + c, 2)}

    barrier = pltpu.get_barrier_semaphore()
    for k, c in around:
        pl.semaphore_signal(barrier, inc=1, device_id=neighbour(k, c), device_id_type=MESH)

    def greet(k, carry):
        pl.semaphore_signal(
            barrier, inc=1, device_id={"dp": rank(k) * G + g}, device_id_type=MESH
        )
        return carry

    lax.fori_loop(1, R, greet, 0)

    local = {}

    def fetch(name, src, dst):
        copy = pltpu.make_async_copy(src, dst, local_sem.at[len(local)])
        copy.start()
        local[name] = copy

    def fetch_native(name, src, dst, base, count):
        for j in range(count):
            fetch(f"{name}{j}", src.at[:, :, 128 * j : 128 * (j + 1)], dst.at[base + j])

    fetch_native("tok", tok_hbm, tok_nat, 0, NJ)
    fetch_native("prom", prompts_hbm, prom_nat, core * HJ, HJ)
    fetch("norms", norms_hbm, norms)
    fetch("bias", bias_hbm, bias)
    fetch("qkv0", qkv_hbm.at[0], w_qkv.at[0])

    remote = {}

    def push(name, src, dst):
        i = len(remote)
        copy = pltpu.make_async_remote_copy(
            src_ref=src,
            dst_ref=dst,
            send_sem=send_sem.at[i],
            recv_sem=recv_sem.at[i],
            device_id={"mlp": other},
            device_id_type=MESH,
        )
        copy.start()
        remote[name] = copy

    pl.semaphore_wait(barrier, len(around) + R - 1)
    for j in range(HJ):
        push(
            f"prom{j}",
            prompts_hbm.at[:, :, 128 * j : 128 * (j + 1)],
            prom_nat.at[core * HJ + j],
        )
    push("ub", ub_hbm, ub.at[1])
    push("up0", up_hbm.at[0], w_up.at[0, 1])
    push("dn0", dn_hbm.at[0], w_dn.at[0, 1])

    tok_v = tok_nat.reshape(NJ, T * B, 128)
    cot_v = cot_nat.reshape(NJ, T * B, 128)
    stage_v = stage_nat.reshape(NJ, T * B, 128)
    prom_v = prom_nat.reshape(NJ, PN * L, 128)

    lane = lax.broadcasted_iota(jnp.int32, (1, S), 1)
    valid = (lane < T) | ((lane >= TK) & (lane < TK + PN))
    key_bias = jnp.where(valid, 0.0, -1e30).astype(F32)
    even_q = lax.broadcasted_iota(jnp.int32, (TQ, 2 * HD), 1) < HD
    even_k = lax.broadcasted_iota(jnp.int32, (S, 2 * HD), 1) < HD
    SH = S // 2
    even_h = lax.broadcasted_iota(jnp.int32, (SH, 2 * HD), 1) < HD
    low_lane = lax.broadcasted_iota(jnp.int32, (TQ, S), 1) < SH
    scale = HD**-0.5

    def spread(src_v, store):
        for j in range(NJ):
            stage_v[j] = src_v[j].astype(F32)
        for b in range(B):
            for j in range(NJ):
                store(b, slice(128 * j, 128 * (j + 1)), stage_v[j, pl.ds(b, T, stride=B), :])

    for b in range(B):
        seq[b, TK - 8 :, :] = jnp.zeros((S - TK + 8, D), F32)
    for j in range(NJ):
        local[f"tok{j}"].wait()

    def store_tok(b, cols, rows):
        seq[b, 0:T, cols] = rows

    spread(tok_v, store_tok)
    local["norms"].wait()
    local["bias"].wait()
    for j in range(HJ):
        local[f"prom{j}"].wait()
        remote[f"prom{j}"].wait()

    def norm_rows(x):
        mean = jnp.mean(x, axis=-1, keepdims=True)
        centre = x - mean
        spread_ = jnp.mean(centre * centre, axis=-1, keepdims=True)
        inv = lax.rsqrt(spread_ + norm_eps)
        return centre * inv, inv

    def ln_back(dy, xh, inv, gain):
        gdy = dy * gain
        a = jnp.mean(gdy, axis=-1, keepdims=True)
        c = jnp.mean(gdy * xh, axis=-1, keepdims=True)
        return inv * (gdy - a - xh * c)

    def attend_forward(l):
        def pair(i, carry):
            b = i // (H // 2)
            hp = i % (H // 2)
            sl = pl.ds(pl.multiple_of(hp * 2 * HD, 2 * HD), 2 * HD)
            qr = pl.ds(pl.multiple_of(b * TQ, 16), TQ)
            kr = pl.ds(pl.multiple_of(b * S, 16), S)
            q = q_s[l, qr, sl]
            k = k_s[l, kr, sl]
            v = v_s[l, kr, sl]
            sums = []
            for h in range(2):
                here = even_k if h == 0 else jnp.logical_not(even_k)
                s = mm_nt(q, jnp.where(here, k, jnp.zeros_like(k))) + key_bias
                top = jnp.max(s, axis=1, keepdims=True)
                e = jnp.exp2((s - top) * (LOG2E * scale)).astype(BF16)
                e_s[l, b, hp * 2 + h] = e
                sums.append(mm(e, jnp.where(here, v, jnp.ones_like(v))))
            top_part = jnp.where(even_q, sums[0], sums[1])
            total = jnp.where(even_q, sums[1], sums[0])
            inv = pltpu.roll(1.0 / total, HD, 1)
            ri_s[l, qr, sl] = inv.astype(BF16)
            o_s[l, qr, sl] = (top_part * inv).astype(BF16)
            return carry

        lax.fori_loop(0, B * H // 2, pair, 0, unroll=6)

    def back_half(l, b, hp, part, first):
        at = pl.multiple_of(hp * 2 * HD, 2 * HD)
        sl = pl.ds(at, 2 * HD)
        qr = pl.ds(pl.multiple_of(b * TQ, 16), TQ)
        kr = pl.ds(pl.multiple_of(b * S + part * SH, 16), SH)
        v = v_s[l, kr, sl]
        spare = pl.ds(pl.multiple_of((b * (H // 2) + hp) * S, 128), TQ)
        if first:
            do = x16[qr, sl].astype(F32) * ri_s[l, qr, sl].astype(F32)
            prod = do * o_s[l, qr, sl].astype(F32)
            d0 = jnp.sum(jnp.where(even_q, prod, 0.0), axis=1, keepdims=True)
            d1 = jnp.sum(jnp.where(even_q, 0.0, prod), axis=1, keepdims=True)
            do16 = do.astype(BF16)
            q_t = q_s[l, qr, sl].T
            do_t = do16.T
            x16[qr, sl] = do16
            gp_s[l, 0 : 2 * HD, spare] = q_t
            gp_s[l, 2 * HD : 4 * HD, spare] = do_t
            acc[qr, sl] = jnp.where(even_q, d0, d1)
        else:
            do16 = x16[qr, sl]
            q_t = gp_s[l, 0 : 2 * HD, spare]
            do_t = gp_s[l, 2 * HD : 4 * HD, spare]
            both = acc[qr, sl]
            d0, d1 = both[:, 0:1], both[:, HD : HD + 1]
        zero = jnp.zeros_like(v)
        stacked = jnp.concatenate([jnp.where(even_h, v, zero), jnp.where(even_h, zero, v)], axis=0)
        dp = mm_nt(do16, stacked)
        keys = slice(part * SH, (part + 1) * SH)
        e = jnp.concatenate([e_s[l, b, hp * 2, :, keys], e_s[l, b, hp * 2 + 1, :, keys]], axis=1)
        ds = (e.astype(F32) * (dp - jnp.where(low_lane, d0, d1))).astype(BF16)
        dk = mm(q_t, ds)
        dv = mm(do_t, e)
        dk = jnp.concatenate([dk[:HD, :SH], dk[HD:, SH:]], axis=0) * scale
        dv = jnp.concatenate([dv[:HD, :SH], dv[HD:, SH:]], axis=0)
        wide[kr, pl.ds(pl.multiple_of(D + at, 128), 2 * HD)] = dk.astype(BF16).T
        wide[kr, pl.ds(pl.multiple_of(2 * D + at, 128), 2 * HD)] = dv.astype(BF16).T
        return ds

    def back_queries(l, b, hp, low, high):
        at = pl.multiple_of(hp * 2 * HD, 2 * HD)
        sl = pl.ds(at, 2 * HD)
        kr = pl.ds(pl.multiple_of(b * S, 16), S)
        k = k_s[l, kr, sl]
        zero = jnp.zeros_like(k)
        dq = mm(jnp.concatenate([low[:, :SH], high[0]], axis=1), jnp.where(even_k, k, zero))
        dq += mm(jnp.concatenate([low[:, SH:], high[1]], axis=1), jnp.where(even_k, zero, k))
        wide[pl.ds(pl.multiple_of(b * S, 16), TQ), sl] = (dq * scale).astype(BF16)

    def pairs_loop(body, lo, hi):
        def one(i, carry):
            body(i // (H // 2), i % (H // 2))
            return carry

        lax.fori_loop(lo, hi, one, 0, unroll=True)

    pairs = B * H // 2

    def send(src, dst, sems, l, device):
        return pltpu.make_async_remote_copy(
            src_ref=src,
            dst_ref=dst,
            send_sem=sems.at[l, 0],
            recv_sem=sems.at[l, 1],
            device_id=device,
            device_id_type=MESH,
        )

    def all_of(slots, l, count, sems):
        view = slots.at[l, 0:count]
        return send(view, view, sems, l, {"mlp": other})

    mine_b = core * G + g

    def reduce_start(l, grad):
        rows = jnp.concatenate([grad, jnp.zeros((G * PB - grad.shape[0], D), F32)], axis=0)
        for j in range(NJ):
            for k in range(G):
                block = rows[k * PB : (k + 1) * PB, 128 * j : 128 * (j + 1)]
                part_h[l, j // HJ * G + k, j % HJ] = block.astype(BF16)
        for k, c in around:
            to = lax.rem(core + c, 2) * G + member(k)
            send(
                part_h.at[l, to], slot_b.at[l, mine_b], sem_b, l, neighbour(k, c)
            ).start()
        slot_b[l, mine_b] = part_h[l, mine_b]

    def reduce_group(l):
        all_of(slot_b, l, 2 * G - 1, sem_b).wait_recv()
        total = slot_b[l, 0].astype(F32)
        for i in range(1, 2 * G):
            total = total + slot_b[l, i].astype(F32)
        slot_c[l, r] = total.astype(BF16)

        def go(k, carry):
            peer = {"dp": rank(k) * G + g}
            send(slot_c.at[l, r], slot_c.at[l, r], sem_c, l, peer).start()
            return carry

        lax.fori_loop(1, R, go, 0, unroll=R <= 4)
        all_of(part_h, l, 2 * G - 1, sem_b).wait_send()

    def square_of(block):
        block = block.astype(F32)
        total = jnp.sum(jnp.sum(block * block, axis=0), axis=(0, 1), keepdims=True)
        return jnp.broadcast_to(total, (8, 128))

    def reduce_ranks(l):
        if R > 1:
            all_of(slot_c, l, R - 1, sem_c).wait_recv()

        def add(k, total):
            return total + slot_c[l, k].astype(F32)

        total = lax.fori_loop(0, R, add, jnp.zeros((HJ, PB, 128), F32), unroll=R <= 4)
        fin[l, g] = total.astype(BF16)
        for k in range(1, G):
            peer = {"dp": r * G + member(k)}
            send(fin.at[l, g], fin.at[l, g], sem_d, l, peer).start()
        sq_out[l] = square_of(fin[l, g])
        for k in range(G):
            send(sq_out.at[l], sq_in.at[l, g], sem_e, l, neighbour(k, 1)).start()
        if R > 1:
            all_of(slot_c, l, R - 1, sem_c).wait_send()

    def reduce_end(l):
        all_of(fin, l, G - 1, sem_d).wait()
        all_of(sq_in, l, G, sem_e).wait()

    def mlp_chunk(l, part, j, last_):
        cols = slice(j * C, (j + 1) * C)
        at = slice((part * (FH // C) + j) * C, (part * (FH // C) + j + 1) * C)
        pre = mm(x16[...], w_up[l, part, :, cols]) + ub[part, l : l + 1, cols]
        cdf = 0.5 + 0.5 * lax.erf(pre * 0.7071067811865476)
        if last_ != "output":
            bell = jnp.exp2(pre * pre * (-0.5 * LOG2E)) * 0.3989422804014327
            gp_s[l, :, at] = (cdf + pre * bell).astype(BF16)
        if last_ != "slope":
            add = mm((pre * cdf).astype(BF16), w_dn[l, part, cols, :])
            if part == 0 and j == 0:
                acc[...] = add
            else:
                acc[...] += add

    chunks = [(part, j) for part in range(2) for j in range(FH // C)]

    for l in range(L):
        for b in range(B):
            for j in range(NJ):
                seq[b, TK : TK + PN, 128 * j : 128 * (j + 1)] = prom_v[
                    j, pl.ds(l, PN, stride=L), :
                ]
        gain, shift = norms[l, 0:1, :], norms[l, 1:2, :]
        for b in range(B):
            xh, inv = norm_rows(seq[b])
            at = slice(b * S, (b + 1) * S)
            xh1[l, at, :] = xh.astype(BF16)
            r1[l, at, :] = inv
            wide[at, 0:D] = (xh * gain + shift).astype(BF16)
        local[f"qkv{l}"].wait()
        if l == 0:
            fetch("out0", out_hbm.at[0], w_out.at[0])
            fetch("ub", ub_hbm, ub.at[0])
            fetch("up0", up_hbm.at[0], w_up.at[0, 0])
            fetch("dn0", dn_hbm.at[0], w_dn.at[0, 0])
        lhs = jnp.concatenate([wide[b * S : b * S + TQ, 0:D] for b in range(B)], axis=0)
        q_s[l] = (mm(lhs, w_qkv[l, :, 0:D]) + bias[l, 0:1, :]).astype(BF16)
        k_s[l] = mm(wide[:, 0:D], w_qkv[l, :, D : 2 * D]).astype(BF16)
        v_s[l] = (mm(wide[:, 0:D], w_qkv[l, :, 2 * D : 3 * D]) + bias[l, 1:2, :]).astype(BF16)
        attend_forward(l)
        local[f"out{l}"].wait()
        if l == 0:
            for i in range(1, L):
                push(f"up{i}", up_hbm.at[i], w_up.at[i, 1])
                push(f"dn{i}", dn_hbm.at[i], w_dn.at[i, 1])
                fetch(f"qkv{i}", qkv_hbm.at[i], w_qkv.at[i])
                fetch(f"out{i}", out_hbm.at[i], w_out.at[i])
                fetch(f"up{i}", up_hbm.at[i], w_up.at[i, 0])
                fetch(f"dn{i}", dn_hbm.at[i], w_dn.at[i, 0])
            fetch_native("cot", cot_hbm, cot_nat, 0, NJ)
            for j in range(HJ):
                cols = slice(128 * j, 128 * (j + 1))
                fetch(f"first{j}", first_hbm.at[:, :, cols], adam_nat.at[0, j, 0:PN])
                fetch(f"second{j}", second_hbm.at[:, :, cols], adam_nat.at[1, j, 0:PN])
        branch = mm(o_s[l], w_out[l]) + bias[l, 2:3, :]
        for b in range(B):
            hid[b * TQ : (b + 1) * TQ, :] = seq[b, 0:TQ, :] + branch[b * TQ : (b + 1) * TQ]
        gain2, shift2 = norms[l, 2:3, :], norms[l, 3:4, :]

        xh, inv = norm_rows(hid[...])
        xh2[l] = xh.astype(BF16)
        r2[l] = inv
        x16[...] = (xh * gain2 + shift2).astype(BF16)
        if l == 0:
            local["ub"].wait()
            remote["ub"].wait()
        for part, j in chunks:
            if j == 0:
                kept = local if part == 0 else remote
                kept[f"up{l}"].wait()
                kept[f"dn{l}"].wait()
            mlp_chunk(l, part, j, "both" if l < L - 1 else "slope")
        for b in range(B):
            seq[b, 0:TQ, :] = hid[b * TQ : (b + 1) * TQ, :] + bias[l, 3:4, :]
            if l < L - 1:
                seq[b, 0:TQ, :] += acc[b * TQ : (b + 1) * TQ, :]

    leaving = []

    def leave(src, dst):
        copy = pltpu.make_async_copy(src, dst, out_sem.at[len(leaving)])
        copy.start()
        leaving.append(copy)

    def activations_out():
        for b in range(B):
            seq[b, 0:TQ, :] += acc[b * TQ : (b + 1) * TQ, :]
            for j in range(NJ):
                stage_v[j, pl.ds(b, T, stride=B), :] = seq[b, 0:T, 128 * j : 128 * (j + 1)]
        for j in range(NJ):
            tok_v[j] = stage_v[j].astype(BF16)
            leave(tok_nat.at[j], act_hbm.at[:, :, 128 * j : 128 * (j + 1)])

    for j in range(NJ):
        local[f"cot{j}"].wait()
    for b in range(B):
        hid[b * TQ + TK - 8 : (b + 1) * TQ, :] = jnp.zeros((TQ - TK + 8, D), F32)
        wide[b * S + TQ : (b + 1) * S, 0:D] = jnp.zeros((S - TQ, D), BF16)

    def store_cot(b, cols, rows):
        hid[b * TQ : b * TQ + T, cols] = rows

    spread(cot_v, store_cot)

    for l in reversed(range(L)):
        last = l == 0
        above = l + 1
        x16[...] = hid[...].astype(BF16)
        for part in range(2):
            for j in range(FH // C):
                cols = slice(j * C, (j + 1) * C)
                at = slice((part * (FH // C) + j) * C, (part * (FH // C) + j + 1) * C)
                ga = mm_nt(x16[...], w_dn[l, part, cols, :])
                gpre = (gp_s[l, :, at].astype(F32) * ga).astype(BF16)
                add = mm_nt(gpre, w_up[l, part, :, cols])
                if part == 0 and j == 0:
                    acc[...] = add
                else:
                    acc[...] += add
            if above < L and part == 0:
                reduce_group(above)
        gain2 = norms[l, 2:3, :]

        new = hid[...] + ln_back(acc[...], xh2[l].astype(F32), r2[l], gain2)
        hid[...] = new
        x16[...] = new.astype(BF16)
        x16[...] = mm_nt(x16[...], w_out[l]).astype(BF16)
        gain = norms[l, 0:1, :]

        def high_keys(b, hp):
            ds = back_half(l, b, hp, 1, True)
            e_s[l, b, hp * 2, :, SH:] = ds[:, :SH]
            e_s[l, b, hp * 2 + 1, :, SH:] = ds[:, SH:]

        def low_keys(b, hp):
            ds = back_half(l, b, hp, 0, False)
            back_queries(
                l, b, hp, ds, (e_s[l, b, hp * 2, :, SH:], e_s[l, b, hp * 2 + 1, :, SH:])
            )

        def prompt_gradient():
            base = TK // 16 * 16
            lhs = jnp.concatenate(
                [wide[b * S + base : (b + 1) * S, D : 3 * D] for b in range(B)], axis=0
            )
            full = mm_nt(lhs, w_qkv[l, :, D : 3 * D])
            n = S - base
            dprom = full[TK - base : n]
            for b in range(1, B):
                dprom = dprom + full[b * n + TK - base : (b + 1) * n]
            xh_p = xh1[l, base:S, :].astype(F32)[TK - base :]
            return ln_back(dprom, xh_p, r1[l, TK:S, :], gain)

        pairs_loop(high_keys, 0, pairs)
        if above < L:
            reduce_ranks(above)
        reduce_start(l, prompt_gradient())
        pairs_loop(low_keys, 0, pairs)
        if above < L:
            reduce_end(above)
        lhs = jnp.concatenate([wide[b * S : b * S + TQ, :] for b in range(B)], axis=0)
        acc[...] = mm_nt(lhs, w_qkv[l])
        if last:
            reduce_group(l)
        for b in range(B):
            at = slice(b * TQ, b * TQ + TK)
            dx = ln_back(
                acc[at, :],
                xh1[l, b * S : b * S + TQ, :].astype(F32)[:TK],
                r1[l, b * S : b * S + TK, :],
                gain,
            )
            hid[at, :] = hid[at, :] + dx

    x16[...] = (xh2[L - 1].astype(F32) * norms[L - 1, 2:3, :] + norms[L - 1, 3:4, :]).astype(BF16)
    for i, (part, j) in enumerate(chunks):
        if i == len(chunks) - 1:
            reduce_ranks(0)
        mlp_chunk(L - 1, part, j, "output")
    activations_out()
    for j in range(NJ):
        for b in range(B):
            stage_v[j, pl.ds(b, T, stride=B), :] = hid[
                b * TQ : b * TQ + T, 128 * j : 128 * (j + 1)
            ]
        leave(stage_nat.at[j], igrad_hbm.at[:, :, 128 * j : 128 * (j + 1)])
    reduce_end(0)

    grad_v = adam_nat.at[2].reshape(HJ, G * PB * L, 128)
    for l in range(L):
        for k in range(G):
            for j in range(HJ):
                grad_v[j, pl.ds(k * PB * L + l, PB, stride=L), :] = fin[l, k, j].astype(F32)
    n = PN * L
    for j in range(HJ):
        leave(adam_nat.at[2, j, 0:PN], pgrad_hbm.at[:, :, 128 * j : 128 * (j + 1)])
    own, theirs = jnp.zeros((8, 128), F32), jnp.zeros((8, 128), F32)
    for l in range(L):
        for k in range(G):
            own += square_of(fin[l, k])
            theirs += sq_in[l, k]
    squares = own + theirs
    grad_norm = jnp.sqrt(squares)
    norm_s[...] = grad_norm[0:1, 0:1]
    leave(norm_s, norm_hbm)
    factor = jnp.minimum(1.0, clip_limit / (grad_norm[0:1, :] + 1e-06))
    fix_first = 1.0 - beta_one**STEP
    fix_second = 1.0 - beta_two**STEP
    for j in range(HJ):
        local[f"first{j}"].wait()
        local[f"second{j}"].wait()
        first_v = adam_nat.at[0].reshape(HJ, G * PB * L, 128)
        second_v = adam_nat.at[1].reshape(HJ, G * PB * L, 128)
        clipped = grad_v[j, 0:n, :] * factor
        new_first = beta_one * first_v[j, 0:n, :] + (1.0 - beta_one) * clipped
        new_second = beta_two * second_v[j, 0:n, :] + (1.0 - beta_two) * clipped * clipped
        first_v[j, 0:n, :] = new_first
        second_v[j, 0:n, :] = new_second
        old = prom_v[core * HJ + j]
        prom_v[core * HJ + j] = old - learn_rate * (
            new_first / fix_first / (jnp.sqrt(new_second / fix_second) + adam_eps)
            + weight_decay * old
        )
        cols = slice(128 * j, 128 * (j + 1))
        leave(adam_nat.at[0, j, 0:PN], new_first_hbm.at[:, :, cols])
        leave(adam_nat.at[1, j, 0:PN], new_second_hbm.at[:, :, cols])
        leave(prom_nat.at[core * HJ + j], new_prompt_hbm.at[:, :, cols])
    for copy in leaving:
        copy.wait()


def hand_on_kernel(parts, *refs):
    n = len(parts)
    sources, targets, held, sem_in, sem_out = (
        refs[:n], refs[n : 2 * n], refs[2 * n : 3 * n], refs[3 * n], refs[3 * n + 1]
    )
    come, go = [], []
    for src, dst, mid, count in zip(sources, targets, held, parts):
        rows = src.shape[0]
        for i in range(count):
            lo, hi = rows * i // count, rows * (i + 1) // count
            a, b, c = (src, mid, dst) if count == 1 else (r.at[lo:hi] for r in (src, mid, dst))
            come.append(pltpu.make_async_copy(a, b, sem_in.at[len(come)]))
            go.append(pltpu.make_async_copy(b, c, sem_out.at[len(go)]))
    for copy in come:
        copy.start()
    for first, second in zip(come, go):
        first.wait()
        second.start()
    for copy in go:
        copy.wait()


def hand_on(parts, arrays):
    any_spec = pl.BlockSpec(memory_space=pl.ANY)
    return pl.pallas_call(
        functools.partial(hand_on_kernel, parts),
        out_shape=tuple(jax.ShapeDtypeStruct(a.shape, a.dtype) for a in arrays),
        in_specs=[any_spec] * len(arrays),
        out_specs=(any_spec,) * len(arrays),
        scratch_shapes=[VMEM(a.shape, a.dtype) for a in arrays]
        + [DMA((sum(parts),)), DMA((sum(parts),))],
        compiler_params=pltpu.CompilerParams(vmem_limit_bytes=60 * 2**20),
    )(*arrays)


def native(x):
    return x.transpose(1, 0, 2)


def local(
    ndp, tokens, cotangent, prompts, first_moment, second_moment, norm_params, bias_rows,
    qkv_weight, out_weight, up_weight, up_bias, down_weight,
):
    B, T, D = tokens.shape
    L, PN, _ = prompts.shape
    FH = down_weight.shape[1]
    TK = up_to(T, 8)
    S = up_to(TK + up_to(PN, 8), 128)
    TQ = up_to(T, 16)
    G = 4
    R = ndp // G
    NJ, HJ, PB = D // 128, D // 256, 16
    dims = (B, T, D, L, PN, TK, S, TQ, FH, G, R)
    H = HEADS
    n_local = 2 * NJ + 3 * HJ + 3 + 4 * L
    n_remote = HJ + 1 + 2 * L
    n_out = 2 * NJ + 4 * HJ + 1
    scratch = [
        VMEM((NJ, T, B, 128), BF16),
        VMEM((NJ, T, B, 128), BF16),
        VMEM((NJ, T, B, 128), F32),
        VMEM((NJ, PN, L, 128), F32),
        VMEM((3, HJ, G * PB, L, 128), F32),
        VMEM((L, 4, D), F32),
        VMEM((L, 4, D), F32),
        VMEM((L, D, 3 * D), BF16),
        VMEM((L, D, D), BF16),
        VMEM((L, 2, D, FH), BF16),
        VMEM((2, L, FH), F32),
        VMEM((L, 2, FH, D), BF16),
        VMEM((B, S, D), F32),
        VMEM((B * TQ, D), F32),
        VMEM((B * TQ, D), F32),
        VMEM((B * S, 3 * D), BF16),
        VMEM((B * TQ, D), BF16),
        VMEM((L, B * S, D), BF16),
        VMEM((L, B * S, 1), F32),
        VMEM((L, B * TQ, D), BF16),
        VMEM((L, B * TQ, 1), F32),
        VMEM((L, B * TQ, D), BF16),
        VMEM((L, B * S, D), BF16),
        VMEM((L, B * S, D), BF16),
        VMEM((L, B, H, TQ, S), BF16),
        VMEM((L, B * TQ, D), BF16),
        VMEM((L, B * TQ, D), BF16),
        VMEM((L, B * TQ, 2 * FH), BF16),
        VMEM((L, 2 * G, HJ, PB, 128), BF16),
        VMEM((L, 2 * G, HJ, PB, 128), BF16),
        VMEM((L, R, HJ, PB, 128), BF16),
        VMEM((L, G, HJ, PB, 128), BF16),
        VMEM((L, 8, 128), F32),
        VMEM((L, G, 8, 128), F32),
        VMEM((1, 1), F32),
        DMA((n_local,)),
        DMA((n_out,)),
        DMA((n_remote,)),
        DMA((n_remote,)),
        DMA((L, 2)),
        DMA((L, 2)),
        DMA((L, 2)),
        DMA((L, 2)),
    ]
    any_spec = pl.BlockSpec(memory_space=pl.ANY)
    small = jax.ShapeDtypeStruct((PN, L, D // 2), F32)
    results = pl.pallas_call(
        functools.partial(main_kernel, dims),
        out_shape=(
            jax.ShapeDtypeStruct((T, B, D), BF16),
            jax.ShapeDtypeStruct((T, B, D), F32),
            small,
            jax.ShapeDtypeStruct((1, 1), F32),
            small,
            small,
            small,
        ),
        in_specs=[any_spec] * 12,
        out_specs=(any_spec,) * 7,
        scratch_shapes=scratch,
        compiler_params=pltpu.CompilerParams(
            collective_id=0, has_side_effects=True, vmem_limit_bytes=64 * 2**20
        ),
    )(
        native(tokens), native(cotangent), native(prompts), native(first_moment),
        native(second_moment), norm_params, bias_rows, qkv_weight, out_weight,
        up_weight, up_bias, down_weight,
    )
    act, igrad, grad, norm, new_first, new_second, new_prompts = hand_on(
        (4, 8, 1, 1, 1, 1, 1), results
    )
    return (
        native(act), native(igrad), native(grad), norm.reshape(()),
        native(new_first), native(new_second), native(new_prompts),
    )


def solution(mesh):
    ndp = mesh.shape["dp"]
    return jax.shard_map(
        functools.partial(local, ndp),
        mesh=mesh,
        in_specs=(
            P(("dp", "mlp"), None, None),
            P(("dp", "mlp"), None, None),
            P(None, None, "mlp"),
            P(None, None, "mlp"),
            P(None, None, "mlp"),
            P(),
            P(),
            P(),
            P(),
            P(None, None, "mlp"),
            P(None, "mlp"),
            P(None, "mlp", None),
        ),
        out_specs=(
            P(("dp", "mlp"), None, None),
            P(("dp", "mlp"), None, None),
            P(None, None, "mlp"),
            P(),
            P(None, None, "mlp"),
            P(None, None, "mlp"),
            P(None, None, "mlp"),
        ),
        check_vma=False,
    )
```

```python
import functools

import jax
import jax.numpy as jnp
from jax import lax
from jax.experimental import pallas as pl
from jax.experimental.pallas import tpu as pltpu
from jax.sharding import PartitionSpec as P

HEADS = 12
STEP = 10
MESH = pl.DeviceIdType.MESH
VMEM = pltpu.VMEM
DMA = pltpu.SemaphoreType.DMA
BF16 = jnp.bfloat16
F32 = jnp.float32

norm_eps = 1e-06
clip_limit = 1.0
beta_one = 0.9
beta_two = 0.999
learn_rate = 1.5
weight_decay = 0.05
adam_eps = 1e-08
LOG2E = 1.4426950408889634


def up_to(value, step):
    return -(-value // step) * step


def mm(left, right):
    return jnp.dot(left, right, preferred_element_type=F32)


def mm_nt(left, right):
    return lax.dot_general(left, right, (((1,), (1,)), ((), ())), preferred_element_type=F32)


def mm_tn(left, right):
    return lax.dot_general(left, right, (((0,), (0,)), ((), ())), preferred_element_type=F32)


def rows_loop(count, step, body, unroll=1):
    def one(i, carry):
        body(pl.multiple_of(i * step, step))
        return carry

    lax.fori_loop(0, count // step, one, 0, unroll=unroll)


def main_kernel(
    dims,
    tok_hbm,
    cot_hbm,
    prompts_hbm,
    first_hbm,
    second_hbm,
    norms_hbm,
    bias_hbm,
    qkv_hbm,
    out_hbm,
    up_hbm,
    ub_hbm,
    dn_hbm,
    tok_nat,
    stage_nat,
    grad_nat,
    norm_s,
    first_nat,
    second_nat,
    prompt_nat,
    cot_nat,
    prom_nat,
    norms,
    bias,
    w_qkv,
    w_out,
    w_up,
    ub,
    w_dn,
    seq,
    hid,
    acc,
    wide,
    x16,
    xh1,
    xh2,
    inv_s,
    q_s,
    k_s,
    v_s,
    e_s,
    ri_s,
    o_s,
    gp_s,
    part_h,
    slot_b,
    slot_c,
    fin,
    sq_out,
    sq_in,
    local_sem,
    weight_sem,
    push_sem,
    push_w_sem,
    sem_b,
    sem_c,
    sem_d,
    sem_e,
):
    B, T, D, L, PN, TK, S, TQ, FH, G, R = dims
    H = HEADS
    HD = D // H
    C = 768
    NJ = D // 128
    HJ = NJ // 2
    PB = 16
    core = lax.axis_index("mlp")
    other = 1 - core
    me = lax.axis_index("dp")
    g, r = lax.rem(me, G), me // G
    half = D // 2

    def member(k):
        return lax.rem(g + k, G)

    def rank(k):
        return lax.rem(r + k, R)

    around = [(k, c) for k in range(G) for c in range(2)][1:]

    def neighbour(k, c):
        return {"dp": r * G + member(k), "mlp": lax.rem(core + c, 2)}

    barrier = pltpu.get_barrier_semaphore()
    for k, c in around:
        pl.semaphore_signal(barrier, inc=1, device_id=neighbour(k, c), device_id_type=MESH)

    def greet(k, carry):
        pl.semaphore_signal(
            barrier, inc=1, device_id={"dp": rank(k) * G + g}, device_id_type=MESH
        )
        return carry

    lax.fori_loop(1, R, greet, 0)

    def columns(j):
        return slice(128 * j, 128 * (j + 1))

    def local(i, src, dst):
        return pltpu.make_async_copy(src, dst, local_sem.at[i])

    def copy_tok(j):
        return local(j, tok_hbm.at[:, :, columns(j)], tok_nat.at[j])

    def copy_cot(j):
        return local(NJ + j, cot_hbm.at[:, :, columns(j)], cot_nat.at[j])

    def copy_prom(j):
        return local(2 * NJ + j, prompts_hbm.at[:, :, columns(j)], prom_nat.at[core * HJ + j])

    def copy_moment(i, j):
        src = (first_hbm, second_hbm)[i]
        return local(
            2 * NJ + (i + 1) * HJ + j, src.at[:, :, columns(j)], (first_nat, second_nat)[i].at[j]
        )

    def copy_small(i):
        src, dst = ((norms_hbm, norms), (bias_hbm, bias), (ub_hbm, ub.at[0]))[i]
        return local(2 * NJ + 3 * HJ + i, src, dst)

    def copy_weight(l, i):
        src, dst = (
            (qkv_hbm.at[l], w_qkv.at[l]),
            (out_hbm.at[l], w_out.at[l]),
            (up_hbm.at[l], w_up.at[l, 0]),
            (dn_hbm.at[l], w_dn.at[l, 0]),
        )[i]
        return pltpu.make_async_copy(src, dst, weight_sem.at[l, i])

    def push(src, dst, send_at, recv_at):
        return pltpu.make_async_remote_copy(
            src_ref=src,
            dst_ref=dst,
            send_sem=send_at,
            recv_sem=recv_at,
            device_id={"mlp": other},
            device_id_type=MESH,
        )

    def push_prom(j):
        return push(
            prompts_hbm.at[:, :, columns(j)],
            prom_nat.at[core * HJ + j],
            push_sem.at[0, j],
            push_sem.at[1, j],
        )

    def push_ub():
        return push(ub_hbm, ub.at[1], push_sem.at[0, HJ], push_sem.at[1, HJ])

    def push_weight(l, i):
        src, dst = ((up_hbm.at[l], w_up.at[l, 1]), (dn_hbm.at[l], w_dn.at[l, 1]))[i]
        return push(src, dst, push_w_sem.at[l, 0, i], push_w_sem.at[l, 1, i])

    for j in range(NJ):
        copy_tok(j).start()
    for j in range(HJ):
        copy_prom(j).start()
    copy_small(0).start()
    copy_small(1).start()
    copy_weight(0, 0).start()
    pl.semaphore_wait(barrier, len(around) + R - 1)
    for j in range(HJ):
        push_prom(j).start()
    push_ub().start()
    push_weight(0, 0).start()
    push_weight(0, 1).start()

    tok_v = tok_nat.reshape(NJ, T * B, 128)
    cot_v = cot_nat.reshape(NJ, T * B, 128)
    stage_v = stage_nat.reshape(NJ, T * B, 128)
    prom_v = prom_nat.reshape(NJ, PN * L, 128)

    lane = lax.broadcasted_iota(jnp.int32, (1, S), 1)
    valid = (lane < T) | ((lane >= TK) & (lane < TK + PN))
    key_bias = jnp.where(valid, 0.0, -1e30).astype(F32)
    even_q = lax.broadcasted_iota(jnp.int32, (TQ, 2 * HD), 1) < HD
    even_k = lax.broadcasted_iota(jnp.int32, (S, 2 * HD), 1) < HD
    SH = S // 2
    even_h = lax.broadcasted_iota(jnp.int32, (SH, 2 * HD), 1) < HD
    low_lane = lax.broadcasted_iota(jnp.int32, (TQ, S), 1) < SH
    scale = HD**-0.5

    def spread(src_v, store):
        for j in range(NJ):
            stage_v[j] = src_v[j].astype(F32)
        for b in range(B):
            for j in range(NJ):
                store(b, slice(128 * j, 128 * (j + 1)), stage_v[j, pl.ds(b, T, stride=B), :])

    for b in range(B):
        seq[b, TK - 8 :, :] = jnp.zeros((S - TK + 8, D), F32)
    for j in range(NJ):
        copy_tok(j).wait()

    def store_tok(b, cols, rows):
        seq[b, 0:T, cols] = rows

    spread(tok_v, store_tok)
    copy_small(0).wait()
    copy_small(1).wait()
    for j in range(HJ):
        copy_prom(j).wait()
        push_prom(j).wait()

    def norm_rows(x):
        mean = jnp.mean(x, axis=-1, keepdims=True)
        centre = x - mean
        spread_ = jnp.mean(centre * centre, axis=-1, keepdims=True)
        inv = lax.rsqrt(spread_ + norm_eps)
        return centre * inv, inv

    def ln_back(dy, xh, inv, gain):
        gdy = dy * gain
        a = jnp.mean(gdy, axis=-1, keepdims=True)
        c = jnp.mean(gdy * xh, axis=-1, keepdims=True)
        return inv * (gdy - a - xh * c)

    def attend_forward(l):
        def pair(i, carry):
            b = i // (H // 2)
            hp = i % (H // 2)
            sl = pl.ds(pl.multiple_of(hp * 2 * HD, 2 * HD), 2 * HD)
            qr = pl.ds(pl.multiple_of(b * TQ, 16), TQ)
            kr = pl.ds(pl.multiple_of(b * S, 16), S)
            q = q_s[l, qr, sl]
            k = k_s[l, kr, sl]
            v = v_s[l, kr, sl]
            sums = []
            for h in range(2):
                here = even_k if h == 0 else jnp.logical_not(even_k)
                s = mm_nt(q, jnp.where(here, k, jnp.zeros_like(k))) + key_bias
                top = jnp.max(s, axis=1, keepdims=True)
                e = jnp.exp2((s - top) * (LOG2E * scale)).astype(BF16)
                e_s[l, b, hp * 2 + h] = e
                sums.append(mm(e, jnp.where(here, v, jnp.ones_like(v))))
            top_part = jnp.where(even_q, sums[0], sums[1])
            total = jnp.where(even_q, sums[1], sums[0])
            inv = pltpu.roll(1.0 / total, HD, 1)
            ri_s[l, qr, sl] = inv.astype(BF16)
            o_s[l, qr, sl] = (top_part * inv).astype(BF16)
            return carry

        lax.fori_loop(0, B * H // 2, pair, 0, unroll=6)

    def back_half(l, b, hp, part, first):
        at = pl.multiple_of(hp * 2 * HD, 2 * HD)
        sl = pl.ds(at, 2 * HD)
        qr = pl.ds(pl.multiple_of(b * TQ, 16), TQ)
        kr = pl.ds(pl.multiple_of(b * S + part * SH, 16), SH)
        v = v_s[l, kr, sl]
        spare = pl.ds(pl.multiple_of((b * (H // 2) + hp) * S, 128), TQ)
        if first:
            do = x16[qr, sl].astype(F32) * ri_s[l, qr, sl].astype(F32)
            prod = do * o_s[l, qr, sl].astype(F32)
            d0 = jnp.sum(jnp.where(even_q, prod, 0.0), axis=1, keepdims=True)
            d1 = jnp.sum(jnp.where(even_q, 0.0, prod), axis=1, keepdims=True)
            do16 = do.astype(BF16)
            q_t = q_s[l, qr, sl].T
            do_t = do16.T
            x16[qr, sl] = do16
            gp_s[l, 0 : 2 * HD, spare] = q_t
            gp_s[l, 2 * HD : 4 * HD, spare] = do_t
            acc[qr, sl] = jnp.where(even_q, d0, d1)
        else:
            do16 = x16[qr, sl]
            q_t = gp_s[l, 0 : 2 * HD, spare]
            do_t = gp_s[l, 2 * HD : 4 * HD, spare]
            both = acc[qr, sl]
            d0, d1 = both[:, 0:1], both[:, HD : HD + 1]
        zero = jnp.zeros_like(v)
        stacked = jnp.concatenate([jnp.where(even_h, v, zero), jnp.where(even_h, zero, v)], axis=0)
        dp = mm_nt(do16, stacked)
        keys = slice(part * SH, (part + 1) * SH)
        e = jnp.concatenate([e_s[l, b, hp * 2, :, keys], e_s[l, b, hp * 2 + 1, :, keys]], axis=1)
        ds = (e.astype(F32) * (dp - jnp.where(low_lane, d0, d1))).astype(BF16)
        dk = mm(q_t, ds)
        dv = mm(do_t, e)
        dk = jnp.concatenate([dk[:HD, :SH], dk[HD:, SH:]], axis=0) * scale
        dv = jnp.concatenate([dv[:HD, :SH], dv[HD:, SH:]], axis=0)
        wide[kr, pl.ds(pl.multiple_of(D + at, 128), 2 * HD)] = dk.astype(BF16).T
        wide[kr, pl.ds(pl.multiple_of(2 * D + at, 128), 2 * HD)] = dv.astype(BF16).T
        return ds

    def back_queries(l, b, hp, low, high):
        at = pl.multiple_of(hp * 2 * HD, 2 * HD)
        sl = pl.ds(at, 2 * HD)
        kr = pl.ds(pl.multiple_of(b * S, 16), S)
        k = k_s[l, kr, sl]
        zero = jnp.zeros_like(k)
        dq = mm(jnp.concatenate([low[:, :SH], high[0]], axis=1), jnp.where(even_k, k, zero))
        dq += mm(jnp.concatenate([low[:, SH:], high[1]], axis=1), jnp.where(even_k, zero, k))
        wide[pl.ds(pl.multiple_of(b * S, 16), TQ), sl] = (dq * scale).astype(BF16)

    def pairs_loop(body, lo, hi):
        def one(i, carry):
            body(i // (H // 2), i % (H // 2))
            return carry

        lax.fori_loop(lo, hi, one, 0, unroll=True)

    pairs = B * H // 2

    def send(src, dst, sems, l, device):
        return pltpu.make_async_remote_copy(
            src_ref=src,
            dst_ref=dst,
            send_sem=sems.at[l, 0],
            recv_sem=sems.at[l, 1],
            device_id=device,
            device_id_type=MESH,
        )

    def all_of(slots, l, count, sems):
        view = slots.at[l, 0:count]
        return send(view, view, sems, l, {"mlp": other})

    mine_b = core * G + g

    def reduce_start(l, grad):
        rows = jnp.concatenate([grad, jnp.zeros((G * PB - grad.shape[0], D), F32)], axis=0)
        for j in range(NJ):
            for k in range(G):
                block = rows[k * PB : (k + 1) * PB, 128 * j : 128 * (j + 1)]
                part_h[l, j // HJ * G + k, j % HJ] = block.astype(BF16)
        for k, c in around:
            to = lax.rem(core + c, 2) * G + member(k)
            send(
                part_h.at[l, to], slot_b.at[l, mine_b], sem_b, l, neighbour(k, c)
            ).start()
        slot_b[l, mine_b] = part_h[l, mine_b]

    def reduce_group(l):
        all_of(slot_b, l, 2 * G - 1, sem_b).wait_recv()
        total = slot_b[l, 0].astype(F32)
        for i in range(1, 2 * G):
            total = total + slot_b[l, i].astype(F32)
        slot_c[l, r] = total.astype(BF16)

        def go(k, carry):
            peer = {"dp": rank(k) * G + g}
            send(slot_c.at[l, r], slot_c.at[l, r], sem_c, l, peer).start()
            return carry

        lax.fori_loop(1, R, go, 0, unroll=R <= 4)
        all_of(part_h, l, 2 * G - 1, sem_b).wait_send()

    def square_of(block):
        block = block.astype(F32)
        total = jnp.sum(jnp.sum(block * block, axis=0), axis=(0, 1), keepdims=True)
        return jnp.broadcast_to(total, (8, 128))

    def reduce_ranks(l):
        if R > 1:
            all_of(slot_c, l, R - 1, sem_c).wait_recv()

        def add(k, total):
            return total + slot_c[l, k].astype(F32)

        total = lax.fori_loop(0, R, add, jnp.zeros((HJ, PB, 128), F32), unroll=R <= 4)
        fin[l, g] = total.astype(BF16)
        for k in range(1, G):
            peer = {"dp": r * G + member(k)}
            send(fin.at[l, g], fin.at[l, g], sem_d, l, peer).start()
        sq_out[l] = square_of(fin[l, g])
        for k in range(G):
            send(sq_out.at[l], sq_in.at[l, g], sem_e, l, neighbour(k, 1)).start()
        if R > 1:
            all_of(slot_c, l, R - 1, sem_c).wait_send()

    def reduce_end(l):
        all_of(fin, l, G - 1, sem_d).wait()
        all_of(sq_in, l, G, sem_e).wait()

    def mlp_chunk(l, part, j, last_):
        cols = slice(j * C, (j + 1) * C)
        at = slice((part * (FH // C) + j) * C, (part * (FH // C) + j + 1) * C)
        pre = mm(x16[...], w_up[l, part, :, cols]) + ub[part, pl.ds(l, 1), cols]
        cdf = 0.5 + 0.5 * lax.erf(pre * 0.7071067811865476)
        if last_ != "output":
            bell = jnp.exp2(pre * pre * (-0.5 * LOG2E)) * 0.3989422804014327
            gp_s[l, :, at] = (cdf + pre * bell).astype(BF16)
        if last_ != "slope":
            add = mm((pre * cdf).astype(BF16), w_dn[l, part, cols, :])
            if part == 0 and j == 0:
                acc[...] = add
            else:
                acc[...] += add

    chunks = [(part, j) for part in range(2) for j in range(FH // C)]

    def forward(l, carry):
        for b in range(B):
            for j in range(NJ):
                seq[b, TK : TK + PN, columns(j)] = prom_v[j, pl.ds(l, PN, stride=L), :]
        gain, shift = norms[l, 0:1, :], norms[l, 1:2, :]
        for b in range(B):
            xh, inv = norm_rows(seq[b])
            at = slice(b * S, (b + 1) * S)
            xh1[l, at, :] = xh.astype(BF16)
            inv_s[l, at, 0:1] = inv
            wide[at, 0:D] = (xh * gain + shift).astype(BF16)
        copy_weight(l, 0).wait()

        @pl.when(l == 0)
        def _():
            copy_small(2).start()
            for i in range(1, 4):
                copy_weight(0, i).start()

        lhs = jnp.concatenate([wide[b * S : b * S + TQ, 0:D] for b in range(B)], axis=0)
        q_s[l] = (mm(lhs, w_qkv[l, :, 0:D]) + bias[l, 0:1, :]).astype(BF16)
        k_s[l] = mm(wide[:, 0:D], w_qkv[l, :, D : 2 * D]).astype(BF16)
        v_s[l] = (mm(wide[:, 0:D], w_qkv[l, :, 2 * D : 3 * D]) + bias[l, 1:2, :]).astype(BF16)
        attend_forward(l)
        copy_weight(l, 1).wait()

        @pl.when(l == 0)
        def _():
            for later in range(1, L):
                for i in range(2):
                    push_weight(later, i).start()
                for i in range(4):
                    copy_weight(later, i).start()
            for j in range(NJ):
                copy_cot(j).start()
            for j in range(HJ):
                copy_moment(0, j).start()
                copy_moment(1, j).start()

        branch = mm(o_s[l], w_out[l]) + bias[l, 2:3, :]
        for b in range(B):
            hid[b * TQ : (b + 1) * TQ, :] = seq[b, 0:TQ, :] + branch[b * TQ : (b + 1) * TQ]
        gain2, shift2 = norms[l, 2:3, :], norms[l, 3:4, :]
        xh, inv = norm_rows(hid[...])
        xh2[l] = xh.astype(BF16)
        inv_s[l, 0 : B * TQ, 1:2] = inv
        x16[...] = (xh * gain2 + shift2).astype(BF16)

        @pl.when(l == 0)
        def _():
            copy_small(2).wait()
            push_ub().wait()

        copy_weight(l, 2).wait()
        copy_weight(l, 3).wait()

        @pl.when(l < L - 1)
        def _():
            for part, j in chunks:
                if part == 1 and j == 0:
                    push_weight(l, 0).wait()
                    push_weight(l, 1).wait()
                mlp_chunk(l, part, j, "both")
            for b in range(B):
                at = slice(b * TQ, (b + 1) * TQ)
                seq[b, 0:TQ, :] = hid[at, :] + acc[at, :] + bias[l, 3:4, :]

        return carry

    lax.fori_loop(0, L, forward, 0)
    for part, j in chunks:
        if part == 1 and j == 0:
            push_weight(L - 1, 0).wait()
            push_weight(L - 1, 1).wait()
        mlp_chunk(L - 1, part, j, "slope")
    for b in range(B):
        seq[b, 0:TQ, :] = hid[b * TQ : (b + 1) * TQ, :] + bias[L - 1, 3:4, :]

    def activations_out():
        for b in range(B):
            seq[b, 0:TQ, :] += acc[b * TQ : (b + 1) * TQ, :]
            for j in range(NJ):
                stage_v[j, pl.ds(b, T, stride=B), :] = seq[b, 0:T, 128 * j : 128 * (j + 1)]
        for j in range(NJ):
            tok_v[j] = stage_v[j].astype(BF16)

    for j in range(NJ):
        copy_cot(j).wait()
    for b in range(B):
        hid[b * TQ + TK - 8 : (b + 1) * TQ, :] = jnp.zeros((TQ - TK + 8, D), F32)

    def store_cot(b, cols, rows):
        hid[b * TQ : b * TQ + T, cols] = rows

    spread(cot_v, store_cot)

    def backward(step, carry):
        l = L - 1 - step
        above = l + 1

        def sum_above(phase):
            pl.when(step > 0)(lambda: phase(above))

        x16[...] = hid[...].astype(BF16)
        for part in range(2):
            for j in range(FH // C):
                cols = slice(j * C, (j + 1) * C)
                at = slice((part * (FH // C) + j) * C, (part * (FH // C) + j + 1) * C)
                ga = mm_nt(x16[...], w_dn[l, part, cols, :])
                gpre = (gp_s[l, :, at].astype(F32) * ga).astype(BF16)
                add = mm_nt(gpre, w_up[l, part, :, cols])
                if part == 0 and j == 0:
                    acc[...] = add
                else:
                    acc[...] += add
            if part == 0:
                sum_above(reduce_group)
        gain2 = norms[l, 2:3, :]

        new = hid[...] + ln_back(
            acc[...], xh2[l].astype(F32), inv_s[l, 0 : B * TQ, 1:2], gain2
        )
        hid[...] = new
        x16[...] = new.astype(BF16)
        x16[...] = mm_nt(x16[...], w_out[l]).astype(BF16)
        gain = norms[l, 0:1, :]

        def high_keys(b, hp):
            ds = back_half(l, b, hp, 1, True)
            e_s[l, b, hp * 2, :, SH:] = ds[:, :SH]
            e_s[l, b, hp * 2 + 1, :, SH:] = ds[:, SH:]

        def low_keys(b, hp):
            ds = back_half(l, b, hp, 0, False)
            back_queries(
                l, b, hp, ds, (e_s[l, b, hp * 2, :, SH:], e_s[l, b, hp * 2 + 1, :, SH:])
            )

        def prompt_gradient():
            base = TK // 16 * 16
            lhs = jnp.concatenate(
                [wide[b * S + base : (b + 1) * S, D : 3 * D] for b in range(B)], axis=0
            )
            full = mm_nt(lhs, w_qkv[l, :, D : 3 * D])
            n = S - base
            dprom = full[TK - base : n]
            for b in range(1, B):
                dprom = dprom + full[b * n + TK - base : (b + 1) * n]
            xh_p = xh1[l, base:S, :].astype(F32)[TK - base :]
            return ln_back(dprom, xh_p, inv_s[l, TK:S, 0:1], gain)

        pairs_loop(high_keys, 0, pairs)
        sum_above(reduce_ranks)
        reduce_start(l, prompt_gradient())
        pairs_loop(low_keys, 0, pairs)
        sum_above(reduce_end)
        lhs = jnp.concatenate([wide[b * S : b * S + TQ, :] for b in range(B)], axis=0)
        acc[...] = mm_nt(lhs, w_qkv[l])
        pl.when(l == 0)(lambda: reduce_group(l))
        for b in range(B):
            at = slice(b * TQ, b * TQ + TK)
            dx = ln_back(
                acc[at, :],
                xh1[l, b * S : b * S + TQ, :].astype(F32)[:TK],
                inv_s[l, b * S : b * S + TK, 0:1],
                gain,
            )
            hid[at, :] = hid[at, :] + dx
        return carry

    lax.fori_loop(0, L, backward, 0)
    x16[...] = (xh2[L - 1].astype(F32) * norms[L - 1, 2:3, :] + norms[L - 1, 3:4, :]).astype(BF16)
    for i, (part, j) in enumerate(chunks):
        if i == len(chunks) - 1:
            reduce_ranks(0)
        mlp_chunk(L - 1, part, j, "output")
    activations_out()
    for j in range(NJ):
        for b in range(B):
            stage_v[j, pl.ds(b, T, stride=B), :] = hid[
                b * TQ : b * TQ + T, 128 * j : 128 * (j + 1)
            ]
    reduce_end(0)

    grad_v = grad_nat.reshape(HJ, PN * L, 128)
    for l in range(L):
        for k in range(G):
            rows = min(PB, PN - k * PB)
            for j in range(HJ):
                grad_v[j, pl.ds(k * PB * L + l, rows, stride=L), :] = fin[l, k, j].astype(F32)[:rows]
    n = PN * L
    own, theirs = jnp.zeros((8, 128), F32), jnp.zeros((8, 128), F32)
    for l in range(L):
        for k in range(G):
            own += square_of(fin[l, k])
            theirs += sq_in[l, k]
    squares = own + theirs
    grad_norm = jnp.sqrt(squares)
    norm_s[...] = grad_norm[0:1, 0:1]
    factor = jnp.minimum(1.0, clip_limit / (grad_norm[0:1, :] + 1e-06))
    fix_first = 1.0 - beta_one**STEP
    fix_second = 1.0 - beta_two**STEP
    for j in range(HJ):
        copy_moment(0, j).wait()
        copy_moment(1, j).wait()
        first_v = first_nat.reshape(HJ, n, 128)
        second_v = second_nat.reshape(HJ, n, 128)
        prompt_v = prompt_nat.reshape(HJ, n, 128)
        clipped = grad_v[j, 0:n, :] * factor
        new_first = beta_one * first_v[j, 0:n, :] + (1.0 - beta_one) * clipped
        new_second = beta_two * second_v[j, 0:n, :] + (1.0 - beta_two) * clipped * clipped
        first_v[j, 0:n, :] = new_first
        second_v[j, 0:n, :] = new_second
        old = prom_v[core * HJ + j]
        prompt_v[j] = old - learn_rate * (
            new_first / fix_first / (jnp.sqrt(new_second / fix_second) + adam_eps)
            + weight_decay * old
        )


def hand_on_kernel(*refs):
    n = (len(refs) - 1) // 2
    sources, targets, sem = refs[:n], refs[n : 2 * n], refs[2 * n]
    copies = []
    for src, dst in zip(sources, targets):
        if len(src.shape) == 2:
            copies.append(pltpu.make_async_copy(src, dst, sem.at[len(copies)]))
        else:
            for j in range(src.shape[0]):
                view = dst.at[:, :, 128 * j : 128 * (j + 1)]
                copies.append(pltpu.make_async_copy(src.at[j], view, sem.at[len(copies)]))
    for copy in copies:
        copy.start()
    for copy in copies:
        copy.wait()


def hand_on(arrays):
    def whole(a):
        shape = a.shape if len(a.shape) == 2 else a.shape[1:3] + (a.shape[0] * a.shape[3],)
        return jax.ShapeDtypeStruct(shape, a.dtype)

    count = sum(1 if len(a.shape) == 2 else a.shape[0] for a in arrays)
    return pl.pallas_call(
        hand_on_kernel,
        out_shape=tuple(whole(a) for a in arrays),
        in_specs=[pl.BlockSpec(memory_space=VMEM)] * len(arrays),
        out_specs=(pl.BlockSpec(memory_space=pl.ANY),) * len(arrays),
        scratch_shapes=[DMA((count,))],
        compiler_params=pltpu.CompilerParams(vmem_limit_bytes=2**20),
    )(*arrays)


def native(x):
    return x.transpose(1, 0, 2)


def local(
    ndp, tokens, cotangent, prompts, first_moment, second_moment, norm_params, bias_rows,
    qkv_weight, out_weight, up_weight, up_bias, down_weight,
):
    B, T, D = tokens.shape
    L, PN, _ = prompts.shape
    FH = down_weight.shape[1]
    TK = up_to(T, 8)
    S = up_to(TK + up_to(PN, 8), 128)
    TQ = up_to(T, 16)
    G = 4
    R = ndp // G
    NJ, HJ, PB = D // 128, D // 256, 16
    dims = (B, T, D, L, PN, TK, S, TQ, FH, G, R)
    H = HEADS
    n_local = 2 * NJ + 3 * HJ + 3
    scratch = [
        VMEM((NJ, T, B, 128), BF16),
        VMEM((NJ, PN, L, 128), F32),
        VMEM((L, 4, D), F32),
        VMEM((L, 4, D), F32),
        VMEM((L, D, 3 * D), BF16),
        VMEM((L, D, D), BF16),
        VMEM((L, 2, D, FH), BF16),
        VMEM((2, L, FH), F32),
        VMEM((L, 2, FH, D), BF16),
        VMEM((B, S, D), F32),
        VMEM((B * TQ, D), F32),
        VMEM((B * TQ, D), F32),
        VMEM((B * S, 3 * D), BF16),
        VMEM((B * TQ, D), BF16),
        VMEM((L, B * S, D), BF16),
        VMEM((L, B * TQ, D), BF16),
        VMEM((L, B * S, 2), F32),
        VMEM((L, B * TQ, D), BF16),
        VMEM((L, B * S, D), BF16),
        VMEM((L, B * S, D), BF16),
        VMEM((L, B, H, TQ, S), BF16),
        VMEM((L, B * TQ, D), BF16),
        VMEM((L, B * TQ, D), BF16),
        VMEM((L, B * TQ, 2 * FH), BF16),
        VMEM((L, 2 * G, HJ, PB, 128), BF16),
        VMEM((L, 2 * G, HJ, PB, 128), BF16),
        VMEM((L, R, HJ, PB, 128), BF16),
        VMEM((L, G, HJ, PB, 128), BF16),
        VMEM((L, 8, 128), F32),
        VMEM((L, G, 8, 128), F32),
        DMA((n_local,)),
        DMA((L, 4)),
        DMA((2, HJ + 1)),
        DMA((L, 2, 2)),
        DMA((L, 2)),
        DMA((L, 2)),
        DMA((L, 2)),
        DMA((L, 2)),
    ]
    any_spec = pl.BlockSpec(memory_space=pl.ANY)
    small = jax.ShapeDtypeStruct((HJ, PN, L, 128), F32)
    small_v = VMEM((HJ, PN, L, 128), F32)
    results = pl.pallas_call(
        functools.partial(main_kernel, dims),
        out_shape=(
            VMEM((NJ, T, B, 128), BF16),
            VMEM((NJ, T, B, 128), F32),
            small_v,
            VMEM((1, 1), F32),
            small_v,
            small_v,
            small_v,
        ),
        in_specs=[any_spec] * 12,
        scratch_shapes=scratch,
        compiler_params=pltpu.CompilerParams(
            collective_id=0, has_side_effects=True, vmem_limit_bytes=61 * 2**20
        ),
    )(
        native(tokens), native(cotangent), native(prompts), native(first_moment),
        native(second_moment), norm_params, bias_rows, qkv_weight, out_weight,
        up_weight, up_bias, down_weight,
    )
    act, igrad, grad, norm, new_first, new_second, new_prompts = hand_on(results)
    return (
        native(act), native(igrad), native(grad), norm.reshape(()),
        native(new_first), native(new_second), native(new_prompts),
    )


def solution(mesh):
    ndp = mesh.shape["dp"]
    return jax.shard_map(
        functools.partial(local, ndp),
        mesh=mesh,
        in_specs=(
            P(("dp", "mlp"), None, None),
            P(("dp", "mlp"), None, None),
            P(None, None, "mlp"),
            P(None, None, "mlp"),
            P(None, None, "mlp"),
            P(),
            P(),
            P(),
            P(),
            P(None, None, "mlp"),
            P(None, "mlp"),
            P(None, "mlp", None),
        ),
        out_specs=(
            P(("dp", "mlp"), None, None),
            P(("dp", "mlp"), None, None),
            P(None, None, "mlp"),
            P(),
            P(None, None, "mlp"),
            P(None, None, "mlp"),
            P(None, None, "mlp"),
        ),
        check_vma=False,
    )
```

```python
import functools

import jax
import jax.numpy as jnp
from jax import lax
from jax.experimental import pallas as pl
from jax.experimental.pallas import tpu as pltpu
from jax.sharding import PartitionSpec as P

HEADS = 12
STEP = 10
MESH = pl.DeviceIdType.MESH
VMEM = pltpu.VMEM
DMA = pltpu.SemaphoreType.DMA
BF16 = jnp.bfloat16
F32 = jnp.float32

norm_eps = 1e-06
clip_limit = 1.0
beta_one = 0.9
beta_two = 0.999
learn_rate = 1.5
weight_decay = 0.05
adam_eps = 1e-08
LOG2E = 1.4426950408889634


def up_to(value, step):
    return -(-value // step) * step


def mm(left, right):
    return jnp.dot(left, right, preferred_element_type=F32)


def mm_nt(left, right):
    return lax.dot_general(left, right, (((1,), (1,)), ((), ())), preferred_element_type=F32)


def mm_tn(left, right):
    return lax.dot_general(left, right, (((0,), (0,)), ((), ())), preferred_element_type=F32)


def rows_loop(count, step, body, unroll=1):
    def one(i, carry):
        body(pl.multiple_of(i * step, step))
        return carry

    lax.fori_loop(0, count // step, one, 0, unroll=unroll)


def main_kernel(
    dims,
    tok_hbm,
    cot_hbm,
    prompts_hbm,
    first_hbm,
    second_hbm,
    norms_hbm,
    bias_hbm,
    qkv_hbm,
    out_hbm,
    up_hbm,
    ub_hbm,
    dn_hbm,
    tok_nat,
    stage_nat,
    grad_nat,
    norm_s,
    first_nat,
    second_nat,
    prompt_nat,
    cot_nat,
    prom_nat,
    norms,
    bias,
    w_qkv,
    w_out,
    w_up,
    ub,
    w_dn,
    seq,
    hid,
    acc,
    wide,
    x16,
    xh1,
    xh2,
    inv_s,
    q_s,
    k_s,
    v_s,
    e_s,
    ri_s,
    o_s,
    gp_s,
    part_h,
    slot_b,
    slot_c,
    fin,
    sq_out,
    sq_in,
    local_sem,
    weight_sem,
    push_sem,
    push_w_sem,
    sem_b,
    sem_c,
    sem_d,
    sem_e,
):
    B, T, D, L, PN, TK, PP, S, TQ, FH, G, R = dims
    H = HEADS
    HD = D // H
    C = 768
    NJ = D // 128
    HJ = NJ // 2
    PB = 16
    core = lax.axis_index("mlp")
    other = 1 - core
    me = lax.axis_index("dp")
    g, r = lax.rem(me, G), me // G
    half = D // 2

    def member(k):
        return lax.rem(g + k, G)

    def rank(k):
        return lax.rem(r + k, R)

    around = [(k, c) for k in range(G) for c in range(2)][1:]

    def neighbour(k, c):
        return {"dp": r * G + member(k), "mlp": lax.rem(core + c, 2)}

    barrier = pltpu.get_barrier_semaphore()
    for k, c in around:
        pl.semaphore_signal(barrier, inc=1, device_id=neighbour(k, c), device_id_type=MESH)

    def greet(k, carry):
        pl.semaphore_signal(
            barrier, inc=1, device_id={"dp": rank(k) * G + g}, device_id_type=MESH
        )
        return carry

    lax.fori_loop(1, R, greet, 0)

    def columns(j):
        return slice(128 * j, 128 * (j + 1))

    def local(i, src, dst):
        return pltpu.make_async_copy(src, dst, local_sem.at[i])

    def copy_tok(j):
        return local(j, tok_hbm.at[:, :, columns(j)], tok_nat.at[j, 0:T])

    def copy_cot(j):
        return local(NJ + j, cot_hbm.at[:, :, columns(j)], cot_nat.at[j, 0:T])

    def copy_prom(j):
        return local(
            2 * NJ + j, prompts_hbm.at[:, :, columns(j)], prom_nat.at[core * HJ + j, 0:PN]
        )

    def copy_moment(i, j):
        src = (first_hbm, second_hbm)[i]
        return local(
            2 * NJ + (i + 1) * HJ + j, src.at[:, :, columns(j)], (first_nat, second_nat)[i].at[j, 0:PN]
        )

    def copy_small(i):
        src, dst = ((norms_hbm, norms), (bias_hbm, bias), (ub_hbm, ub.at[0]))[i]
        return local(2 * NJ + 3 * HJ + i, src, dst)

    def copy_weight(l, i):
        src, dst = (
            (qkv_hbm.at[l], w_qkv.at[l]),
            (out_hbm.at[l], w_out.at[l]),
            (up_hbm.at[l], w_up.at[l, 0]),
            (dn_hbm.at[l], w_dn.at[l, 0]),
        )[i]
        return pltpu.make_async_copy(src, dst, weight_sem.at[l, i])

    def push(src, dst, send_at, recv_at):
        return pltpu.make_async_remote_copy(
            src_ref=src,
            dst_ref=dst,
            send_sem=send_at,
            recv_sem=recv_at,
            device_id={"mlp": other},
            device_id_type=MESH,
        )

    def push_prom(j):
        return push(
            prompts_hbm.at[:, :, columns(j)],
            prom_nat.at[core * HJ + j, 0:PN],
            push_sem.at[0, j],
            push_sem.at[1, j],
        )

    def push_ub():
        return push(ub_hbm, ub.at[1], push_sem.at[0, HJ], push_sem.at[1, HJ])

    def push_weight(l, i):
        src, dst = ((up_hbm.at[l], w_up.at[l, 1]), (dn_hbm.at[l], w_dn.at[l, 1]))[i]
        return push(src, dst, push_w_sem.at[l, 0, i], push_w_sem.at[l, 1, i])

    for j in range(NJ):
        copy_tok(j).start()
    for j in range(HJ):
        copy_prom(j).start()
    copy_small(0).start()
    copy_small(1).start()
    copy_weight(0, 0).start()
    pl.semaphore_wait(barrier, len(around) + R - 1)
    for j in range(HJ):
        push_prom(j).start()
    push_ub().start()
    push_weight(0, 0).start()
    push_weight(0, 1).start()

    tok_v = tok_nat.reshape(NJ, TK * B, 128)
    cot_v = cot_nat.reshape(NJ, TK * B, 128)
    stage_v = stage_nat.reshape(NJ, TK * B, 128)
    prom_v = prom_nat.reshape(NJ, PP * L, 128)

    lane = lax.broadcasted_iota(jnp.int32, (1, S), 1)
    valid = (lane < T) | ((lane >= TK) & (lane < TK + PN))
    key_bias = jnp.where(valid, 0.0, -1e30).astype(F32)
    even_q = lax.broadcasted_iota(jnp.int32, (TQ, 2 * HD), 1) < HD
    even_k = lax.broadcasted_iota(jnp.int32, (S, 2 * HD), 1) < HD
    SH = S // 2
    even_h = lax.broadcasted_iota(jnp.int32, (SH, 2 * HD), 1) < HD
    low_lane = lax.broadcasted_iota(jnp.int32, (TQ, S), 1) < SH
    scale = HD**-0.5

    def spread(src_v, store):
        for j in range(NJ):
            stage_v[j, 0 : T * B] = src_v[j, 0 : T * B].astype(F32)
        for b in range(B):
            for j in range(NJ):
                store(b, slice(128 * j, 128 * (j + 1)), stage_v[j, pl.ds(b, T, stride=B), :])

    for b in range(B):
        seq[b, TK - 8 :, :] = jnp.zeros((S - TK + 8, D), F32)
    for j in range(NJ):
        copy_tok(j).wait()

    def store_tok(b, cols, rows):
        seq[b, 0:T, cols] = rows

    spread(tok_v, store_tok)
    copy_small(0).wait()
    copy_small(1).wait()
    for j in range(HJ):
        copy_prom(j).wait()
        push_prom(j).wait()

    def norm_rows(x):
        mean = jnp.mean(x, axis=-1, keepdims=True)
        centre = x - mean
        spread_ = jnp.mean(centre * centre, axis=-1, keepdims=True)
        inv = lax.rsqrt(spread_ + norm_eps)
        return centre * inv, inv

    def ln_back(dy, xh, inv, gain):
        gdy = dy * gain
        a = jnp.mean(gdy, axis=-1, keepdims=True)
        c = jnp.mean(gdy * xh, axis=-1, keepdims=True)
        return inv * (gdy - a - xh * c)

    def attend_forward(l):
        def pair(i, carry):
            b = i // (H // 2)
            hp = i % (H // 2)
            sl = pl.ds(pl.multiple_of(hp * 2 * HD, 2 * HD), 2 * HD)
            qr = pl.ds(pl.multiple_of(b * TQ, 16), TQ)
            kr = pl.ds(pl.multiple_of(b * S, 16), S)
            q = q_s[l, qr, sl]
            k = k_s[l, kr, sl]
            v = v_s[l, kr, sl]
            sums = []
            for h in range(2):
                here = even_k if h == 0 else jnp.logical_not(even_k)
                s = mm_nt(q, jnp.where(here, k, jnp.zeros_like(k))) + key_bias
                top = jnp.max(s, axis=1, keepdims=True)
                e = jnp.exp2((s - top) * (LOG2E * scale)).astype(BF16)
                e_s[l, b, hp * 2 + h] = e
                sums.append(mm(e, jnp.where(here, v, jnp.ones_like(v))))
            top_part = jnp.where(even_q, sums[0], sums[1])
            total = jnp.where(even_q, sums[1], sums[0])
            inv = pltpu.roll(1.0 / total, HD, 1)
            ri_s[l, qr, sl] = inv.astype(BF16)
            o_s[l, qr, sl] = (top_part * inv).astype(BF16)
            return carry

        lax.fori_loop(0, B * H // 2, pair, 0, unroll=6)

    def back_half(l, b, hp, part, first):
        at = pl.multiple_of(hp * 2 * HD, 2 * HD)
        sl = pl.ds(at, 2 * HD)
        qr = pl.ds(pl.multiple_of(b * TQ, 16), TQ)
        kr = pl.ds(pl.multiple_of(b * S + part * SH, 16), SH)
        v = v_s[l, kr, sl]
        spare = pl.ds(pl.multiple_of((b * (H // 2) + hp) * S, 128), TQ)
        if first:
            do = x16[qr, sl].astype(F32) * ri_s[l, qr, sl].astype(F32)
            prod = do * o_s[l, qr, sl].astype(F32)
            d0 = jnp.sum(jnp.where(even_q, prod, 0.0), axis=1, keepdims=True)
            d1 = jnp.sum(jnp.where(even_q, 0.0, prod), axis=1, keepdims=True)
            do16 = do.astype(BF16)
            q_t = q_s[l, qr, sl].T
            do_t = do16.T
            x16[qr, sl] = do16
            gp_s[l, 0 : 2 * HD, spare] = q_t
            gp_s[l, 2 * HD : 4 * HD, spare] = do_t
            acc[qr, sl] = jnp.where(even_q, d0, d1)
        else:
            do16 = x16[qr, sl]
            q_t = gp_s[l, 0 : 2 * HD, spare]
            do_t = gp_s[l, 2 * HD : 4 * HD, spare]
            both = acc[qr, sl]
            d0, d1 = both[:, 0:1], both[:, HD : HD + 1]
        zero = jnp.zeros_like(v)
        stacked = jnp.concatenate([jnp.where(even_h, v, zero), jnp.where(even_h, zero, v)], axis=0)
        dp = mm_nt(do16, stacked)
        keys = slice(part * SH, (part + 1) * SH)
        e = jnp.concatenate([e_s[l, b, hp * 2, :, keys], e_s[l, b, hp * 2 + 1, :, keys]], axis=1)
        ds = (e.astype(F32) * (dp - jnp.where(low_lane, d0, d1))).astype(BF16)
        dk = mm(q_t, ds)
        dv = mm(do_t, e)
        dk = jnp.concatenate([dk[:HD, :SH], dk[HD:, SH:]], axis=0) * scale
        dv = jnp.concatenate([dv[:HD, :SH], dv[HD:, SH:]], axis=0)
        wide[kr, pl.ds(pl.multiple_of(D + at, 128), 2 * HD)] = dk.astype(BF16).T
        wide[kr, pl.ds(pl.multiple_of(2 * D + at, 128), 2 * HD)] = dv.astype(BF16).T
        return ds

    def back_queries(l, b, hp, low, high):
        at = pl.multiple_of(hp * 2 * HD, 2 * HD)
        sl = pl.ds(at, 2 * HD)
        kr = pl.ds(pl.multiple_of(b * S, 16), S)
        k = k_s[l, kr, sl]
        zero = jnp.zeros_like(k)
        dq = mm(jnp.concatenate([low[:, :SH], high[0]], axis=1), jnp.where(even_k, k, zero))
        dq += mm(jnp.concatenate([low[:, SH:], high[1]], axis=1), jnp.where(even_k, zero, k))
        wide[pl.ds(pl.multiple_of(b * S, 16), TQ), sl] = (dq * scale).astype(BF16)

    def pairs_loop(body, lo, hi):
        def one(i, carry):
            body(i // (H // 2), i % (H // 2))
            return carry

        lax.fori_loop(lo, hi, one, 0, unroll=True)

    pairs = B * H // 2

    def send(src, dst, sems, l, device):
        return pltpu.make_async_remote_copy(
            src_ref=src,
            dst_ref=dst,
            send_sem=sems.at[l, 0],
            recv_sem=sems.at[l, 1],
            device_id=device,
            device_id_type=MESH,
        )

    def all_of(slots, l, count, sems):
        view = slots.at[l, 0:count]
        return send(view, view, sems, l, {"mlp": other})

    mine_b = core * G + g

    def reduce_start(l, grad):
        rows = jnp.concatenate([grad, jnp.zeros((G * PB - grad.shape[0], D), F32)], axis=0)
        for j in range(NJ):
            for k in range(G):
                block = rows[k * PB : (k + 1) * PB, 128 * j : 128 * (j + 1)]
                part_h[l, j // HJ * G + k, j % HJ] = block.astype(BF16)
        for k, c in around:
            to = lax.rem(core + c, 2) * G + member(k)
            send(
                part_h.at[l, to], slot_b.at[l, mine_b], sem_b, l, neighbour(k, c)
            ).start()
        slot_b[l, mine_b] = part_h[l, mine_b]

    def reduce_group(l):
        all_of(slot_b, l, 2 * G - 1, sem_b).wait_recv()
        total = slot_b[l, 0].astype(F32)
        for i in range(1, 2 * G):
            total = total + slot_b[l, i].astype(F32)
        slot_c[l, r] = total.astype(BF16)

        def go(k, carry):
            peer = {"dp": rank(k) * G + g}
            send(slot_c.at[l, r], slot_c.at[l, r], sem_c, l, peer).start()
            return carry

        lax.fori_loop(1, R, go, 0, unroll=R <= 4)
        all_of(part_h, l, 2 * G - 1, sem_b).wait_send()

    def square_of(block):
        block = block.astype(F32)
        total = jnp.sum(jnp.sum(block * block, axis=0), axis=(0, 1), keepdims=True)
        return jnp.broadcast_to(total, (8, 128))

    def reduce_ranks(l):
        if R > 1:
            all_of(slot_c, l, R - 1, sem_c).wait_recv()

        def add(k, total):
            return total + slot_c[l, k].astype(F32)

        total = lax.fori_loop(0, R, add, jnp.zeros((HJ, PB, 128), F32), unroll=R <= 4)
        fin[l, g] = total.astype(BF16)
        for k in range(1, G):
            peer = {"dp": r * G + member(k)}
            send(fin.at[l, g], fin.at[l, g], sem_d, l, peer).start()
        sq_out[l] = square_of(fin[l, g])
        for k in range(G):
            send(sq_out.at[l], sq_in.at[l, g], sem_e, l, neighbour(k, 1)).start()
        if R > 1:
            all_of(slot_c, l, R - 1, sem_c).wait_send()

    def reduce_end(l):
        all_of(fin, l, G - 1, sem_d).wait()
        all_of(sq_in, l, G, sem_e).wait()

    def mlp_chunk(l, part, j, last_):
        cols = slice(j * C, (j + 1) * C)
        at = slice((part * (FH // C) + j) * C, (part * (FH // C) + j + 1) * C)
        pre = mm(x16[...], w_up[l, part, :, cols]) + ub[part, pl.ds(l, 1), cols]
        cdf = 0.5 + 0.5 * lax.erf(pre * 0.7071067811865476)
        if last_ != "output":
            bell = jnp.exp2(pre * pre * (-0.5 * LOG2E)) * 0.3989422804014327
            gp_s[l, :, at] = (cdf + pre * bell).astype(BF16)
        if last_ != "slope":
            add = mm((pre * cdf).astype(BF16), w_dn[l, part, cols, :])
            if part == 0 and j == 0:
                acc[...] = add
            else:
                acc[...] += add

    chunks = [(part, j) for part in range(2) for j in range(FH // C)]

    def norm_one(l):
        for b in range(B):
            for j in range(NJ):
                seq[b, TK : TK + PN, columns(j)] = prom_v[j, pl.ds(l, PN, stride=L), :]
        gain, shift = norms[l, 0:1, :], norms[l, 1:2, :]
        for b in range(B):
            xh, inv = norm_rows(seq[b])
            at = slice(b * S, (b + 1) * S)
            xh1[l, at, :] = xh.astype(BF16)
            inv_s[l, at, 0:1] = inv
            wide[at, 0:D] = (xh * gain + shift).astype(BF16)

    def attend(l):
        lhs = jnp.concatenate([wide[b * S : b * S + TQ, 0:D] for b in range(B)], axis=0)
        q_s[l] = (mm(lhs, w_qkv[l, :, 0:D]) + bias[l, 0:1, :]).astype(BF16)
        k_s[l] = mm(wide[:, 0:D], w_qkv[l, :, D : 2 * D]).astype(BF16)
        v_s[l] = (mm(wide[:, 0:D], w_qkv[l, :, 2 * D : 3 * D]) + bias[l, 1:2, :]).astype(BF16)
        attend_forward(l)

    def norm_two(l):
        branch = mm(o_s[l], w_out[l]) + bias[l, 2:3, :]
        for b in range(B):
            hid[b * TQ : (b + 1) * TQ, :] = seq[b, 0:TQ, :] + branch[b * TQ : (b + 1) * TQ]
        gain2, shift2 = norms[l, 2:3, :], norms[l, 3:4, :]
        xh, inv = norm_rows(hid[...])
        xh2[l] = xh.astype(BF16)
        inv_s[l, 0 : B * TQ, 1:2] = inv
        x16[...] = (xh * gain2 + shift2).astype(BF16)

    norm_one(0)
    copy_weight(0, 0).wait()
    copy_small(2).start()
    for i in range(1, 4):
        copy_weight(0, i).start()

    def forward(l, carry):
        attend(l)
        for i in range(1, 4):
            copy_weight(l, i).wait()

        @pl.when(l == 0)
        def _():
            for later in range(1, L):
                for i in range(2):
                    push_weight(later, i).start()
                for i in range(4):
                    copy_weight(later, i).start()
            for j in range(NJ):
                copy_cot(j).start()
            for j in range(HJ):
                copy_moment(0, j).start()
                copy_moment(1, j).start()
            copy_small(2).wait()
            push_ub().wait()

        @pl.when(l < L - 1)
        def _():
            norm_two(l)
            for part, j in chunks:
                if part == 1 and j == 0:
                    push_weight(l, 0).wait()
                    push_weight(l, 1).wait()
                mlp_chunk(l, part, j, "both")
            for b in range(B):
                at = slice(b * TQ, (b + 1) * TQ)
                seq[b, 0:TQ, :] = hid[at, :] + acc[at, :] + bias[l, 3:4, :]
            norm_one(l + 1)
            copy_weight(l + 1, 0).wait()

        return carry

    lax.fori_loop(0, L, forward, 0)
    push_weight(L - 1, 0).wait()
    push_weight(L - 1, 1).wait()
    for j in range(NJ):
        copy_cot(j).wait()
    norm_two(L - 1)
    for part, j in chunks:
        mlp_chunk(L - 1, part, j, "slope")
    for b in range(B):
        seq[b, 0:TQ, :] = hid[b * TQ : (b + 1) * TQ, :] + bias[L - 1, 3:4, :]

    def activations_out():
        for b in range(B):
            seq[b, 0:TQ, :] += acc[b * TQ : (b + 1) * TQ, :]
            for j in range(NJ):
                stage_v[j, pl.ds(b, T, stride=B), :] = seq[b, 0:T, 128 * j : 128 * (j + 1)]
        for j in range(NJ):
            tok_v[j, 0 : T * B] = stage_v[j, 0 : T * B].astype(BF16)

    for b in range(B):
        hid[b * TQ + TK - 8 : (b + 1) * TQ, :] = jnp.zeros((TQ - TK + 8, D), F32)

    def store_cot(b, cols, rows):
        hid[b * TQ : b * TQ + T, cols] = rows

    spread(cot_v, store_cot)

    def backward(step, carry):
        l = L - 1 - step
        above = l + 1

        def sum_above(phase):
            pl.when(step > 0)(lambda: phase(above))

        x16[...] = hid[...].astype(BF16)
        sum_above(reduce_group)
        for part in range(2):
            for j in range(FH // C):
                cols = slice(j * C, (j + 1) * C)
                at = slice((part * (FH // C) + j) * C, (part * (FH // C) + j + 1) * C)
                ga = mm_nt(x16[...], w_dn[l, part, cols, :])
                gpre = (gp_s[l, :, at].astype(F32) * ga).astype(BF16)
                add = mm_nt(gpre, w_up[l, part, :, cols])
                if part == 0 and j == 0:
                    acc[...] = add
                else:
                    acc[...] += add
        gain2 = norms[l, 2:3, :]

        new = hid[...] + ln_back(
            acc[...], xh2[l].astype(F32), inv_s[l, 0 : B * TQ, 1:2], gain2
        )
        hid[...] = new
        x16[...] = new.astype(BF16)
        x16[...] = mm_nt(x16[...], w_out[l]).astype(BF16)
        gain = norms[l, 0:1, :]

        def high_keys(b, hp):
            ds = back_half(l, b, hp, 1, True)
            e_s[l, b, hp * 2, :, SH:] = ds[:, :SH]
            e_s[l, b, hp * 2 + 1, :, SH:] = ds[:, SH:]

        def low_keys(b, hp):
            ds = back_half(l, b, hp, 0, False)
            back_queries(
                l, b, hp, ds, (e_s[l, b, hp * 2, :, SH:], e_s[l, b, hp * 2 + 1, :, SH:])
            )

        def prompt_gradient():
            base = TK // 16 * 16
            lhs = jnp.concatenate(
                [wide[b * S + base : (b + 1) * S, D : 3 * D] for b in range(B)], axis=0
            )
            full = mm_nt(lhs, w_qkv[l, :, D : 3 * D])
            n = S - base
            dprom = full[TK - base : n]
            for b in range(1, B):
                dprom = dprom + full[b * n + TK - base : (b + 1) * n]
            xh_p = xh1[l, base:S, :].astype(F32)[TK - base :]
            return ln_back(dprom, xh_p, inv_s[l, TK:S, 0:1], gain)

        pairs_loop(high_keys, 0, pairs)
        reduce_start(l, prompt_gradient())
        sum_above(reduce_ranks)
        pairs_loop(low_keys, 0, pairs)
        lhs = jnp.concatenate([wide[b * S : b * S + TQ, :] for b in range(B)], axis=0)
        acc[...] = mm_nt(lhs, w_qkv[l])
        pl.when(l == 0)(lambda: reduce_group(l))
        sum_above(reduce_end)
        for b in range(B):
            at = slice(b * TQ, b * TQ + TK)
            dx = ln_back(
                acc[at, :],
                xh1[l, b * S : b * S + TQ, :].astype(F32)[:TK],
                inv_s[l, b * S : b * S + TK, 0:1],
                gain,
            )
            hid[at, :] = hid[at, :] + dx
        return carry

    lax.fori_loop(0, L, backward, 0)
    x16[...] = (xh2[L - 1].astype(F32) * norms[L - 1, 2:3, :] + norms[L - 1, 3:4, :]).astype(BF16)
    for i, (part, j) in enumerate(chunks):
        if i == len(chunks) - 1:
            reduce_ranks(0)
        mlp_chunk(L - 1, part, j, "output")
    activations_out()
    for j in range(NJ):
        for b in range(B):
            stage_v[j, pl.ds(b, T, stride=B), :] = hid[
                b * TQ : b * TQ + T, 128 * j : 128 * (j + 1)
            ]
    reduce_end(0)

    grad_v = grad_nat.reshape(HJ, PP * L, 128)
    for l in range(L):
        for k in range(G):
            rows = min(PB, PN - k * PB)
            for j in range(HJ):
                grad_v[j, pl.ds(k * PB * L + l, rows, stride=L), :] = fin[l, k, j].astype(F32)[:rows]
    n = PN * L
    own, theirs = jnp.zeros((8, 128), F32), jnp.zeros((8, 128), F32)
    for l in range(L):
        for k in range(G):
            own += square_of(fin[l, k])
            theirs += sq_in[l, k]
    squares = own + theirs
    grad_norm = jnp.sqrt(squares)
    norm_s[...] = grad_norm[0:1, 0:1]
    factor = jnp.minimum(1.0, clip_limit / (grad_norm[0:1, :] + 1e-06))
    fix_first = 1.0 - beta_one**STEP
    fix_second = 1.0 - beta_two**STEP
    for j in range(HJ):
        copy_moment(0, j).wait()
        copy_moment(1, j).wait()
        first_v = first_nat.reshape(HJ, PP * L, 128)
        second_v = second_nat.reshape(HJ, PP * L, 128)
        prompt_v = prompt_nat.reshape(HJ, PP * L, 128)
        clipped = grad_v[j, 0:n, :] * factor
        new_first = beta_one * first_v[j, 0:n, :] + (1.0 - beta_one) * clipped
        new_second = beta_two * second_v[j, 0:n, :] + (1.0 - beta_two) * clipped * clipped
        first_v[j, 0:n, :] = new_first
        second_v[j, 0:n, :] = new_second
        old = prom_v[core * HJ + j, 0:n, :]
        prompt_v[j, 0:n, :] = old - learn_rate * (
            new_first / fix_first / (jnp.sqrt(new_second / fix_second) + adam_eps)
            + weight_decay * old
        )


def hand_on_kernel(*refs):
    n = (len(refs) - 1) // 2
    sources, targets, sem = refs[:n], refs[n : 2 * n], refs[2 * n]
    copies = []
    for src, dst in zip(sources, targets):
        if len(src.shape) == 2:
            copies.append(pltpu.make_async_copy(src, dst, sem.at[len(copies)]))
        else:
            rows = dst.shape[0]
            for j in range(src.shape[0]):
                view = dst.at[:, :, 128 * j : 128 * (j + 1)]
                copies.append(
                    pltpu.make_async_copy(src.at[j, 0:rows], view, sem.at[len(copies)])
                )
    for copy in copies:
        copy.start()
    for copy in copies:
        copy.wait()


def hand_on(arrays, counts):
    def whole(a, rows):
        shape = a.shape if len(a.shape) == 2 else (rows, a.shape[2], a.shape[0] * a.shape[3])
        return jax.ShapeDtypeStruct(shape, a.dtype)

    copies = sum(1 if len(a.shape) == 2 else a.shape[0] for a in arrays)
    return pl.pallas_call(
        hand_on_kernel,
        out_shape=tuple(whole(a, rows) for a, rows in zip(arrays, counts)),
        in_specs=[pl.BlockSpec(memory_space=VMEM)] * len(arrays),
        out_specs=(pl.BlockSpec(memory_space=pl.ANY),) * len(arrays),
        scratch_shapes=[DMA((copies,))],
        compiler_params=pltpu.CompilerParams(vmem_limit_bytes=2**20),
    )(*arrays)


def native(x):
    return x.transpose(1, 0, 2)


def local(
    ndp, tokens, cotangent, prompts, first_moment, second_moment, norm_params, bias_rows,
    qkv_weight, out_weight, up_weight, up_bias, down_weight,
):
    B, T, D = tokens.shape
    L, PN, _ = prompts.shape
    FH = down_weight.shape[1]
    TK = up_to(T, 8)
    PP = up_to(PN, 8)
    S = up_to(TK + PP, 128)
    TQ = up_to(T, 16)
    G = 4
    R = ndp // G
    NJ, HJ, PB = D // 128, D // 256, 16
    dims = (B, T, D, L, PN, TK, PP, S, TQ, FH, G, R)
    H = HEADS
    n_local = 2 * NJ + 3 * HJ + 3
    scratch = [
        VMEM((NJ, TK, B, 128), BF16),
        VMEM((NJ, PP, L, 128), F32),
        VMEM((L, 4, D), F32),
        VMEM((L, 4, D), F32),
        VMEM((L, D, 3 * D), BF16),
        VMEM((L, D, D), BF16),
        VMEM((L, 2, D, FH), BF16),
        VMEM((2, L, FH), F32),
        VMEM((L, 2, FH, D), BF16),
        VMEM((B, S, D), F32),
        VMEM((B * TQ, D), F32),
        VMEM((B * TQ, D), F32),
        VMEM((B * S, 3 * D), BF16),
        VMEM((B * TQ, D), BF16),
        VMEM((L, B * S, D), BF16),
        VMEM((L, B * TQ, D), BF16),
        VMEM((L, B * S, 2), F32),
        VMEM((L, B * TQ, D), BF16),
        VMEM((L, B * S, D), BF16),
        VMEM((L, B * S, D), BF16),
        VMEM((L, B, H, TQ, S), BF16),
        VMEM((L, B * TQ, D), BF16),
        VMEM((L, B * TQ, D), BF16),
        VMEM((L, B * TQ, 2 * FH), BF16),
        VMEM((L, 2 * G, HJ, PB, 128), BF16),
        VMEM((L, 2 * G, HJ, PB, 128), BF16),
        VMEM((L, R, HJ, PB, 128), BF16),
        VMEM((L, G, HJ, PB, 128), BF16),
        VMEM((L, 8, 128), F32),
        VMEM((L, G, 8, 128), F32),
        DMA((n_local,)),
        DMA((L, 4)),
        DMA((2, HJ + 1)),
        DMA((L, 2, 2)),
        DMA((L, 2)),
        DMA((L, 2)),
        DMA((L, 2)),
        DMA((L, 2)),
    ]
    any_spec = pl.BlockSpec(memory_space=pl.ANY)
    small = VMEM((HJ, PP, L, 128), F32)
    results = pl.pallas_call(
        functools.partial(main_kernel, dims),
        out_shape=(
            VMEM((NJ, TK, B, 128), BF16),
            VMEM((NJ, TK, B, 128), F32),
            small,
            VMEM((1, 1), F32),
            small,
            small,
            small,
        ),
        in_specs=[any_spec] * 12,
        scratch_shapes=scratch,
        compiler_params=pltpu.CompilerParams(
            collective_id=0, has_side_effects=True, vmem_limit_bytes=61 * 2**20
        ),
    )(
        native(tokens), native(cotangent), native(prompts), native(first_moment),
        native(second_moment), norm_params, bias_rows, qkv_weight, out_weight,
        up_weight, up_bias, down_weight,
    )
    act, igrad, grad, norm, new_first, new_second, new_prompts = hand_on(
        results, (T, T, PN, 1, PN, PN, PN)
    )
    return (
        native(act), native(igrad), native(grad), norm.reshape(()),
        native(new_first), native(new_second), native(new_prompts),
    )


def solution(mesh):
    ndp = mesh.shape["dp"]
    return jax.shard_map(
        functools.partial(local, ndp),
        mesh=mesh,
        in_specs=(
            P(("dp", "mlp"), None, None),
            P(("dp", "mlp"), None, None),
            P(None, None, "mlp"),
            P(None, None, "mlp"),
            P(None, None, "mlp"),
            P(),
            P(),
            P(),
            P(),
            P(None, None, "mlp"),
            P(None, "mlp"),
            P(None, "mlp", None),
        ),
        out_specs=(
            P(("dp", "mlp"), None, None),
            P(("dp", "mlp"), None, None),
            P(None, None, "mlp"),
            P(),
            P(None, None, "mlp"),
            P(None, None, "mlp"),
            P(None, None, "mlp"),
        ),
        check_vma=False,
    )
```

```python
import functools

import jax
import jax.numpy as jnp
from jax import lax
from jax.experimental import pallas as pl
from jax.experimental.pallas import tpu as pltpu
from jax.sharding import PartitionSpec as P

HEADS = 12
STEP = 10
MESH = pl.DeviceIdType.MESH
VMEM = pltpu.VMEM
DMA = pltpu.SemaphoreType.DMA
BF16 = jnp.bfloat16
F32 = jnp.float32

norm_eps = 1e-06
clip_limit = 1.0
beta_one = 0.9
beta_two = 0.999
learn_rate = 1.5
weight_decay = 0.05
adam_eps = 1e-08
LOG2E = 1.4426950408889634


def up_to(value, step):
    return -(-value // step) * step


def mm(left, right):
    return jnp.dot(left, right, preferred_element_type=F32)


def mm_nt(left, right):
    return lax.dot_general(left, right, (((1,), (1,)), ((), ())), preferred_element_type=F32)


def mm_tn(left, right):
    return lax.dot_general(left, right, (((0,), (0,)), ((), ())), preferred_element_type=F32)


def rows_loop(count, step, body, unroll=1):
    def one(i, carry):
        body(pl.multiple_of(i * step, step))
        return carry

    lax.fori_loop(0, count // step, one, 0, unroll=unroll)


def main_kernel(
    dims,
    tok_hbm,
    cot_hbm,
    prompts_hbm,
    first_hbm,
    second_hbm,
    norms_hbm,
    bias_hbm,
    qkv_hbm,
    out_hbm,
    up_hbm,
    ub_hbm,
    dn_hbm,
    tok_nat,
    stage_nat,
    grad_nat,
    norm_s,
    first_nat,
    second_nat,
    prompt_nat,
    cot_nat,
    prom_nat,
    norms,
    bias,
    w_qkv,
    w_out,
    w_up,
    ub,
    w_dn,
    seq,
    hid,
    acc,
    wide,
    x16,
    xh1,
    xh2,
    inv_s,
    q_s,
    k_s,
    v_s,
    e_s,
    ri_s,
    o_s,
    gp_s,
    part_h,
    slot_b,
    slot_c,
    fin,
    sq_out,
    sq_in,
    local_sem,
    weight_sem,
    push_sem,
    push_w_sem,
    sem_b,
    sem_c,
    sem_d,
    sem_e,
):
    B, T, D, L, PN, TK, PP, S, TQ, FH, G, R = dims
    H = HEADS
    HD = D // H
    C = 768
    NJ = D // 128
    HJ = NJ // 2
    PB = 16
    core = lax.axis_index("mlp")
    other = 1 - core
    me = lax.axis_index("dp")
    g, r = lax.rem(me, G), me // G
    half = D // 2

    def member(k):
        return lax.rem(g + k, G)

    def rank(k):
        return lax.rem(r + k, R)

    around = [(k, c) for k in range(G) for c in range(2)][1:]

    def neighbour(k, c):
        return {"dp": r * G + member(k), "mlp": lax.rem(core + c, 2)}

    def columns(j):
        return slice(128 * j, 128 * (j + 1))

    def local(i, src, dst):
        return pltpu.make_async_copy(src, dst, local_sem.at[i])

    def copy_tok(j):
        return local(j, tok_hbm.at[:, :, columns(j)], tok_nat.at[j, 0:T])

    def copy_cot(j):
        return local(NJ + j, cot_hbm.at[:, :, columns(j)], cot_nat.at[j, 0:T])

    def copy_prom(j):
        return local(
            2 * NJ + j, prompts_hbm.at[:, :, columns(j)], prom_nat.at[core * HJ + j, 0:PN]
        )

    def copy_moment(i, j):
        src = (first_hbm, second_hbm)[i]
        return local(
            2 * NJ + (i + 1) * HJ + j, src.at[:, :, columns(j)], (first_nat, second_nat)[i].at[j, 0:PN]
        )

    def copy_small(i):
        src, dst = ((norms_hbm, norms), (bias_hbm, bias), (ub_hbm, ub.at[0]))[i]
        return local(2 * NJ + 3 * HJ + i, src, dst)

    def copy_weight(l, i):
        src, dst = (
            (qkv_hbm.at[l], w_qkv.at[l]),
            (out_hbm.at[l], w_out.at[l]),
            (up_hbm.at[l], w_up.at[l, 0]),
            (dn_hbm.at[l], w_dn.at[l, 0]),
        )[i]
        return pltpu.make_async_copy(src, dst, weight_sem.at[l, i])

    def push(src, dst, send_at, recv_at):
        return pltpu.make_async_remote_copy(
            src_ref=src,
            dst_ref=dst,
            send_sem=send_at,
            recv_sem=recv_at,
            device_id={"mlp": other},
            device_id_type=MESH,
        )

    def push_prom(j):
        return push(
            prompts_hbm.at[:, :, columns(j)],
            prom_nat.at[core * HJ + j, 0:PN],
            push_sem.at[0, j],
            push_sem.at[1, j],
        )

    def push_ub():
        return push(ub_hbm, ub.at[1], push_sem.at[0, HJ], push_sem.at[1, HJ])

    def push_weight(l, i):
        src, dst = ((up_hbm.at[l], w_up.at[l, 1]), (dn_hbm.at[l], w_dn.at[l, 1]))[i]
        return push(src, dst, push_w_sem.at[l, 0, i], push_w_sem.at[l, 1, i])

    copy_weight(0, 0).start()
    barrier = pltpu.get_barrier_semaphore()
    for k, c in around:
        pl.semaphore_signal(barrier, inc=1, device_id=neighbour(k, c), device_id_type=MESH)

    def greet(k, carry):
        pl.semaphore_signal(
            barrier, inc=1, device_id={"dp": rank(k) * G + g}, device_id_type=MESH
        )
        return carry

    lax.fori_loop(1, R, greet, 0)
    for j in range(NJ):
        copy_tok(j).start()
    for j in range(HJ):
        copy_prom(j).start()
    copy_small(0).start()
    copy_small(1).start()
    pl.semaphore_wait(barrier, len(around) + R - 1)
    for j in range(HJ):
        push_prom(j).start()
    push_ub().start()
    push_weight(0, 0).start()
    push_weight(0, 1).start()

    tok_v = tok_nat.reshape(NJ, TK * B, 128)
    cot_v = cot_nat.reshape(NJ, TK * B, 128)
    stage_v = stage_nat.reshape(NJ, TK * B, 128)
    prom_v = prom_nat.reshape(NJ, PP * L, 128)

    lane = lax.broadcasted_iota(jnp.int32, (1, S), 1)
    valid = (lane < T) | ((lane >= TK) & (lane < TK + PN))
    key_bias = jnp.where(valid, 0.0, -1e30).astype(F32)
    even_q = lax.broadcasted_iota(jnp.int32, (TQ, 2 * HD), 1) < HD
    even_k = lax.broadcasted_iota(jnp.int32, (S, 2 * HD), 1) < HD
    SH = S // 2
    even_h = lax.broadcasted_iota(jnp.int32, (SH, 2 * HD), 1) < HD
    low_lane = lax.broadcasted_iota(jnp.int32, (TQ, S), 1) < SH
    scale = HD**-0.5

    def spread(src_v, store):
        for j in range(NJ):
            stage_v[j, 0 : T * B] = src_v[j, 0 : T * B].astype(F32)
        for b in range(B):
            for j in range(NJ):
                store(b, slice(128 * j, 128 * (j + 1)), stage_v[j, pl.ds(b, T, stride=B), :])

    for b in range(B):
        seq[b, TK - 8 :, :] = jnp.zeros((S - TK + 8, D), F32)
    for j in range(NJ):
        copy_tok(j).wait()

    def store_tok(b, cols, rows):
        seq[b, 0:T, cols] = rows

    spread(tok_v, store_tok)
    copy_small(0).wait()
    copy_small(1).wait()
    for j in range(HJ):
        copy_prom(j).wait()
        push_prom(j).wait()

    def norm_rows(x):
        mean = jnp.mean(x, axis=-1, keepdims=True)
        centre = x - mean
        spread_ = jnp.mean(centre * centre, axis=-1, keepdims=True)
        inv = lax.rsqrt(spread_ + norm_eps)
        return centre * inv, inv

    def ln_back(dy, xh, inv, gain):
        gdy = dy * gain
        a = jnp.mean(gdy, axis=-1, keepdims=True)
        c = jnp.mean(gdy * xh, axis=-1, keepdims=True)
        return inv * (gdy - a - xh * c)

    def scores_at(n):
        place, n = (acc, n) if n < B * (D // S) else (hid, n - B * (D // S))
        rows, cols = n // (D // S) * TQ, n % (D // S) * S
        return place.at[rows : rows + TQ, cols : cols + S]

    def attend_forward(l):
        def image(b, carry):
            qr = pl.ds(pl.multiple_of(b * TQ, 16), TQ)
            kr = pl.ds(pl.multiple_of(b * S, 16), S)
            for hp in range(H // 2):
                sl = slice(2 * HD * hp, 2 * HD * (hp + 1))
                q = q_s[l, qr, sl]
                k = k_s[l, kr, sl]
                zero = jnp.zeros_like(k)
                scores_at(2 * hp)[...] = mm_nt(q, jnp.where(even_k, k, zero))
                scores_at(2 * hp + 1)[...] = mm_nt(q, jnp.where(even_k, zero, k))
            for hp in range(H // 2):
                sl = slice(2 * HD * hp, 2 * HD * (hp + 1))
                v = v_s[l, kr, sl]
                sums = []
                for h in range(2):
                    here = even_k if h == 0 else jnp.logical_not(even_k)
                    s = scores_at(2 * hp + h)[...] + key_bias
                    top = jnp.max(s, axis=1, keepdims=True)
                    e = jnp.exp2((s - top) * (LOG2E * scale)).astype(BF16)
                    e_s[l, b, hp * 2 + h] = e
                    sums.append(mm(e, jnp.where(here, v, jnp.ones_like(v))))
                top_part = jnp.where(even_q, sums[0], sums[1])
                total = jnp.where(even_q, sums[1], sums[0])
                inv = pltpu.roll(1.0 / total, HD, 1)
                ri_s[l, qr, sl] = inv.astype(BF16)
                o_s[l, qr, sl] = (top_part * inv).astype(BF16)
            return carry

        lax.fori_loop(0, B, image, 0)

    def back_half(l, b, hp, part, first):
        at = pl.multiple_of(hp * 2 * HD, 2 * HD)
        sl = pl.ds(at, 2 * HD)
        qr = pl.ds(pl.multiple_of(b * TQ, 16), TQ)
        kr = pl.ds(pl.multiple_of(b * S + part * SH, 16), SH)
        v = v_s[l, kr, sl]
        spare = pl.ds(pl.multiple_of((b * (H // 2) + hp) * S, 128), TQ)
        if first:
            do = x16[qr, sl].astype(F32) * ri_s[l, qr, sl].astype(F32)
            prod = do * o_s[l, qr, sl].astype(F32)
            d0 = jnp.sum(jnp.where(even_q, prod, 0.0), axis=1, keepdims=True)
            d1 = jnp.sum(jnp.where(even_q, 0.0, prod), axis=1, keepdims=True)
            do16 = do.astype(BF16)
            q_t = q_s[l, qr, sl].T
            do_t = do16.T
            x16[qr, sl] = do16
            gp_s[l, 0 : 2 * HD, spare] = q_t
            gp_s[l, 2 * HD : 4 * HD, spare] = do_t
            acc[qr, sl] = jnp.where(even_q, d0, d1)
        else:
            do16 = x16[qr, sl]
            q_t = gp_s[l, 0 : 2 * HD, spare]
            do_t = gp_s[l, 2 * HD : 4 * HD, spare]
            both = acc[qr, sl]
            d0, d1 = both[:, 0:1], both[:, HD : HD + 1]
        zero = jnp.zeros_like(v)
        stacked = jnp.concatenate([jnp.where(even_h, v, zero), jnp.where(even_h, zero, v)], axis=0)
        dp = mm_nt(do16, stacked)
        keys = slice(part * SH, (part + 1) * SH)
        e = jnp.concatenate([e_s[l, b, hp * 2, :, keys], e_s[l, b, hp * 2 + 1, :, keys]], axis=1)
        ds = (e.astype(F32) * (dp - jnp.where(low_lane, d0, d1))).astype(BF16)
        dk = mm(q_t, ds)
        dv = mm(do_t, e)
        dk = jnp.concatenate([dk[:HD, :SH], dk[HD:, SH:]], axis=0) * scale
        dv = jnp.concatenate([dv[:HD, :SH], dv[HD:, SH:]], axis=0)
        wide[kr, pl.ds(pl.multiple_of(D + at, 128), 2 * HD)] = dk.astype(BF16).T
        wide[kr, pl.ds(pl.multiple_of(2 * D + at, 128), 2 * HD)] = dv.astype(BF16).T
        return ds

    def back_queries(l, b, hp, low, high):
        at = pl.multiple_of(hp * 2 * HD, 2 * HD)
        sl = pl.ds(at, 2 * HD)
        kr = pl.ds(pl.multiple_of(b * S, 16), S)
        k = k_s[l, kr, sl]
        zero = jnp.zeros_like(k)
        dq = mm(jnp.concatenate([low[:, :SH], high[0]], axis=1), jnp.where(even_k, k, zero))
        dq += mm(jnp.concatenate([low[:, SH:], high[1]], axis=1), jnp.where(even_k, zero, k))
        wide[pl.ds(pl.multiple_of(b * S, 16), TQ), sl] = (dq * scale).astype(BF16)

    def pairs_loop(body, lo, hi):
        def one(i, carry):
            body(i // (H // 2), i % (H // 2))
            return carry

        lax.fori_loop(lo, hi, one, 0, unroll=True)

    pairs = B * H // 2

    def send(src, dst, sems, l, device):
        return pltpu.make_async_remote_copy(
            src_ref=src,
            dst_ref=dst,
            send_sem=sems.at[l, 0],
            recv_sem=sems.at[l, 1],
            device_id=device,
            device_id_type=MESH,
        )

    def all_of(slots, l, count, sems):
        view = slots.at[l, 0:count]
        return send(view, view, sems, l, {"mlp": other})

    mine_b = core * G + g

    def reduce_start(l, grad):
        rows = jnp.concatenate([grad, jnp.zeros((G * PB - grad.shape[0], D), F32)], axis=0)
        for j in range(NJ):
            for k in range(G):
                block = rows[k * PB : (k + 1) * PB, 128 * j : 128 * (j + 1)]
                part_h[l, j // HJ * G + k, j % HJ] = block.astype(BF16)
        for k, c in around:
            to = lax.rem(core + c, 2) * G + member(k)
            send(
                part_h.at[l, to], slot_b.at[l, mine_b], sem_b, l, neighbour(k, c)
            ).start()
        slot_b[l, mine_b] = part_h[l, mine_b]

    def reduce_group(l):
        all_of(slot_b, l, 2 * G - 1, sem_b).wait_recv()
        total = slot_b[l, 0].astype(F32)
        for i in range(1, 2 * G):
            total = total + slot_b[l, i].astype(F32)
        slot_c[l, r] = total.astype(BF16)

        def go(k, carry):
            peer = {"dp": rank(k) * G + g}
            send(slot_c.at[l, r], slot_c.at[l, r], sem_c, l, peer).start()
            return carry

        lax.fori_loop(1, R, go, 0, unroll=R <= 4)
        all_of(part_h, l, 2 * G - 1, sem_b).wait_send()

    def square_of(block):
        block = block.astype(F32)
        total = block[0] * block[0]
        for j in range(1, HJ):
            total += block[j] * block[j]
        return total

    def reduce_ranks(l):
        if R > 1:
            all_of(slot_c, l, R - 1, sem_c).wait_recv()

        def add(k, total):
            return total + slot_c[l, k].astype(F32)

        total = lax.fori_loop(0, R, add, jnp.zeros((HJ, PB, 128), F32), unroll=R <= 4)
        fin[l, g] = total.astype(BF16)
        for k in range(1, G):
            peer = {"dp": r * G + member(k)}
            send(fin.at[l, g], fin.at[l, g], sem_d, l, peer).start()
        sq_out[l] = square_of(fin[l, g])
        for k in range(G):
            send(sq_out.at[l], sq_in.at[l, g], sem_e, l, neighbour(k, 1)).start()
        if R > 1:
            all_of(slot_c, l, R - 1, sem_c).wait_send()

    def reduce_end(l):
        all_of(fin, l, G - 1, sem_d).wait()
        all_of(sq_in, l, G, sem_e).wait()

    def mlp_chunk(l, part, j, last_):
        cols = slice(j * C, (j + 1) * C)
        at = slice((part * (FH // C) + j) * C, (part * (FH // C) + j + 1) * C)
        pre = mm(x16[...], w_up[l, part, :, cols]) + ub[part, pl.ds(l, 1), cols]
        cdf = 0.5 + 0.5 * lax.erf(pre * 0.7071067811865476)
        if last_ != "output":
            bell = jnp.exp2(pre * pre * (-0.5 * LOG2E)) * 0.3989422804014327
            gp_s[l, :, at] = (cdf + pre * bell).astype(BF16)
        if last_ != "slope":
            add = mm((pre * cdf).astype(BF16), w_dn[l, part, cols, :])
            if part == 0 and j == 0:
                acc[...] = add
            else:
                acc[...] += add

    chunks = [(part, j) for part in range(2) for j in range(FH // C)]

    def norm_one(l):
        for b in range(B):
            for j in range(NJ):
                seq[b, TK : TK + PN, columns(j)] = prom_v[j, pl.ds(l, PN, stride=L), :]
        gain, shift = norms[l, 0:1, :], norms[l, 1:2, :]
        for b in range(B):
            xh, inv = norm_rows(seq[b])
            at = slice(b * S, (b + 1) * S)
            xh1[l, at, :] = xh.astype(BF16)
            inv_s[l, at, 0:1] = inv
            wide[at, 0:D] = (xh * gain + shift).astype(BF16)

    def attend(l):
        lhs = jnp.concatenate([wide[b * S : b * S + TQ, 0:D] for b in range(B)], axis=0)
        q_s[l] = (mm(lhs, w_qkv[l, :, 0:D]) + bias[l, 0:1, :]).astype(BF16)
        k_s[l] = mm(wide[:, 0:D], w_qkv[l, :, D : 2 * D]).astype(BF16)
        v_s[l] = (mm(wide[:, 0:D], w_qkv[l, :, 2 * D : 3 * D]) + bias[l, 1:2, :]).astype(BF16)
        attend_forward(l)

    def norm_two(l):
        branch = mm(o_s[l], w_out[l]) + bias[l, 2:3, :]
        for b in range(B):
            hid[b * TQ : (b + 1) * TQ, :] = seq[b, 0:TQ, :] + branch[b * TQ : (b + 1) * TQ]
        gain2, shift2 = norms[l, 2:3, :], norms[l, 3:4, :]
        xh, inv = norm_rows(hid[...])
        xh2[l] = xh.astype(BF16)
        inv_s[l, 0 : B * TQ, 1:2] = inv
        x16[...] = (xh * gain2 + shift2).astype(BF16)

    norm_one(0)
    copy_weight(0, 0).wait()
    copy_small(2).start()
    for i in range(1, 4):
        copy_weight(0, i).start()

    def forward(l, carry):
        attend(l)
        for i in range(1, 4):
            copy_weight(l, i).wait()

        @pl.when(l == 0)
        def _():
            for later in range(1, L):
                for i in range(2):
                    push_weight(later, i).start()
                for i in range(4):
                    copy_weight(later, i).start()
            for j in range(NJ):
                copy_cot(j).start()
            copy_small(2).wait()
            push_ub().wait()

        @pl.when(l < L - 1)
        def _():
            norm_two(l)
            for part, j in chunks:
                if part == 1 and j == 0:
                    push_weight(l, 0).wait()
                    push_weight(l, 1).wait()
                mlp_chunk(l, part, j, "both")
            for b in range(B):
                at = slice(b * TQ, (b + 1) * TQ)
                seq[b, 0:TQ, :] = hid[at, :] + acc[at, :] + bias[l, 3:4, :]
            norm_one(l + 1)
            copy_weight(l + 1, 0).wait()

        return carry

    lax.fori_loop(0, L, forward, 0)
    push_weight(L - 1, 0).wait()
    push_weight(L - 1, 1).wait()
    for j in range(NJ):
        copy_cot(j).wait()
    norm_two(L - 1)
    for part, j in chunks:
        mlp_chunk(L - 1, part, j, "slope")
    for b in range(B):
        seq[b, 0:TQ, :] = hid[b * TQ : (b + 1) * TQ, :] + bias[L - 1, 3:4, :]

    def activations_out():
        for b in range(B):
            seq[b, 0:TQ, :] += acc[b * TQ : (b + 1) * TQ, :]
            for j in range(NJ):
                stage_v[j, pl.ds(b, T, stride=B), :] = seq[b, 0:T, 128 * j : 128 * (j + 1)]
        for j in range(NJ):
            tok_v[j, 0 : T * B] = stage_v[j, 0 : T * B].astype(BF16)

    for b in range(B):
        hid[b * TQ + TK - 8 : (b + 1) * TQ, :] = jnp.zeros((TQ - TK + 8, D), F32)

    def store_cot(b, cols, rows):
        hid[b * TQ : b * TQ + T, cols] = rows

    spread(cot_v, store_cot)

    def backward(step, carry):
        l = L - 1 - step
        above = l + 1

        def sum_above(phase):
            pl.when(step > 0)(lambda: phase(above))

        sum_above(reduce_group)
        x16[...] = hid[...].astype(BF16)
        for part in range(2):
            for j in range(FH // C):
                cols = slice(j * C, (j + 1) * C)
                at = slice((part * (FH // C) + j) * C, (part * (FH // C) + j + 1) * C)
                ga = mm_nt(x16[...], w_dn[l, part, cols, :])
                gpre = (gp_s[l, :, at].astype(F32) * ga).astype(BF16)
                add = mm_nt(gpre, w_up[l, part, :, cols])
                if part == 0 and j == 0:
                    acc[...] = add
                else:
                    acc[...] += add
        gain2 = norms[l, 2:3, :]

        new = hid[...] + ln_back(
            acc[...], xh2[l].astype(F32), inv_s[l, 0 : B * TQ, 1:2], gain2
        )
        hid[...] = new
        x16[...] = mm_nt(new.astype(BF16), w_out[l]).astype(BF16)
        gain = norms[l, 0:1, :]

        def high_keys(b, hp):
            ds = back_half(l, b, hp, 1, True)
            e_s[l, b, hp * 2, :, SH:] = ds[:, :SH]
            e_s[l, b, hp * 2 + 1, :, SH:] = ds[:, SH:]

        def low_keys(b, hp):
            ds = back_half(l, b, hp, 0, False)
            back_queries(
                l, b, hp, ds, (e_s[l, b, hp * 2, :, SH:], e_s[l, b, hp * 2 + 1, :, SH:])
            )

        def prompt_gradient():
            base = TK // 16 * 16
            lhs = jnp.concatenate(
                [wide[b * S + base : (b + 1) * S, D : 3 * D] for b in range(B)], axis=0
            )
            full = mm_nt(lhs, w_qkv[l, :, D : 3 * D])
            n = S - base
            dprom = full[TK - base : n]
            for b in range(1, B):
                dprom = dprom + full[b * n + TK - base : (b + 1) * n]
            xh_p = xh1[l, base:S, :].astype(F32)[TK - base :]
            return ln_back(dprom, xh_p, inv_s[l, TK:S, 0:1], gain)

        pairs_loop(high_keys, 0, pairs)
        reduce_start(l, prompt_gradient())
        sum_above(reduce_ranks)
        pairs_loop(low_keys, 0, pairs)
        lhs = jnp.concatenate([wide[b * S : b * S + TQ, :] for b in range(B)], axis=0)
        acc[...] = mm_nt(lhs, w_qkv[l])
        pl.when(l == 0)(lambda: reduce_group(l))
        sum_above(reduce_end)
        for b in range(B):
            at = slice(b * TQ, b * TQ + TK)
            dx = ln_back(
                acc[at, :],
                xh1[l, b * S : b * S + TQ, :].astype(F32)[:TK],
                inv_s[l, b * S : b * S + TK, 0:1],
                gain,
            )
            hid[at, :] = hid[at, :] + dx
        return carry

    lax.fori_loop(0, L, backward, 0)
    for j in range(HJ):
        copy_moment(0, j).start()
        copy_moment(1, j).start()
    x16[...] = (xh2[L - 1].astype(F32) * norms[L - 1, 2:3, :] + norms[L - 1, 3:4, :]).astype(BF16)
    for i, (part, j) in enumerate(chunks):
        if i == len(chunks) - 2:
            reduce_ranks(0)
        mlp_chunk(L - 1, part, j, "output")
    activations_out()
    for j in range(NJ):
        for b in range(B):
            stage_v[j, pl.ds(b, T, stride=B), :] = hid[
                b * TQ : b * TQ + T, 128 * j : 128 * (j + 1)
            ]
    reduce_end(0)

    grad_v = grad_nat.reshape(HJ, PP * L, 128)
    for l in range(L):
        for k in range(G):
            rows = min(PB, PN - k * PB)
            for j in range(HJ):
                grad_v[j, pl.ds(k * PB * L + l, rows, stride=L), :] = fin[l, k, j].astype(F32)[:rows]
    n = PN * L
    own, theirs = jnp.zeros((PB, 128), F32), jnp.zeros((PB, 128), F32)
    for l in range(L):
        for k in range(G):
            own += square_of(fin[l, k])
            theirs += sq_in[l, k]
    squares = jnp.sum(own + theirs, axis=(0, 1), keepdims=True)
    grad_norm = jnp.sqrt(squares)
    norm_s[...] = grad_norm
    factor = jnp.minimum(1.0, clip_limit / (grad_norm + 1e-06))
    fix_first = 1.0 - beta_one**STEP
    fix_second = 1.0 - beta_two**STEP
    for j in range(HJ):
        copy_moment(0, j).wait()
        copy_moment(1, j).wait()
        first_v = first_nat.reshape(HJ, PP * L, 128)
        second_v = second_nat.reshape(HJ, PP * L, 128)
        prompt_v = prompt_nat.reshape(HJ, PP * L, 128)
        clipped = grad_v[j, 0:n, :] * factor
        new_first = beta_one * first_v[j, 0:n, :] + (1.0 - beta_one) * clipped
        new_second = beta_two * second_v[j, 0:n, :] + (1.0 - beta_two) * clipped * clipped
        first_v[j, 0:n, :] = new_first
        second_v[j, 0:n, :] = new_second
        old = prom_v[core * HJ + j, 0:n, :]
        prompt_v[j, 0:n, :] = old - learn_rate * (
            new_first / fix_first / (jnp.sqrt(new_second / fix_second) + adam_eps)
            + weight_decay * old
        )


def hand_on_kernel(*refs):
    n = (len(refs) - 1) // 2
    sources, targets, sem = refs[:n], refs[n : 2 * n], refs[2 * n]
    copies = []
    for src, dst in zip(sources, targets):
        if len(src.shape) == 2:
            copies.append(pltpu.make_async_copy(src, dst, sem.at[len(copies)]))
        else:
            rows = dst.shape[0]
            for j in range(src.shape[0]):
                view = dst.at[:, :, 128 * j : 128 * (j + 1)]
                copies.append(
                    pltpu.make_async_copy(src.at[j, 0:rows], view, sem.at[len(copies)])
                )
    for copy in copies:
        copy.start()
    for copy in copies:
        copy.wait()


def hand_on(arrays, counts):
    def whole(a, rows):
        shape = a.shape if len(a.shape) == 2 else (rows, a.shape[2], a.shape[0] * a.shape[3])
        return jax.ShapeDtypeStruct(shape, a.dtype)

    copies = sum(1 if len(a.shape) == 2 else a.shape[0] for a in arrays)
    return pl.pallas_call(
        hand_on_kernel,
        out_shape=tuple(whole(a, rows) for a, rows in zip(arrays, counts)),
        in_specs=[pl.BlockSpec(memory_space=VMEM)] * len(arrays),
        out_specs=(pl.BlockSpec(memory_space=pl.ANY),) * len(arrays),
        scratch_shapes=[DMA((copies,))],
        compiler_params=pltpu.CompilerParams(vmem_limit_bytes=2**20),
    )(*arrays)


def native(x):
    return x.transpose(1, 0, 2)


def local(
    ndp, tokens, cotangent, prompts, first_moment, second_moment, norm_params, bias_rows,
    qkv_weight, out_weight, up_weight, up_bias, down_weight,
):
    B, T, D = tokens.shape
    L, PN, _ = prompts.shape
    FH = down_weight.shape[1]
    TK = up_to(T, 8)
    PP = up_to(PN, 8)
    S = up_to(TK + PP, 128)
    TQ = up_to(T, 16)
    G = 4
    R = ndp // G
    NJ, HJ, PB = D // 128, D // 256, 16
    dims = (B, T, D, L, PN, TK, PP, S, TQ, FH, G, R)
    H = HEADS
    n_local = 2 * NJ + 3 * HJ + 3
    scratch = [
        VMEM((NJ, TK, B, 128), BF16),
        VMEM((NJ, PP, L, 128), F32),
        VMEM((L, 4, D), F32),
        VMEM((L, 4, D), F32),
        VMEM((L, D, 3 * D), BF16),
        VMEM((L, D, D), BF16),
        VMEM((L, 2, D, FH), BF16),
        VMEM((2, L, FH), F32),
        VMEM((L, 2, FH, D), BF16),
        VMEM((B, S, D), F32),
        VMEM((B * TQ, D), F32),
        VMEM((B * TQ, D), F32),
        VMEM((B * S, 3 * D), BF16),
        VMEM((B * TQ, D), BF16),
        VMEM((L, B * S, D), BF16),
        VMEM((L, B * TQ, D), BF16),
        VMEM((L, B * S, 2), F32),
        VMEM((L, B * TQ, D), BF16),
        VMEM((L, B * S, D), BF16),
        VMEM((L, B * S, D), BF16),
        VMEM((L, B, H, TQ, S), BF16),
        VMEM((L, B * TQ, D), BF16),
        VMEM((L, B * TQ, D), BF16),
        VMEM((L, B * TQ, 2 * FH), BF16),
        VMEM((L, 2 * G, HJ, PB, 128), BF16),
        VMEM((L, 2 * G, HJ, PB, 128), BF16),
        VMEM((L, R, HJ, PB, 128), BF16),
        VMEM((L, G, HJ, PB, 128), BF16),
        VMEM((L, PB, 128), F32),
        VMEM((L, G, PB, 128), F32),
        DMA((n_local,)),
        DMA((L, 4)),
        DMA((2, HJ + 1)),
        DMA((L, 2, 2)),
        DMA((L, 2)),
        DMA((L, 2)),
        DMA((L, 2)),
        DMA((L, 2)),
    ]
    any_spec = pl.BlockSpec(memory_space=pl.ANY)
    small = VMEM((HJ, PP, L, 128), F32)
    results = pl.pallas_call(
        functools.partial(main_kernel, dims),
        out_shape=(
            VMEM((NJ, TK, B, 128), BF16),
            VMEM((NJ, TK, B, 128), F32),
            small,
            VMEM((1, 1), F32),
            small,
            small,
            small,
        ),
        in_specs=[any_spec] * 12,
        scratch_shapes=scratch,
        compiler_params=pltpu.CompilerParams(
            collective_id=0, has_side_effects=True, vmem_limit_bytes=61 * 2**20
        ),
    )(
        native(tokens), native(cotangent), native(prompts), native(first_moment),
        native(second_moment), norm_params, bias_rows, qkv_weight, out_weight,
        up_weight, up_bias, down_weight,
    )
    act, igrad, grad, norm, new_first, new_second, new_prompts = hand_on(
        results, (T, T, PN, 1, PN, PN, PN)
    )
    return (
        native(act), native(igrad), native(grad), norm.reshape(()),
        native(new_first), native(new_second), native(new_prompts),
    )


def solution(mesh):
    ndp = mesh.shape["dp"]
    return jax.shard_map(
        functools.partial(local, ndp),
        mesh=mesh,
        in_specs=(
            P(("dp", "mlp"), None, None),
            P(("dp", "mlp"), None, None),
            P(None, None, "mlp"),
            P(None, None, "mlp"),
            P(None, None, "mlp"),
            P(),
            P(),
            P(),
            P(),
            P(None, None, "mlp"),
            P(None, "mlp"),
            P(None, "mlp", None),
        ),
        out_specs=(
            P(("dp", "mlp"), None, None),
            P(("dp", "mlp"), None, None),
            P(None, None, "mlp"),
            P(),
            P(None, None, "mlp"),
            P(None, None, "mlp"),
            P(None, None, "mlp"),
        ),
        check_vma=False,
    )
```

```python
import functools

import jax
import jax.numpy as jnp
from jax import lax
from jax.experimental import pallas as pl
from jax.experimental.pallas import tpu as pltpu
from jax.sharding import PartitionSpec as P

HEADS = 12
STEP = 10
MESH = pl.DeviceIdType.MESH
VMEM = pltpu.VMEM
DMA = pltpu.SemaphoreType.DMA
BF16 = jnp.bfloat16
F32 = jnp.float32

norm_eps = 1e-06
clip_limit = 1.0
beta_one = 0.9
beta_two = 0.999
learn_rate = 1.5
weight_decay = 0.05
adam_eps = 1e-08
LOG2E = 1.4426950408889634


def up_to(value, step):
    return -(-value // step) * step


def mm(left, right):
    return jnp.dot(left, right, preferred_element_type=F32)


def mm_nt(left, right):
    return lax.dot_general(left, right, (((1,), (1,)), ((), ())), preferred_element_type=F32)


def mm_tn(left, right):
    return lax.dot_general(left, right, (((0,), (0,)), ((), ())), preferred_element_type=F32)


def rows_loop(count, step, body, unroll=1):
    def one(i, carry):
        body(pl.multiple_of(i * step, step))
        return carry

    lax.fori_loop(0, count // step, one, 0, unroll=unroll)


def main_kernel(
    dims,
    tok_hbm,
    cot_hbm,
    prompts_hbm,
    first_hbm,
    second_hbm,
    norms_hbm,
    bias_hbm,
    qkv_hbm,
    out_hbm,
    up_hbm,
    ub_hbm,
    dn_hbm,
    tok_nat,
    stage_nat,
    grad_nat,
    norm_s,
    first_nat,
    second_nat,
    prompt_nat,
    cot_nat,
    prom_nat,
    norms,
    bias,
    w_qkv,
    w_out,
    w_up,
    ub,
    w_dn,
    seq,
    hid,
    acc,
    wide,
    x16,
    xh1,
    xh2,
    inv_s,
    q_s,
    k_s,
    v_s,
    e_s,
    ri_s,
    o_s,
    gp_s,
    part_h,
    slot_b,
    slot_c,
    fin,
    sq_out,
    sq_in,
    local_sem,
    weight_sem,
    push_sem,
    push_w_sem,
    sem_b,
    sem_c,
    sem_d,
    sem_e,
):
    B, T, D, L, PN, TK, PP, S, TQ, FH, G, R = dims
    H = HEADS
    HD = D // H
    C = 768
    NJ = D // 128
    HJ = NJ // 2
    PB = 16
    M = B * TK
    core = lax.axis_index("mlp")
    other = 1 - core
    me = lax.axis_index("dp")
    g, r = lax.rem(me, G), me // G
    half = D // 2

    def member(k):
        return lax.rem(g + k, G)

    def rank(k):
        return lax.rem(r + k, R)

    around = [(k, c) for k in range(G) for c in range(2)][1:]

    def neighbour(k, c):
        return {"dp": r * G + member(k), "mlp": lax.rem(core + c, 2)}

    def columns(j):
        return slice(128 * j, 128 * (j + 1))

    def local(i, src, dst):
        return pltpu.make_async_copy(src, dst, local_sem.at[i])

    def copy_tok(j):
        return local(j, tok_hbm.at[:, :, columns(j)], tok_nat.at[j, 0:T])

    def copy_cot(j):
        return local(NJ + j, cot_hbm.at[:, :, columns(j)], cot_nat.at[j, 0:T])

    def copy_prom(j):
        return local(
            2 * NJ + j, prompts_hbm.at[:, :, columns(j)], prom_nat.at[core * HJ + j, 0:PN]
        )

    def copy_moment(i, j):
        src = (first_hbm, second_hbm)[i]
        return local(
            2 * NJ + (i + 1) * HJ + j, src.at[:, :, columns(j)], (first_nat, second_nat)[i].at[j, 0:PN]
        )

    def copy_small(i):
        src, dst = ((norms_hbm, norms), (bias_hbm, bias), (ub_hbm, ub.at[0]))[i]
        return local(2 * NJ + 3 * HJ + i, src, dst)

    def copy_weight(l, i):
        src, dst = (
            (qkv_hbm.at[l], w_qkv.at[l]),
            (out_hbm.at[l], w_out.at[l]),
            (up_hbm.at[l], w_up.at[l, 0]),
            (dn_hbm.at[l], w_dn.at[l, 0]),
        )[i]
        return pltpu.make_async_copy(src, dst, weight_sem.at[l, i])

    def push(src, dst, send_at, recv_at):
        return pltpu.make_async_remote_copy(
            src_ref=src,
            dst_ref=dst,
            send_sem=send_at,
            recv_sem=recv_at,
            device_id={"mlp": other},
            device_id_type=MESH,
        )

    def push_prom(j):
        return push(
            prompts_hbm.at[:, :, columns(j)],
            prom_nat.at[core * HJ + j, 0:PN],
            push_sem.at[0, j],
            push_sem.at[1, j],
        )

    def push_ub():
        return push(ub_hbm, ub.at[1], push_sem.at[0, HJ], push_sem.at[1, HJ])

    def push_weight(l, i):
        src, dst = ((up_hbm.at[l], w_up.at[l, 1]), (dn_hbm.at[l], w_dn.at[l, 1]))[i]
        return push(src, dst, push_w_sem.at[l, 0, i], push_w_sem.at[l, 1, i])

    copy_weight(0, 0).start()
    barrier = pltpu.get_barrier_semaphore()
    for k, c in around:
        pl.semaphore_signal(barrier, inc=1, device_id=neighbour(k, c), device_id_type=MESH)

    def greet(k, carry):
        pl.semaphore_signal(
            barrier, inc=1, device_id={"dp": rank(k) * G + g}, device_id_type=MESH
        )
        return carry

    lax.fori_loop(1, R, greet, 0)
    for j in range(NJ):
        copy_tok(j).start()
    for j in range(HJ):
        copy_prom(j).start()
    copy_small(0).start()
    copy_small(1).start()
    pl.semaphore_wait(barrier, len(around) + R - 1)
    for j in range(HJ):
        push_prom(j).start()
    push_ub().start()
    push_weight(0, 0).start()
    push_weight(0, 1).start()

    tok_v = tok_nat.reshape(NJ, TK * B, 128)
    cot_v = cot_nat.reshape(NJ, TK * B, 128)
    stage_v = stage_nat.reshape(NJ, TK * B, 128)
    prom_v = prom_nat.reshape(NJ, PP * L, 128)

    lane = lax.broadcasted_iota(jnp.int32, (1, S), 1)
    valid = (lane < T) | ((lane >= TK) & (lane < TK + PN))
    key_bias = jnp.where(valid, 0.0, -1e30).astype(F32)
    even_q = lax.broadcasted_iota(jnp.int32, (TQ, 2 * HD), 1) < HD
    even_k = lax.broadcasted_iota(jnp.int32, (S, 2 * HD), 1) < HD
    SH = S // 2
    even_h = lax.broadcasted_iota(jnp.int32, (SH, 2 * HD), 1) < HD
    low_lane = lax.broadcasted_iota(jnp.int32, (TQ, S), 1) < SH
    scale = HD**-0.5

    def spread(src_v, store):
        for j in range(NJ):
            stage_v[j] = src_v[j].astype(F32)
        for b in range(B):
            for j in range(NJ):
                store(b, slice(128 * j, 128 * (j + 1)), stage_v[j, pl.ds(b, T, stride=B), :])

    for b in range(B):
        seq[b, TK - 8 :, :] = jnp.zeros((S - TK + 8, D), F32)
    for j in range(NJ):
        copy_tok(j).wait()

    def store_tok(b, cols, rows):
        seq[b, 0:T, cols] = rows

    spread(tok_v, store_tok)
    copy_small(0).wait()
    copy_small(1).wait()
    for j in range(HJ):
        copy_prom(j).wait()
        push_prom(j).wait()

    def norm_rows(x):
        mean = jnp.mean(x, axis=-1, keepdims=True)
        centre = x - mean
        spread_ = jnp.mean(centre * centre, axis=-1, keepdims=True)
        inv = lax.rsqrt(spread_ + norm_eps)
        return centre * inv, inv

    def ln_back(dy, xh, inv, gain):
        gdy = dy * gain
        a = jnp.mean(gdy, axis=-1, keepdims=True)
        c = jnp.mean(gdy * xh, axis=-1, keepdims=True)
        return inv * (gdy - a - xh * c)

    def scores_at(n):
        place, n = (acc, n) if n < B * (D // S) else (hid, n - B * (D // S))
        rows, cols = n // (D // S) * TQ, n % (D // S) * S
        return place.at[rows : rows + TQ, cols : cols + S]

    def attend_forward(l):
        for b in range(B):
            qr = slice(b * TQ, (b + 1) * TQ)
            kr = slice(b * S, (b + 1) * S)
            for hp in range(H // 2):
                sl = slice(2 * HD * hp, 2 * HD * (hp + 1))
                q = q_s[l, qr, sl]
                k = k_s[l, kr, sl]
                zero = jnp.zeros_like(k)
                scores_at(2 * hp)[...] = mm_nt(q, jnp.where(even_k, k, zero))
                scores_at(2 * hp + 1)[...] = mm_nt(q, jnp.where(even_k, zero, k))
            for hp in range(H // 2):
                sl = slice(2 * HD * hp, 2 * HD * (hp + 1))
                v = v_s[l, kr, sl]
                sums = []
                for h in range(2):
                    here = even_k if h == 0 else jnp.logical_not(even_k)
                    s = scores_at(2 * hp + h)[...] + key_bias
                    top = jnp.max(s, axis=1, keepdims=True)
                    e = jnp.exp2((s - top) * (LOG2E * scale)).astype(BF16)
                    e_s[l, b, hp * 2 + h] = e
                    sums.append(mm(e, jnp.where(here, v, jnp.ones_like(v))))
                top_part = jnp.where(even_q, sums[0], sums[1])
                total = jnp.where(even_q, sums[1], sums[0])
                inv = pltpu.roll(1.0 / total, HD, 1)
                ri_s[l, qr, sl] = inv.astype(BF16)
                o_s[l, qr, sl] = (top_part * inv).astype(BF16)

    def back_half(l, b, hp, part, first):
        at = pl.multiple_of(hp * 2 * HD, 2 * HD)
        sl = pl.ds(at, 2 * HD)
        qr = pl.ds(pl.multiple_of(b * TQ, 16), TQ)
        kr = pl.ds(pl.multiple_of(b * S + part * SH, 16), SH)
        v = v_s[l, kr, sl]
        spare = pl.ds(pl.multiple_of((b * (H // 2) + hp) * S, 128), TQ)
        if first:
            do = x16[qr, sl].astype(F32) * ri_s[l, qr, sl].astype(F32)
            prod = do * o_s[l, qr, sl].astype(F32)
            d0 = jnp.sum(jnp.where(even_q, prod, 0.0), axis=1, keepdims=True)
            d1 = jnp.sum(jnp.where(even_q, 0.0, prod), axis=1, keepdims=True)
            do16 = do.astype(BF16)
            q_t = q_s[l, qr, sl].T
            do_t = do16.T
            x16[qr, sl] = do16
            gp_s[l, 0 : 2 * HD, spare] = q_t
            gp_s[l, 2 * HD : 4 * HD, spare] = do_t
            acc[qr, sl] = jnp.where(even_q, d0, d1)
        else:
            do16 = x16[qr, sl]
            q_t = gp_s[l, 0 : 2 * HD, spare]
            do_t = gp_s[l, 2 * HD : 4 * HD, spare]
            both = acc[qr, sl]
            d0, d1 = both[:, 0:1], both[:, HD : HD + 1]
        zero = jnp.zeros_like(v)
        stacked = jnp.concatenate([jnp.where(even_h, v, zero), jnp.where(even_h, zero, v)], axis=0)
        dp = mm_nt(do16, stacked)
        keys = slice(part * SH, (part + 1) * SH)
        e = jnp.concatenate([e_s[l, b, hp * 2, :, keys], e_s[l, b, hp * 2 + 1, :, keys]], axis=1)
        ds = (e.astype(F32) * (dp - jnp.where(low_lane, d0, d1))).astype(BF16)
        dk = mm(q_t, ds)
        dv = mm(do_t, e)
        dk = jnp.concatenate([dk[:HD, :SH], dk[HD:, SH:]], axis=0) * scale
        dv = jnp.concatenate([dv[:HD, :SH], dv[HD:, SH:]], axis=0)
        wide[kr, pl.ds(pl.multiple_of(D + at, 128), 2 * HD)] = dk.astype(BF16).T
        wide[kr, pl.ds(pl.multiple_of(2 * D + at, 128), 2 * HD)] = dv.astype(BF16).T
        return ds

    def back_queries(l, b, hp, low, high):
        at = pl.multiple_of(hp * 2 * HD, 2 * HD)
        sl = pl.ds(at, 2 * HD)
        kr = pl.ds(pl.multiple_of(b * S, 16), S)
        k = k_s[l, kr, sl]
        zero = jnp.zeros_like(k)
        dq = mm(jnp.concatenate([low[:, :SH], high[0]], axis=1), jnp.where(even_k, k, zero))
        dq += mm(jnp.concatenate([low[:, SH:], high[1]], axis=1), jnp.where(even_k, zero, k))
        wide[pl.ds(pl.multiple_of(b * S, 16), TQ), sl] = (dq * scale).astype(BF16)

    def pairs_loop(body, lo, hi):
        def one(i, carry):
            body(i // (H // 2), i % (H // 2))
            return carry

        lax.fori_loop(lo, hi, one, 0, unroll=True)

    pairs = B * H // 2

    def send(src, dst, sems, l, device):
        return pltpu.make_async_remote_copy(
            src_ref=src,
            dst_ref=dst,
            send_sem=sems.at[l, 0],
            recv_sem=sems.at[l, 1],
            device_id=device,
            device_id_type=MESH,
        )

    def all_of(slots, l, count, sems):
        view = slots.at[l, 0:count]
        return send(view, view, sems, l, {"mlp": other})

    mine_b = core * G + g

    def reduce_start(l, grad):
        rows = jnp.concatenate([grad, jnp.zeros((G * PB - grad.shape[0], D), F32)], axis=0)
        for j in range(NJ):
            for k in range(G):
                block = rows[k * PB : (k + 1) * PB, 128 * j : 128 * (j + 1)]
                part_h[l, j // HJ * G + k, j % HJ] = block.astype(BF16)
        for k, c in around:
            to = lax.rem(core + c, 2) * G + member(k)
            send(
                part_h.at[l, to], slot_b.at[l, mine_b], sem_b, l, neighbour(k, c)
            ).start()
        slot_b[l, mine_b] = part_h[l, mine_b]

    def reduce_group(l):
        all_of(slot_b, l, 2 * G - 1, sem_b).wait_recv()
        total = slot_b[l, 0].astype(F32)
        for i in range(1, 2 * G):
            total = total + slot_b[l, i].astype(F32)
        slot_c[l, r] = total.astype(BF16)

        def go(k, carry):
            peer = {"dp": rank(k) * G + g}
            send(slot_c.at[l, r], slot_c.at[l, r], sem_c, l, peer).start()
            return carry

        lax.fori_loop(1, R, go, 0, unroll=R <= 4)
        all_of(part_h, l, 2 * G - 1, sem_b).wait_send()

    def square_of(block):
        block = block.astype(F32)
        total = block[0] * block[0]
        for j in range(1, HJ):
            total += block[j] * block[j]
        return total

    def reduce_ranks(l):
        if R > 1:
            all_of(slot_c, l, R - 1, sem_c).wait_recv()

        def add(k, total):
            return total + slot_c[l, k].astype(F32)

        total = lax.fori_loop(0, R, add, jnp.zeros((HJ, PB, 128), F32), unroll=R <= 4)
        fin[l, g] = total.astype(BF16)
        for k in range(1, G):
            peer = {"dp": r * G + member(k)}
            send(fin.at[l, g], fin.at[l, g], sem_d, l, peer).start()
        sq_out[l] = square_of(fin[l, g])
        for k in range(G):
            send(sq_out.at[l], sq_in.at[l, g], sem_e, l, neighbour(k, 1)).start()
        if R > 1:
            all_of(slot_c, l, R - 1, sem_c).wait_send()

    def reduce_end(l):
        all_of(fin, l, G - 1, sem_d).wait()
        all_of(sq_in, l, G, sem_e).wait()

    def mlp_chunk(l, part, j, last_):
        cols = slice(j * C, (j + 1) * C)
        at = slice((part * (FH // C) + j) * C, (part * (FH // C) + j + 1) * C)
        pre = mm(x16[0:M, :], w_up[l, part, :, cols]) + ub[part, pl.ds(l, 1), cols]
        cdf = 0.5 + 0.5 * lax.erf(pre * 0.7071067811865476)
        if last_ != "output":
            bell = jnp.exp2(pre * pre * (-0.5 * LOG2E)) * 0.3989422804014327
            gp_s[l, :, at] = (cdf + pre * bell).astype(BF16)
        if last_ != "slope":
            add = mm((pre * cdf).astype(BF16), w_dn[l, part, cols, :])
            if part == 0 and j == 0:
                acc[0:M, :] = add
            else:
                acc[0:M, :] += add

    chunks = [(part, j) for part in range(2) for j in range(FH // C)]

    def norm_one(l):
        for b in range(B):
            for j in range(NJ):
                seq[b, TK : TK + PN, columns(j)] = prom_v[j, pl.ds(l, PN, stride=L), :]
        gain, shift = norms[l, 0:1, :], norms[l, 1:2, :]
        for b in range(B):
            xh, inv = norm_rows(seq[b])
            at = slice(b * S, (b + 1) * S)
            xh1[l, at, :] = xh.astype(BF16)
            inv_s[l, at, 0:1] = inv
            wide[at, 0:D] = (xh * gain + shift).astype(BF16)

    def attend(l):
        lhs = jnp.concatenate([wide[b * S : b * S + TQ, 0:D] for b in range(B)], axis=0)
        q_s[l] = (mm(lhs, w_qkv[l, :, 0:D]) + bias[l, 0:1, :]).astype(BF16)
        k_s[l] = mm(wide[:, 0:D], w_qkv[l, :, D : 2 * D]).astype(BF16)
        v_s[l] = (mm(wide[:, 0:D], w_qkv[l, :, 2 * D : 3 * D]) + bias[l, 1:2, :]).astype(BF16)
        attend_forward(l)

    def norm_two(l):
        branch = mm(o_s[l], w_out[l]) + bias[l, 2:3, :]
        for b in range(B):
            hid[b * TK : (b + 1) * TK, :] = seq[b, 0:TK, :] + branch[b * TQ : b * TQ + TK]
        gain2, shift2 = norms[l, 2:3, :], norms[l, 3:4, :]
        xh, inv = norm_rows(hid[0:M, :])
        xh2[l] = xh.astype(BF16)
        inv_s[l, 0:M, 1:2] = inv
        x16[0:M, :] = (xh * gain2 + shift2).astype(BF16)

    norm_one(0)
    copy_weight(0, 0).wait()
    copy_small(2).start()
    for i in range(1, 4):
        copy_weight(0, i).start()

    def forward(l, carry):
        attend(l)
        for i in range(1, 4):
            copy_weight(l, i).wait()

        @pl.when(l == 0)
        def _():
            for later in range(1, L):
                for i in range(2):
                    push_weight(later, i).start()
                for i in range(4):
                    copy_weight(later, i).start()
            for j in range(NJ):
                copy_cot(j).start()
            copy_small(2).wait()
            push_ub().wait()

        @pl.when(l < L - 1)
        def _():
            norm_two(l)
            for part, j in chunks:
                if part == 1 and j == 0:
                    push_weight(l, 0).wait()
                    push_weight(l, 1).wait()
                mlp_chunk(l, part, j, "both")
            for b in range(B):
                at = slice(b * TK, (b + 1) * TK)
                seq[b, 0:TK, :] = hid[at, :] + acc[at, :] + bias[l, 3:4, :]
            norm_one(l + 1)
            copy_weight(l + 1, 0).wait()

        return carry

    lax.fori_loop(0, L, forward, 0)
    push_weight(L - 1, 0).wait()
    push_weight(L - 1, 1).wait()
    for j in range(NJ):
        copy_cot(j).wait()
    norm_two(L - 1)
    for part, j in chunks:
        mlp_chunk(L - 1, part, j, "slope")
    for b in range(B):
        seq[b, 0:TK, :] = hid[b * TK : (b + 1) * TK, :] + bias[L - 1, 3:4, :]

    def activations_out():
        for b in range(B):
            seq[b, 0:TK, :] += acc[b * TK : (b + 1) * TK, :]
            for j in range(NJ):
                stage_v[j, pl.ds(b, T, stride=B), :] = seq[b, 0:T, 128 * j : 128 * (j + 1)]
        for j in range(NJ):
            tok_v[j] = stage_v[j].astype(BF16)

    for b in range(B):
        hid[(b + 1) * TK - 8 : (b + 1) * TK, :] = jnp.zeros((8, D), F32)

    def store_cot(b, cols, rows):
        hid[b * TK : b * TK + T, cols] = rows

    spread(cot_v, store_cot)

    def backward(step, carry):
        l = L - 1 - step
        above = l + 1

        def sum_above(phase):
            pl.when(step > 0)(lambda: phase(above))

        sum_above(reduce_group)
        x16[0:M, :] = hid[0:M, :].astype(BF16)
        for part in range(2):
            for j in range(FH // C):
                cols = slice(j * C, (j + 1) * C)
                at = slice((part * (FH // C) + j) * C, (part * (FH // C) + j + 1) * C)
                ga = mm_nt(x16[0:M, :], w_dn[l, part, cols, :])
                gpre = (gp_s[l, :, at].astype(F32) * ga).astype(BF16)
                add = mm_nt(gpre, w_up[l, part, :, cols])
                if part == 0 and j == 0:
                    acc[0:M, :] = add
                else:
                    acc[0:M, :] += add
        gain2 = norms[l, 2:3, :]

        new = hid[0:M, :] + ln_back(
            acc[0:M, :], xh2[l].astype(F32), inv_s[l, 0:M, 1:2], gain2
        )
        hid[0:M, :] = new
        grad_mixed = mm_nt(new.astype(BF16), w_out[l])
        for b in range(B):
            rows = [grad_mixed[b * TK : (b + 1) * TK], jnp.zeros((TQ - TK, D), F32)]
            x16[b * TQ : (b + 1) * TQ, :] = jnp.concatenate(rows, axis=0).astype(BF16)
        gain = norms[l, 0:1, :]

        def high_keys(b, hp):
            ds = back_half(l, b, hp, 1, True)
            e_s[l, b, hp * 2, :, SH:] = ds[:, :SH]
            e_s[l, b, hp * 2 + 1, :, SH:] = ds[:, SH:]

        def low_keys(b, hp):
            ds = back_half(l, b, hp, 0, False)
            back_queries(
                l, b, hp, ds, (e_s[l, b, hp * 2, :, SH:], e_s[l, b, hp * 2 + 1, :, SH:])
            )

        def prompt_gradient():
            base = TK // 16 * 16
            lhs = jnp.concatenate(
                [wide[b * S + base : (b + 1) * S, D : 3 * D] for b in range(B)], axis=0
            )
            full = mm_nt(lhs, w_qkv[l, :, D : 3 * D])
            n = S - base
            dprom = full[TK - base : n]
            for b in range(1, B):
                dprom = dprom + full[b * n + TK - base : (b + 1) * n]
            xh_p = xh1[l, base:S, :].astype(F32)[TK - base :]
            return ln_back(dprom, xh_p, inv_s[l, TK:S, 0:1], gain)

        pairs_loop(high_keys, 0, pairs)
        reduce_start(l, prompt_gradient())
        sum_above(reduce_ranks)
        pairs_loop(low_keys, 0, pairs)
        lhs = jnp.concatenate([wide[b * S : b * S + TQ, :] for b in range(B)], axis=0)
        acc[...] = mm_nt(lhs, w_qkv[l])
        pl.when(l == 0)(lambda: reduce_group(l))
        sum_above(reduce_end)
        for b in range(B):
            at = slice(b * TK, (b + 1) * TK)
            dx = ln_back(
                acc[b * TQ : b * TQ + TK, :],
                xh1[l, b * S : b * S + TQ, :].astype(F32)[:TK],
                inv_s[l, b * S : b * S + TK, 0:1],
                gain,
            )
            hid[at, :] = hid[at, :] + dx
        return carry

    lax.fori_loop(0, L, backward, 0)
    for j in range(HJ):
        copy_moment(0, j).start()
        copy_moment(1, j).start()
    x16[0:M, :] = (xh2[L - 1].astype(F32) * norms[L - 1, 2:3, :] + norms[L - 1, 3:4, :]).astype(BF16)
    for i, (part, j) in enumerate(chunks):
        if i == len(chunks) - 2:
            reduce_ranks(0)
        mlp_chunk(L - 1, part, j, "output")
    activations_out()
    for j in range(NJ):
        for b in range(B):
            stage_v[j, pl.ds(b, T, stride=B), :] = hid[
                b * TK : b * TK + T, 128 * j : 128 * (j + 1)
            ]
    reduce_end(0)

    grad_v = grad_nat.reshape(HJ, PP * L, 128)
    for l in range(L):
        for k in range(G):
            rows = min(PB, PN - k * PB)
            for j in range(HJ):
                grad_v[j, pl.ds(k * PB * L + l, rows, stride=L), :] = fin[l, k, j].astype(F32)[:rows]
    n = PN * L
    own, theirs = jnp.zeros((PB, 128), F32), jnp.zeros((PB, 128), F32)
    for l in range(L):
        for k in range(G):
            own += square_of(fin[l, k])
            theirs += sq_in[l, k]
    squares = jnp.sum(own + theirs, axis=(0, 1), keepdims=True)
    grad_norm = jnp.sqrt(squares)
    norm_s[...] = grad_norm
    factor = jnp.minimum(1.0, clip_limit / (grad_norm + 1e-06))
    fix_first = 1.0 - beta_one**STEP
    fix_second = 1.0 - beta_two**STEP
    for j in range(HJ):
        copy_moment(0, j).wait()
        copy_moment(1, j).wait()
        first_v = first_nat.reshape(HJ, PP * L, 128)
        second_v = second_nat.reshape(HJ, PP * L, 128)
        prompt_v = prompt_nat.reshape(HJ, PP * L, 128)
        clipped = grad_v[j, 0:n, :] * factor
        new_first = beta_one * first_v[j, 0:n, :] + (1.0 - beta_one) * clipped
        new_second = beta_two * second_v[j, 0:n, :] + (1.0 - beta_two) * clipped * clipped
        first_v[j, 0:n, :] = new_first
        second_v[j, 0:n, :] = new_second
        old = prom_v[core * HJ + j, 0:n, :]
        prompt_v[j, 0:n, :] = old - learn_rate * (
            new_first / fix_first / (jnp.sqrt(new_second / fix_second) + adam_eps)
            + weight_decay * old
        )


def hand_on_kernel(*refs):
    n = (len(refs) - 1) // 2
    sources, targets, sem = refs[:n], refs[n : 2 * n], refs[2 * n]
    copies = []
    for src, dst in zip(sources, targets):
        if len(src.shape) == 2:
            copies.append(pltpu.make_async_copy(src, dst, sem.at[len(copies)]))
        else:
            rows = dst.shape[0]
            for j in range(src.shape[0]):
                view = dst.at[:, :, 128 * j : 128 * (j + 1)]
                copies.append(
                    pltpu.make_async_copy(src.at[j, 0:rows], view, sem.at[len(copies)])
                )
    for copy in copies:
        copy.start()
    for copy in copies:
        copy.wait()


def hand_on(arrays, counts):
    def whole(a, rows):
        shape = a.shape if len(a.shape) == 2 else (rows, a.shape[2], a.shape[0] * a.shape[3])
        return jax.ShapeDtypeStruct(shape, a.dtype)

    copies = sum(1 if len(a.shape) == 2 else a.shape[0] for a in arrays)
    return pl.pallas_call(
        hand_on_kernel,
        out_shape=tuple(whole(a, rows) for a, rows in zip(arrays, counts)),
        in_specs=[pl.BlockSpec(memory_space=VMEM)] * len(arrays),
        out_specs=(pl.BlockSpec(memory_space=pl.ANY),) * len(arrays),
        scratch_shapes=[DMA((copies,))],
        compiler_params=pltpu.CompilerParams(vmem_limit_bytes=2**20),
    )(*arrays)


def native(x):
    return x.transpose(1, 0, 2)


def local(
    ndp, tokens, cotangent, prompts, first_moment, second_moment, norm_params, bias_rows,
    qkv_weight, out_weight, up_weight, up_bias, down_weight,
):
    B, T, D = tokens.shape
    L, PN, _ = prompts.shape
    FH = down_weight.shape[1]
    TK = up_to(T, 8)
    PP = up_to(PN, 8)
    S = up_to(TK + PP, 128)
    TQ = up_to(T, 16)
    G = 4
    R = ndp // G
    NJ, HJ, PB = D // 128, D // 256, 16
    dims = (B, T, D, L, PN, TK, PP, S, TQ, FH, G, R)
    H = HEADS
    n_local = 2 * NJ + 3 * HJ + 3
    scratch = [
        VMEM((NJ, TK, B, 128), BF16),
        VMEM((NJ, PP, L, 128), F32),
        VMEM((L, 4, D), F32),
        VMEM((L, 4, D), F32),
        VMEM((L, D, 3 * D), BF16),
        VMEM((L, D, D), BF16),
        VMEM((L, 2, D, FH), BF16),
        VMEM((2, L, FH), F32),
        VMEM((L, 2, FH, D), BF16),
        VMEM((B, S, D), F32),
        VMEM((B * TQ, D), F32),
        VMEM((B * TQ, D), F32),
        VMEM((B * S, 3 * D), BF16),
        VMEM((B * TQ, D), BF16),
        VMEM((L, B * S, D), BF16),
        VMEM((L, B * TK, D), BF16),
        VMEM((L, B * S, 2), F32),
        VMEM((L, B * TQ, D), BF16),
        VMEM((L, B * S, D), BF16),
        VMEM((L, B * S, D), BF16),
        VMEM((L, B, H, TQ, S), BF16),
        VMEM((L, B * TQ, D), BF16),
        VMEM((L, B * TQ, D), BF16),
        VMEM((L, B * TK, 2 * FH), BF16),
        VMEM((L, 2 * G, HJ, PB, 128), BF16),
        VMEM((L, 2 * G, HJ, PB, 128), BF16),
        VMEM((L, R, HJ, PB, 128), BF16),
        VMEM((L, G, HJ, PB, 128), BF16),
        VMEM((L, PB, 128), F32),
        VMEM((L, G, PB, 128), F32),
        DMA((n_local,)),
        DMA((L, 4)),
        DMA((2, HJ + 1)),
        DMA((L, 2, 2)),
        DMA((L, 2)),
        DMA((L, 2)),
        DMA((L, 2)),
        DMA((L, 2)),
    ]
    any_spec = pl.BlockSpec(memory_space=pl.ANY)
    small = VMEM((HJ, PP, L, 128), F32)
    results = pl.pallas_call(
        functools.partial(main_kernel, dims),
        out_shape=(
            VMEM((NJ, TK, B, 128), BF16),
            VMEM((NJ, TK, B, 128), F32),
            small,
            VMEM((1, 1), F32),
            small,
            small,
            small,
        ),
        in_specs=[any_spec] * 12,
        scratch_shapes=scratch,
        compiler_params=pltpu.CompilerParams(
            collective_id=0, has_side_effects=True, vmem_limit_bytes=61 * 2**20
        ),
    )(
        native(tokens), native(cotangent), native(prompts), native(first_moment),
        native(second_moment), norm_params, bias_rows, qkv_weight, out_weight,
        up_weight, up_bias, down_weight,
    )
    act, igrad, grad, norm, new_first, new_second, new_prompts = hand_on(
        results, (T, T, PN, 1, PN, PN, PN)
    )
    return (
        native(act), native(igrad), native(grad), norm.reshape(()),
        native(new_first), native(new_second), native(new_prompts),
    )


def solution(mesh):
    ndp = mesh.shape["dp"]
    return jax.shard_map(
        functools.partial(local, ndp),
        mesh=mesh,
        in_specs=(
            P(("dp", "mlp"), None, None),
            P(("dp", "mlp"), None, None),
            P(None, None, "mlp"),
            P(None, None, "mlp"),
            P(None, None, "mlp"),
            P(),
            P(),
            P(),
            P(),
            P(None, None, "mlp"),
            P(None, "mlp"),
            P(None, "mlp", None),
        ),
        out_specs=(
            P(("dp", "mlp"), None, None),
            P(("dp", "mlp"), None, None),
            P(None, None, "mlp"),
            P(),
            P(None, None, "mlp"),
            P(None, None, "mlp"),
            P(None, None, "mlp"),
        ),
        check_vma=False,
    )
```

```python
import functools

import jax
import jax.numpy as jnp
from jax import lax
from jax.experimental import pallas as pl
from jax.experimental.pallas import tpu as pltpu
from jax.sharding import PartitionSpec as P

HEADS = 12
STEP = 10
MESH = pl.DeviceIdType.MESH
VMEM = pltpu.VMEM
DMA = pltpu.SemaphoreType.DMA
BF16 = jnp.bfloat16
F32 = jnp.float32

norm_eps = 1e-06
clip_limit = 1.0
beta_one = 0.9
beta_two = 0.999
learn_rate = 1.5
weight_decay = 0.05
adam_eps = 1e-08
LOG2E = 1.4426950408889634


def up_to(value, step):
    return -(-value // step) * step


def mm(left, right):
    return jnp.dot(left, right, preferred_element_type=F32)


def mm_nt(left, right):
    return lax.dot_general(left, right, (((1,), (1,)), ((), ())), preferred_element_type=F32)


def mm_tn(left, right):
    return lax.dot_general(left, right, (((0,), (0,)), ((), ())), preferred_element_type=F32)


def rows_loop(count, step, body, unroll=1):
    def one(i, carry):
        body(pl.multiple_of(i * step, step))
        return carry

    lax.fori_loop(0, count // step, one, 0, unroll=unroll)


def square_of(block):
    block = block.astype(F32)
    total = block[0] * block[0]
    for j in range(1, block.shape[0]):
        total += block[j] * block[j]
    return total


def main_kernel(
    dims,
    tok_hbm,
    cot_hbm,
    prompts_hbm,
    first_hbm,
    second_hbm,
    norms_hbm,
    bias_hbm,
    qkv_hbm,
    out_hbm,
    up_hbm,
    ub_hbm,
    dn_hbm,
    tok_nat,
    stage_nat,
    sums_out,
    squares_out,
    first_nat,
    second_nat,
    prompt_nat,
    cot_nat,
    prom_nat,
    norms,
    bias,
    w_qkv,
    w_out,
    w_up,
    ub,
    w_dn,
    seq,
    hid,
    acc,
    wide,
    x16,
    xh1,
    xh2,
    inv_s,
    q_s,
    k_s,
    v_s,
    e_s,
    ri_s,
    o_s,
    gp_s,
    part_h,
    slot_b,
    slot_c,
    fin,
    sq_out,
    sq_in,
    local_sem,
    weight_sem,
    push_sem,
    push_w_sem,
    sem_b,
    sem_c,
    sem_d,
    sem_e,
):
    B, T, D, L, PN, TK, PP, S, TQ, FH, G, R = dims
    H = HEADS
    HD = D // H
    C = 768
    NJ = D // 128
    HJ = NJ // 2
    PB = 16
    M = B * TK
    core = lax.axis_index("mlp")
    other = 1 - core
    me = lax.axis_index("dp")
    g, r = lax.rem(me, G), me // G
    half = D // 2

    def member(k):
        return lax.rem(g + k, G)

    def rank(k):
        return lax.rem(r + k, R)

    around = [(k, c) for k in range(G) for c in range(2)][1:]

    def neighbour(k, c):
        return {"dp": r * G + member(k), "mlp": lax.rem(core + c, 2)}

    def columns(j):
        return slice(128 * j, 128 * (j + 1))

    def local(i, src, dst):
        return pltpu.make_async_copy(src, dst, local_sem.at[i])

    def copy_tok(j):
        return local(j, tok_hbm.at[:, :, columns(j)], tok_nat.at[j, 0:T])

    def copy_cot(j):
        return local(NJ + j, cot_hbm.at[:, :, columns(j)], cot_nat.at[j, 0:T])

    def copy_prom(j):
        return local(
            2 * NJ + j, prompts_hbm.at[:, :, columns(j)], prom_nat.at[core * HJ + j, 0:PN]
        )

    def copy_moment(i, j):
        src = (first_hbm, second_hbm)[i]
        return local(
            2 * NJ + (i + 1) * HJ + j, src.at[:, :, columns(j)], (first_nat, second_nat)[i].at[j, 0:PN]
        )

    def copy_small(i):
        src, dst = ((norms_hbm, norms), (bias_hbm, bias), (ub_hbm, ub.at[0]))[i]
        return local(2 * NJ + 3 * HJ + i, src, dst)

    def copy_weight(l, i):
        src, dst = (
            (qkv_hbm.at[l], w_qkv.at[l]),
            (out_hbm.at[l], w_out.at[l]),
            (up_hbm.at[l], w_up.at[l, 0]),
            (dn_hbm.at[l], w_dn.at[l, 0]),
        )[i]
        return pltpu.make_async_copy(src, dst, weight_sem.at[l, i])

    def push(src, dst, send_at, recv_at):
        return pltpu.make_async_remote_copy(
            src_ref=src,
            dst_ref=dst,
            send_sem=send_at,
            recv_sem=recv_at,
            device_id={"mlp": other},
            device_id_type=MESH,
        )

    def push_prom(j):
        return push(
            prompts_hbm.at[:, :, columns(j)],
            prom_nat.at[core * HJ + j, 0:PN],
            push_sem.at[0, j],
            push_sem.at[1, j],
        )

    def push_ub():
        return push(ub_hbm, ub.at[1], push_sem.at[0, HJ], push_sem.at[1, HJ])

    def push_weight(l, i):
        src, dst = ((up_hbm.at[l], w_up.at[l, 1]), (dn_hbm.at[l], w_dn.at[l, 1]))[i]
        return push(src, dst, push_w_sem.at[l, 0, i], push_w_sem.at[l, 1, i])

    copy_weight(0, 0).start()
    barrier = pltpu.get_barrier_semaphore()
    for k, c in around:
        pl.semaphore_signal(barrier, inc=1, device_id=neighbour(k, c), device_id_type=MESH)

    def greet(k, carry):
        pl.semaphore_signal(
            barrier, inc=1, device_id={"dp": rank(k) * G + g}, device_id_type=MESH
        )
        return carry

    lax.fori_loop(1, R, greet, 0)
    for j in range(NJ):
        copy_tok(j).start()
    for j in range(HJ):
        copy_prom(j).start()
    copy_small(0).start()
    copy_small(1).start()
    pl.semaphore_wait(barrier, len(around) + R - 1)
    for j in range(HJ):
        push_prom(j).start()
    push_ub().start()
    push_weight(0, 0).start()
    push_weight(0, 1).start()

    tok_v = tok_nat.reshape(NJ, TK * B, 128)
    cot_v = cot_nat.reshape(NJ, TK * B, 128)
    stage_v = stage_nat.reshape(NJ, TK * B, 128)
    prom_v = prom_nat.reshape(NJ, PP * L, 128)

    lane = lax.broadcasted_iota(jnp.int32, (1, S), 1)
    valid = (lane < T) | ((lane >= TK) & (lane < TK + PN))
    key_bias = jnp.where(valid, 0.0, -1e30).astype(F32)
    even_q = lax.broadcasted_iota(jnp.int32, (TQ, 2 * HD), 1) < HD
    even_k = lax.broadcasted_iota(jnp.int32, (S, 2 * HD), 1) < HD
    SH = S // 2
    even_h = lax.broadcasted_iota(jnp.int32, (SH, 2 * HD), 1) < HD
    low_lane = lax.broadcasted_iota(jnp.int32, (TQ, S), 1) < SH
    scale = HD**-0.5

    def spread(src_v, store):
        for j in range(NJ):
            stage_v[j] = src_v[j].astype(F32)
        for b in range(B):
            for j in range(NJ):
                store(b, slice(128 * j, 128 * (j + 1)), stage_v[j, pl.ds(b, T, stride=B), :])

    for b in range(B):
        seq[b, TK - 8 :, :] = jnp.zeros((S - TK + 8, D), F32)
    for j in range(NJ):
        copy_tok(j).wait()

    def store_tok(b, cols, rows):
        seq[b, 0:T, cols] = rows

    spread(tok_v, store_tok)
    copy_small(0).wait()
    copy_small(1).wait()
    for j in range(HJ):
        copy_prom(j).wait()
        push_prom(j).wait()

    def norm_rows(x):
        mean = jnp.mean(x, axis=-1, keepdims=True)
        centre = x - mean
        spread_ = jnp.mean(centre * centre, axis=-1, keepdims=True)
        inv = lax.rsqrt(spread_ + norm_eps)
        return centre * inv, inv

    def ln_back(dy, xh, inv, gain):
        gdy = dy * gain
        a = jnp.mean(gdy, axis=-1, keepdims=True)
        c = jnp.mean(gdy * xh, axis=-1, keepdims=True)
        return inv * (gdy - a - xh * c)

    def scores_at(n):
        place, n = (acc, n) if n < B * (D // S) else (hid, n - B * (D // S))
        rows, cols = n // (D // S) * TQ, n % (D // S) * S
        return place.at[rows : rows + TQ, cols : cols + S]

    def attend_forward(l):
        for b in range(B):
            qr = slice(b * TQ, (b + 1) * TQ)
            kr = slice(b * S, (b + 1) * S)
            for hp in range(H // 2):
                sl = slice(2 * HD * hp, 2 * HD * (hp + 1))
                q = q_s[l, qr, sl]
                k = k_s[l, kr, sl]
                zero = jnp.zeros_like(k)
                scores_at(2 * hp)[...] = mm_nt(q, jnp.where(even_k, k, zero))
                scores_at(2 * hp + 1)[...] = mm_nt(q, jnp.where(even_k, zero, k))
            for hp in range(H // 2):
                sl = slice(2 * HD * hp, 2 * HD * (hp + 1))
                v = v_s[l, kr, sl]
                sums = []
                for h in range(2):
                    here = even_k if h == 0 else jnp.logical_not(even_k)
                    s = scores_at(2 * hp + h)[...] + key_bias
                    top = jnp.max(s, axis=1, keepdims=True)
                    e = jnp.exp2((s - top) * (LOG2E * scale)).astype(BF16)
                    e_s[l, b, hp * 2 + h] = e
                    sums.append(mm(e, jnp.where(here, v, jnp.ones_like(v))))
                top_part = jnp.where(even_q, sums[0], sums[1])
                total = jnp.where(even_q, sums[1], sums[0])
                inv = pltpu.roll(1.0 / total, HD, 1)
                ri_s[l, qr, sl] = inv.astype(BF16)
                o_s[l, qr, sl] = (top_part * inv).astype(BF16)

    def back_half(l, b, hp, part, first):
        at = pl.multiple_of(hp * 2 * HD, 2 * HD)
        sl = pl.ds(at, 2 * HD)
        qr = pl.ds(pl.multiple_of(b * TQ, 16), TQ)
        kr = pl.ds(pl.multiple_of(b * S + part * SH, 16), SH)
        v = v_s[l, kr, sl]
        spare = pl.ds(pl.multiple_of((b * (H // 2) + hp) * S, 128), TQ)
        if first:
            do = x16[qr, sl].astype(F32) * ri_s[l, qr, sl].astype(F32)
            prod = do * o_s[l, qr, sl].astype(F32)
            d0 = jnp.sum(jnp.where(even_q, prod, 0.0), axis=1, keepdims=True)
            d1 = jnp.sum(jnp.where(even_q, 0.0, prod), axis=1, keepdims=True)
            do16 = do.astype(BF16)
            q_t = q_s[l, qr, sl].T
            do_t = do16.T
            x16[qr, sl] = do16
            gp_s[l, 0 : 2 * HD, spare] = q_t
            gp_s[l, 2 * HD : 4 * HD, spare] = do_t
            acc[qr, sl] = jnp.where(even_q, d0, d1)
        else:
            do16 = x16[qr, sl]
            q_t = gp_s[l, 0 : 2 * HD, spare]
            do_t = gp_s[l, 2 * HD : 4 * HD, spare]
            both = acc[qr, sl]
            d0, d1 = both[:, 0:1], both[:, HD : HD + 1]
        zero = jnp.zeros_like(v)
        stacked = jnp.concatenate([jnp.where(even_h, v, zero), jnp.where(even_h, zero, v)], axis=0)
        dp = mm_nt(do16, stacked)
        keys = slice(part * SH, (part + 1) * SH)
        e = jnp.concatenate([e_s[l, b, hp * 2, :, keys], e_s[l, b, hp * 2 + 1, :, keys]], axis=1)
        ds = (e.astype(F32) * (dp - jnp.where(low_lane, d0, d1))).astype(BF16)
        dk = mm(q_t, ds)
        dv = mm(do_t, e)
        dk = jnp.concatenate([dk[:HD, :SH], dk[HD:, SH:]], axis=0) * scale
        dv = jnp.concatenate([dv[:HD, :SH], dv[HD:, SH:]], axis=0)
        wide[kr, pl.ds(pl.multiple_of(D + at, 128), 2 * HD)] = dk.astype(BF16).T
        wide[kr, pl.ds(pl.multiple_of(2 * D + at, 128), 2 * HD)] = dv.astype(BF16).T
        return ds

    def back_queries(l, b, hp, low, high):
        at = pl.multiple_of(hp * 2 * HD, 2 * HD)
        sl = pl.ds(at, 2 * HD)
        kr = pl.ds(pl.multiple_of(b * S, 16), S)
        k = k_s[l, kr, sl]
        zero = jnp.zeros_like(k)
        dq = mm(jnp.concatenate([low[:, :SH], high[0]], axis=1), jnp.where(even_k, k, zero))
        dq += mm(jnp.concatenate([low[:, SH:], high[1]], axis=1), jnp.where(even_k, zero, k))
        wide[pl.ds(pl.multiple_of(b * S, 16), TQ), sl] = (dq * scale).astype(BF16)

    def pairs_loop(body, lo, hi):
        def one(i, carry):
            body(i // (H // 2), i % (H // 2))
            return carry

        lax.fori_loop(lo, hi, one, 0, unroll=True)

    pairs = B * H // 2

    def send(src, dst, sems, l, device):
        return pltpu.make_async_remote_copy(
            src_ref=src,
            dst_ref=dst,
            send_sem=sems.at[l, 0],
            recv_sem=sems.at[l, 1],
            device_id=device,
            device_id_type=MESH,
        )

    def all_of(slots, l, count, sems):
        view = slots.at[l, 0:count]
        return send(view, view, sems, l, {"mlp": other})

    mine_b = core * G + g

    def reduce_start(l, grad):
        rows = jnp.concatenate([grad, jnp.zeros((G * PB - grad.shape[0], D), F32)], axis=0)
        for j in range(NJ):
            for k in range(G):
                block = rows[k * PB : (k + 1) * PB, 128 * j : 128 * (j + 1)]
                part_h[l, j // HJ * G + k, j % HJ] = block.astype(BF16)
        for k, c in around:
            to = lax.rem(core + c, 2) * G + member(k)
            send(
                part_h.at[l, to], slot_b.at[l, mine_b], sem_b, l, neighbour(k, c)
            ).start()
        slot_b[l, mine_b] = part_h[l, mine_b]

    def reduce_group(l):
        all_of(slot_b, l, 2 * G - 1, sem_b).wait_recv()
        total = slot_b[l, 0].astype(F32)
        for i in range(1, 2 * G):
            total = total + slot_b[l, i].astype(F32)
        slot_c[l, r] = total.astype(BF16)

        def go(k, carry):
            peer = {"dp": rank(k) * G + g}
            send(slot_c.at[l, r], slot_c.at[l, r], sem_c, l, peer).start()
            return carry

        lax.fori_loop(1, R, go, 0, unroll=R <= 4)
        all_of(part_h, l, 2 * G - 1, sem_b).wait_send()

    def reduce_ranks(l):
        if R > 1:
            all_of(slot_c, l, R - 1, sem_c).wait_recv()

        def add(k, total):
            return total + slot_c[l, k].astype(F32)

        total = lax.fori_loop(0, R, add, jnp.zeros((HJ, PB, 128), F32), unroll=R <= 4)
        fin[l, g] = total.astype(BF16)
        for k in range(1, G):
            peer = {"dp": r * G + member(k)}
            send(fin.at[l, g], fin.at[l, g], sem_d, l, peer).start()
        sq_out[l] = square_of(fin[l, g])
        for k in range(G):
            send(sq_out.at[l], sq_in.at[l, g], sem_e, l, neighbour(k, 1)).start()
        if R > 1:
            all_of(slot_c, l, R - 1, sem_c).wait_send()

    def reduce_end(l):
        all_of(fin, l, G - 1, sem_d).wait()
        all_of(sq_in, l, G, sem_e).wait()

    def mlp_chunk(l, part, j, last_):
        cols = slice(j * C, (j + 1) * C)
        at = slice((part * (FH // C) + j) * C, (part * (FH // C) + j + 1) * C)
        pre = mm(x16[0:M, :], w_up[l, part, :, cols]) + ub[part, pl.ds(l, 1), cols]
        cdf = 0.5 + 0.5 * lax.erf(pre * 0.7071067811865476)
        if last_ != "output":
            bell = jnp.exp2(pre * pre * (-0.5 * LOG2E)) * 0.3989422804014327
            gp_s[l, :, at] = (cdf + pre * bell).astype(BF16)
        if last_ != "slope":
            add = mm((pre * cdf).astype(BF16), w_dn[l, part, cols, :])
            if part == 0 and j == 0:
                acc[0:M, :] = add
            else:
                acc[0:M, :] += add

    chunks = [(part, j) for part in range(2) for j in range(FH // C)]

    def norm_one(l):
        for b in range(B):
            for j in range(NJ):
                seq[b, TK : TK + PN, columns(j)] = prom_v[j, pl.ds(l, PN, stride=L), :]
        gain, shift = norms[l, 0:1, :], norms[l, 1:2, :]
        for b in range(B):
            xh, inv = norm_rows(seq[b])
            at = slice(b * S, (b + 1) * S)
            xh1[l, at, :] = xh.astype(BF16)
            inv_s[l, at, 0:1] = inv
            wide[at, 0:D] = (xh * gain + shift).astype(BF16)

    def attend(l):
        lhs = jnp.concatenate([wide[b * S : b * S + TQ, 0:D] for b in range(B)], axis=0)
        q_s[l] = (mm(lhs, w_qkv[l, :, 0:D]) + bias[l, 0:1, :]).astype(BF16)
        k_s[l] = mm(wide[:, 0:D], w_qkv[l, :, D : 2 * D]).astype(BF16)
        v_s[l] = (mm(wide[:, 0:D], w_qkv[l, :, 2 * D : 3 * D]) + bias[l, 1:2, :]).astype(BF16)
        attend_forward(l)

    def norm_two(l):
        branch = mm(o_s[l], w_out[l]) + bias[l, 2:3, :]
        for b in range(B):
            hid[b * TK : (b + 1) * TK, :] = seq[b, 0:TK, :] + branch[b * TQ : b * TQ + TK]
        gain2, shift2 = norms[l, 2:3, :], norms[l, 3:4, :]
        xh, inv = norm_rows(hid[0:M, :])
        xh2[l] = xh.astype(BF16)
        inv_s[l, 0:M, 1:2] = inv
        x16[0:M, :] = (xh * gain2 + shift2).astype(BF16)

    norm_one(0)
    copy_weight(0, 0).wait()
    copy_small(2).start()
    for i in range(1, 4):
        copy_weight(0, i).start()

    def forward(l, carry):
        attend(l)
        for i in range(1, 4):
            copy_weight(l, i).wait()

        @pl.when(l == 0)
        def _():
            for later in range(1, L):
                for i in range(2):
                    push_weight(later, i).start()
                for i in range(4):
                    copy_weight(later, i).start()
            for j in range(NJ):
                copy_cot(j).start()
            copy_small(2).wait()
            push_ub().wait()

        @pl.when(l < L - 1)
        def _():
            norm_two(l)
            for part, j in chunks:
                if part == 1 and j == 0:
                    push_weight(l, 0).wait()
                    push_weight(l, 1).wait()
                mlp_chunk(l, part, j, "both")
            for b in range(B):
                at = slice(b * TK, (b + 1) * TK)
                seq[b, 0:TK, :] = hid[at, :] + acc[at, :] + bias[l, 3:4, :]
            norm_one(l + 1)
            copy_weight(l + 1, 0).wait()

        return carry

    lax.fori_loop(0, L, forward, 0)
    push_weight(L - 1, 0).wait()
    push_weight(L - 1, 1).wait()
    for j in range(NJ):
        copy_cot(j).wait()
    norm_two(L - 1)
    for part, j in chunks:
        mlp_chunk(L - 1, part, j, "slope")
    for b in range(B):
        seq[b, 0:TK, :] = hid[b * TK : (b + 1) * TK, :] + bias[L - 1, 3:4, :]

    def activations_out():
        for b in range(B):
            seq[b, 0:TK, :] += acc[b * TK : (b + 1) * TK, :]
            for j in range(NJ):
                stage_v[j, pl.ds(b, T, stride=B), :] = seq[b, 0:T, 128 * j : 128 * (j + 1)]
        for j in range(NJ):
            tok_v[j] = stage_v[j].astype(BF16)

    for b in range(B):
        hid[(b + 1) * TK - 8 : (b + 1) * TK, :] = jnp.zeros((8, D), F32)

    def store_cot(b, cols, rows):
        hid[b * TK : b * TK + T, cols] = rows

    spread(cot_v, store_cot)

    def backward(step, carry):
        l = L - 1 - step
        above = l + 1

        def sum_above(phase):
            pl.when(step > 0)(lambda: phase(above))

        sum_above(reduce_group)
        x16[0:M, :] = hid[0:M, :].astype(BF16)
        for part in range(2):
            for j in range(FH // C):
                cols = slice(j * C, (j + 1) * C)
                at = slice((part * (FH // C) + j) * C, (part * (FH // C) + j + 1) * C)
                ga = mm_nt(x16[0:M, :], w_dn[l, part, cols, :])
                gpre = (gp_s[l, :, at].astype(F32) * ga).astype(BF16)
                add = mm_nt(gpre, w_up[l, part, :, cols])
                if part == 0 and j == 0:
                    acc[0:M, :] = add
                else:
                    acc[0:M, :] += add
        gain2 = norms[l, 2:3, :]

        new = hid[0:M, :] + ln_back(
            acc[0:M, :], xh2[l].astype(F32), inv_s[l, 0:M, 1:2], gain2
        )
        hid[0:M, :] = new
        grad_mixed = mm_nt(new.astype(BF16), w_out[l])
        for b in range(B):
            rows = [grad_mixed[b * TK : (b + 1) * TK], jnp.zeros((TQ - TK, D), F32)]
            x16[b * TQ : (b + 1) * TQ, :] = jnp.concatenate(rows, axis=0).astype(BF16)
        gain = norms[l, 0:1, :]

        def high_keys(b, hp):
            ds = back_half(l, b, hp, 1, True)
            e_s[l, b, hp * 2, :, SH:] = ds[:, :SH]
            e_s[l, b, hp * 2 + 1, :, SH:] = ds[:, SH:]

        def low_keys(b, hp):
            ds = back_half(l, b, hp, 0, False)
            back_queries(
                l, b, hp, ds, (e_s[l, b, hp * 2, :, SH:], e_s[l, b, hp * 2 + 1, :, SH:])
            )

        def prompt_gradient():
            base = TK // 16 * 16
            lhs = jnp.concatenate(
                [wide[b * S + base : (b + 1) * S, D : 3 * D] for b in range(B)], axis=0
            )
            full = mm_nt(lhs, w_qkv[l, :, D : 3 * D])
            n = S - base
            dprom = full[TK - base : n]
            for b in range(1, B):
                dprom = dprom + full[b * n + TK - base : (b + 1) * n]
            xh_p = xh1[l, base:S, :].astype(F32)[TK - base :]
            return ln_back(dprom, xh_p, inv_s[l, TK:S, 0:1], gain)

        pairs_loop(high_keys, 0, pairs)
        reduce_start(l, prompt_gradient())
        sum_above(reduce_ranks)
        pairs_loop(low_keys, 0, pairs)
        lhs = jnp.concatenate([wide[b * S : b * S + TQ, :] for b in range(B)], axis=0)
        acc[...] = mm_nt(lhs, w_qkv[l])
        pl.when(l == 0)(lambda: reduce_group(l))
        sum_above(reduce_end)
        for b in range(B):
            at = slice(b * TK, (b + 1) * TK)
            dx = ln_back(
                acc[b * TQ : b * TQ + TK, :],
                xh1[l, b * S : b * S + TQ, :].astype(F32)[:TK],
                inv_s[l, b * S : b * S + TK, 0:1],
                gain,
            )
            hid[at, :] = hid[at, :] + dx
        return carry

    lax.fori_loop(0, L, backward, 0)
    for j in range(HJ):
        copy_moment(0, j).start()
        copy_moment(1, j).start()
    x16[0:M, :] = (xh2[L - 1].astype(F32) * norms[L - 1, 2:3, :] + norms[L - 1, 3:4, :]).astype(BF16)
    for i, (part, j) in enumerate(chunks):
        if i == len(chunks) - 2:
            reduce_ranks(0)
        mlp_chunk(L - 1, part, j, "output")
    activations_out()
    for j in range(NJ):
        for b in range(B):
            stage_v[j, pl.ds(b, T, stride=B), :] = hid[
                b * TK : b * TK + T, 128 * j : 128 * (j + 1)
            ]
    for j in range(HJ):
        prompt_nat[j] = prom_nat[core * HJ + j]
        copy_moment(0, j).wait()
        copy_moment(1, j).wait()
    reduce_end(0)
    sums_out[...] = fin[...]
    squares_out[...] = sq_in[...]


def finish_kernel(
    act, igrad, sums, theirs, first, second, prompt,
    act_hbm, igrad_hbm, grad_hbm, norm_hbm, first_hbm, second_hbm, prompt_hbm,
    grad, norm, new_first, new_second, new_prompt, sem,
):
    leaving = []

    def leave(src, dst):
        copy = pltpu.make_async_copy(src, dst, sem.at[len(leaving)])
        copy.start()
        leaving.append(copy)

    def columns_out(src, dst, j):
        leave(src.at[j, 0 : dst.shape[0]], dst.at[:, :, 128 * j : 128 * (j + 1)])

    for src, dst in ((igrad, igrad_hbm), (act, act_hbm)):
        for j in range(src.shape[0]):
            columns_out(src, dst, j)
    L, G, HJ, PB, _ = sums.shape
    PP = grad.shape[1]
    n = grad_hbm.shape[0] * L
    flat = (HJ, PP * L, 128)
    grad_v = grad.reshape(*flat)
    for l in range(L):
        for k in range(G):
            rows = min(PB, n // L - k * PB)
            for j in range(HJ):
                grad_v[j, pl.ds(k * PB * L + l, rows, stride=L), :] = sums[l, k, j].astype(F32)[
                    :rows
                ]
    for j in range(HJ):
        columns_out(grad, grad_hbm, j)
    own_sum, other_sum = jnp.zeros((PB, 128), F32), jnp.zeros((PB, 128), F32)
    for l in range(L):
        for k in range(G):
            own_sum += square_of(sums[l, k])
            other_sum += theirs[l, k]
    grad_norm = jnp.sqrt(jnp.sum(own_sum + other_sum, axis=(0, 1), keepdims=True))
    norm[...] = grad_norm
    leave(norm, norm_hbm)
    factor = jnp.minimum(1.0, clip_limit / (grad_norm + 1e-06))
    fix_first = 1.0 - beta_one**STEP
    fix_second = 1.0 - beta_two**STEP
    for j in range(HJ):
        clipped = grad_v[j, 0:n, :] * factor
        up_first = beta_one * first.reshape(*flat)[j, 0:n, :] + (1.0 - beta_one) * clipped
        up_second = (
            beta_two * second.reshape(*flat)[j, 0:n, :] + (1.0 - beta_two) * clipped * clipped
        )
        new_first.reshape(*flat)[j, 0:n, :] = up_first
        new_second.reshape(*flat)[j, 0:n, :] = up_second
        old = prompt.reshape(*flat)[j, 0:n, :]
        new_prompt.reshape(*flat)[j, 0:n, :] = old - learn_rate * (
            up_first / fix_first / (jnp.sqrt(up_second / fix_second) + adam_eps)
            + weight_decay * old
        )
        columns_out(new_first, first_hbm, j)
        columns_out(new_second, second_hbm, j)
        columns_out(new_prompt, prompt_hbm, j)
    for copy in leaving:
        copy.wait()


def finish(arrays, T, PN):
    act, igrad, _, _, first, _, _ = arrays
    HJ, PP, L, _ = first.shape
    small = jax.ShapeDtypeStruct((PN, L, HJ * 128), F32)
    big = (T, act.shape[2], act.shape[0] * 128)
    return pl.pallas_call(
        finish_kernel,
        out_shape=(
            jax.ShapeDtypeStruct(big, act.dtype),
            jax.ShapeDtypeStruct(big, igrad.dtype),
            small,
            jax.ShapeDtypeStruct((1, 1), F32),
            small,
            small,
            small,
        ),
        in_specs=[pl.BlockSpec(memory_space=VMEM)] * len(arrays),
        out_specs=(pl.BlockSpec(memory_space=pl.ANY),) * 7,
        scratch_shapes=[
            VMEM(first.shape, F32),
            VMEM((1, 1), F32),
            VMEM(first.shape, F32),
            VMEM(first.shape, F32),
            VMEM(first.shape, F32),
            DMA((2 * act.shape[0] + 4 * HJ + 1,)),
        ],
        compiler_params=pltpu.CompilerParams(vmem_limit_bytes=2 * 2**20),
    )(*arrays)


def native(x):
    return x.transpose(1, 0, 2)


def local(
    ndp, tokens, cotangent, prompts, first_moment, second_moment, norm_params, bias_rows,
    qkv_weight, out_weight, up_weight, up_bias, down_weight,
):
    B, T, D = tokens.shape
    L, PN, _ = prompts.shape
    FH = down_weight.shape[1]
    TK = up_to(T, 8)
    PP = up_to(PN, 8)
    S = up_to(TK + PP, 128)
    TQ = up_to(T, 16)
    G = 4
    R = ndp // G
    NJ, HJ, PB = D // 128, D // 256, 16
    dims = (B, T, D, L, PN, TK, PP, S, TQ, FH, G, R)
    H = HEADS
    n_local = 2 * NJ + 3 * HJ + 3
    scratch = [
        VMEM((NJ, TK, B, 128), BF16),
        VMEM((NJ, PP, L, 128), F32),
        VMEM((L, 4, D), F32),
        VMEM((L, 4, D), F32),
        VMEM((L, D, 3 * D), BF16),
        VMEM((L, D, D), BF16),
        VMEM((L, 2, D, FH), BF16),
        VMEM((2, L, FH), F32),
        VMEM((L, 2, FH, D), BF16),
        VMEM((B, S, D), F32),
        VMEM((B * TQ, D), F32),
        VMEM((B * TQ, D), F32),
        VMEM((B * S, 3 * D), BF16),
        VMEM((B * TQ, D), BF16),
        VMEM((L, B * S, D), BF16),
        VMEM((L, B * TK, D), BF16),
        VMEM((L, B * S, 2), F32),
        VMEM((L, B * TQ, D), BF16),
        VMEM((L, B * S, D), BF16),
        VMEM((L, B * S, D), BF16),
        VMEM((L, B, H, TQ, S), BF16),
        VMEM((L, B * TQ, D), BF16),
        VMEM((L, B * TQ, D), BF16),
        VMEM((L, B * TK, 2 * FH), BF16),
        VMEM((L, 2 * G, HJ, PB, 128), BF16),
        VMEM((L, 2 * G, HJ, PB, 128), BF16),
        VMEM((L, R, HJ, PB, 128), BF16),
        VMEM((L, G, HJ, PB, 128), BF16),
        VMEM((L, PB, 128), F32),
        VMEM((L, G, PB, 128), F32),
        DMA((n_local,)),
        DMA((L, 4)),
        DMA((2, HJ + 1)),
        DMA((L, 2, 2)),
        DMA((L, 2)),
        DMA((L, 2)),
        DMA((L, 2)),
        DMA((L, 2)),
    ]
    any_spec = pl.BlockSpec(memory_space=pl.ANY)
    small = VMEM((HJ, PP, L, 128), F32)
    results = pl.pallas_call(
        functools.partial(main_kernel, dims),
        out_shape=(
            VMEM((NJ, TK, B, 128), BF16),
            VMEM((NJ, TK, B, 128), F32),
            VMEM((L, G, HJ, PB, 128), BF16),
            VMEM((L, G, PB, 128), F32),
            small,
            small,
            small,
        ),
        in_specs=[any_spec] * 12,
        scratch_shapes=scratch,
        compiler_params=pltpu.CompilerParams(
            collective_id=0, has_side_effects=True, vmem_limit_bytes=61 * 2**20
        ),
    )(
        native(tokens), native(cotangent), native(prompts), native(first_moment),
        native(second_moment), norm_params, bias_rows, qkv_weight, out_weight,
        up_weight, up_bias, down_weight,
    )
    act, igrad, grad, norm, new_first, new_second, new_prompts = finish(results, T, PN)
    return (
        native(act), native(igrad), native(grad), norm.reshape(()),
        native(new_first), native(new_second), native(new_prompts),
    )


def solution(mesh):
    ndp = mesh.shape["dp"]
    return jax.shard_map(
        functools.partial(local, ndp),
        mesh=mesh,
        in_specs=(
            P(("dp", "mlp"), None, None),
            P(("dp", "mlp"), None, None),
            P(None, None, "mlp"),
            P(None, None, "mlp"),
            P(None, None, "mlp"),
            P(),
            P(),
            P(),
            P(),
            P(None, None, "mlp"),
            P(None, "mlp"),
            P(None, "mlp", None),
        ),
        out_specs=(
            P(("dp", "mlp"), None, None),
            P(("dp", "mlp"), None, None),
            P(None, None, "mlp"),
            P(),
            P(None, None, "mlp"),
            P(None, None, "mlp"),
            P(None, None, "mlp"),
        ),
        check_vma=False,
    )
```

```python
import functools

import jax
import jax.numpy as jnp
from jax import lax
from jax.experimental import pallas as pl
from jax.experimental.pallas import tpu as pltpu
from jax.sharding import PartitionSpec as P

HEADS = 12
STEP = 10
MESH = pl.DeviceIdType.MESH
VMEM = pltpu.VMEM
DMA = pltpu.SemaphoreType.DMA
BF16 = jnp.bfloat16
F32 = jnp.float32

norm_eps = 1e-06
clip_limit = 1.0
beta_one = 0.9
beta_two = 0.999
learn_rate = 1.5
weight_decay = 0.05
adam_eps = 1e-08
LOG2E = 1.4426950408889634


def up_to(value, step):
    return -(-value // step) * step


def mm(left, right):
    return jnp.dot(left, right, preferred_element_type=F32)


def mm_nt(left, right):
    return lax.dot_general(left, right, (((1,), (1,)), ((), ())), preferred_element_type=F32)


def mm_tn(left, right):
    return lax.dot_general(left, right, (((0,), (0,)), ((), ())), preferred_element_type=F32)


def rows_loop(count, step, body, unroll=1):
    def one(i, carry):
        body(pl.multiple_of(i * step, step))
        return carry

    lax.fori_loop(0, count // step, one, 0, unroll=unroll)


def square_of(block):
    block = block.astype(F32)
    total = block[0] * block[0]
    for j in range(1, block.shape[0]):
        total += block[j] * block[j]
    return total


def main_kernel(
    dims,
    tok_hbm,
    cot_hbm,
    prompts_hbm,
    first_hbm,
    second_hbm,
    norms_hbm,
    bias_hbm,
    qkv_hbm,
    out_hbm,
    up_hbm,
    ub_hbm,
    dn_hbm,
    tok_nat,
    stage_nat,
    sums_out,
    squares_out,
    first_nat,
    second_nat,
    prompt_nat,
    cot_nat,
    prom_nat,
    norms,
    bias,
    w_qkv,
    w_out,
    w_up,
    ub,
    w_dn,
    seq,
    hid,
    acc,
    wide,
    x16,
    xh1,
    xh2,
    inv_s,
    q_s,
    k_s,
    v_s,
    e_s,
    ri_s,
    o_s,
    gp_s,
    part_h,
    slot_b,
    slot_c,
    fin,
    sq_out,
    sq_in,
    local_sem,
    weight_sem,
    push_sem,
    push_w_sem,
    sem_b,
    sem_c,
    sem_d,
    sem_e,
):
    B, T, D, L, PN, TK, PP, S, TQ, FH, G, R = dims
    H = HEADS
    HD = D // H
    C = 768
    NJ = D // 128
    HJ = NJ // 2
    PB = 16
    M = B * TK
    core = lax.axis_index("mlp")
    other = 1 - core
    me = lax.axis_index("dp")
    g, r = lax.rem(me, G), me // G
    half = D // 2

    def member(k):
        return lax.rem(g + k, G)

    def rank(k):
        return lax.rem(r + k, R)

    around = [(k, c) for k in range(G) for c in range(2)][1:]

    def neighbour(k, c):
        return {"dp": r * G + member(k), "mlp": lax.rem(core + c, 2)}

    def columns(j):
        return slice(128 * j, 128 * (j + 1))

    def local(i, src, dst):
        return pltpu.make_async_copy(src, dst, local_sem.at[i])

    def copy_tok(j):
        return local(j, tok_hbm.at[:, :, columns(j)], tok_nat.at[j, 0:T])

    def copy_cot(j):
        return local(NJ + j, cot_hbm.at[:, :, columns(j)], cot_nat.at[j, 0:T])

    def copy_prom(j):
        return local(
            2 * NJ + j, prompts_hbm.at[:, :, columns(j)], prom_nat.at[core * HJ + j, 0:PN]
        )

    def copy_moment(i, j):
        src = (first_hbm, second_hbm)[i]
        return local(
            2 * NJ + (i + 1) * HJ + j, src.at[:, :, columns(j)], (first_nat, second_nat)[i].at[j, 0:PN]
        )

    def copy_small(i):
        src, dst = ((norms_hbm, norms), (bias_hbm, bias), (ub_hbm, ub.at[0]))[i]
        return local(2 * NJ + 3 * HJ + i, src, dst)

    def copy_weight(l, i):
        src, dst = (
            (qkv_hbm.at[l], w_qkv.at[l]),
            (out_hbm.at[l], w_out.at[l]),
            (up_hbm.at[l], w_up.at[l, 0]),
            (dn_hbm.at[l], w_dn.at[l, 0]),
        )[i]
        return pltpu.make_async_copy(src, dst, weight_sem.at[l, i])

    def push(src, dst, send_at, recv_at):
        return pltpu.make_async_remote_copy(
            src_ref=src,
            dst_ref=dst,
            send_sem=send_at,
            recv_sem=recv_at,
            device_id={"mlp": other},
            device_id_type=MESH,
        )

    def push_prom(j):
        return push(
            prompts_hbm.at[:, :, columns(j)],
            prom_nat.at[core * HJ + j, 0:PN],
            push_sem.at[0, j],
            push_sem.at[1, j],
        )

    def push_ub():
        return push(ub_hbm, ub.at[1], push_sem.at[0, HJ], push_sem.at[1, HJ])

    def push_weight(l, i):
        src, dst = ((up_hbm.at[l], w_up.at[l, 1]), (dn_hbm.at[l], w_dn.at[l, 1]))[i]
        return push(src, dst, push_w_sem.at[l, 0, i], push_w_sem.at[l, 1, i])

    copy_weight(0, 0).start()
    barrier = pltpu.get_barrier_semaphore()
    for k, c in around:
        pl.semaphore_signal(barrier, inc=1, device_id=neighbour(k, c), device_id_type=MESH)

    def greet(k, carry):
        pl.semaphore_signal(
            barrier, inc=1, device_id={"dp": rank(k) * G + g}, device_id_type=MESH
        )
        return carry

    lax.fori_loop(1, R, greet, 0)
    for j in range(NJ):
        copy_tok(j).start()
    for j in range(HJ):
        copy_prom(j).start()
    copy_small(0).start()
    copy_small(1).start()
    pl.semaphore_wait(barrier, len(around) + R - 1)
    for j in range(HJ):
        push_prom(j).start()
    push_ub().start()
    push_weight(0, 0).start()
    push_weight(0, 1).start()

    tok_v = tok_nat.reshape(NJ, TK * B, 128)
    cot_v = cot_nat.reshape(NJ, TK * B, 128)
    stage_v = stage_nat.reshape(NJ, TK * B, 128)
    prom_v = prom_nat.reshape(NJ, PP * L, 128)

    lane = lax.broadcasted_iota(jnp.int32, (1, S), 1)
    valid = (lane < T) | ((lane >= TK) & (lane < TK + PN))
    key_bias = jnp.where(valid, 0.0, -1e30).astype(F32)
    even_q = lax.broadcasted_iota(jnp.int32, (TQ, 2 * HD), 1) < HD
    even_k = lax.broadcasted_iota(jnp.int32, (S, 2 * HD), 1) < HD
    SH = S // 2
    even_h = lax.broadcasted_iota(jnp.int32, (SH, 2 * HD), 1) < HD
    low_lane = lax.broadcasted_iota(jnp.int32, (TQ, S), 1) < SH
    scale = HD**-0.5

    def spread(src_v, store):
        for j in range(NJ):
            stage_v[j] = src_v[j].astype(F32)
        for b in range(B):
            for j in range(NJ):
                store(b, slice(128 * j, 128 * (j + 1)), stage_v[j, pl.ds(b, T, stride=B), :])

    for b in range(B):
        seq[b, TK - 8 :, :] = jnp.zeros((S - TK + 8, D), F32)
    for j in range(NJ):
        copy_tok(j).wait()

    def store_tok(b, cols, rows):
        seq[b, 0:T, cols] = rows

    spread(tok_v, store_tok)
    copy_small(0).wait()
    copy_small(1).wait()
    for j in range(HJ):
        copy_prom(j).wait()
        push_prom(j).wait()

    def norm_rows(x):
        mean = jnp.mean(x, axis=-1, keepdims=True)
        centre = x - mean
        spread_ = jnp.mean(centre * centre, axis=-1, keepdims=True)
        inv = lax.rsqrt(spread_ + norm_eps)
        return centre * inv, inv

    def ln_back(dy, xh, inv, gain):
        gdy = dy * gain
        a = jnp.mean(gdy, axis=-1, keepdims=True)
        c = jnp.mean(gdy * xh, axis=-1, keepdims=True)
        return inv * (gdy - a - xh * c)

    def scores_at(n):
        place, n = (acc, n) if n < B * (D // S) else (hid, n - B * (D // S))
        rows, cols = n // (D // S) * TQ, n % (D // S) * S
        return place.at[rows : rows + TQ, cols : cols + S]

    def attend_forward(l):
        for b in range(B):
            qr = slice(b * TQ, (b + 1) * TQ)
            kr = slice(b * S, (b + 1) * S)
            for hp in range(H // 2):
                sl = slice(2 * HD * hp, 2 * HD * (hp + 1))
                q = q_s[l, qr, sl]
                k = k_s[l, kr, sl]
                zero = jnp.zeros_like(k)
                scores_at(2 * hp)[...] = mm_nt(q, jnp.where(even_k, k, zero))
                scores_at(2 * hp + 1)[...] = mm_nt(q, jnp.where(even_k, zero, k))
            for hp in range(H // 2):
                sl = slice(2 * HD * hp, 2 * HD * (hp + 1))
                v = v_s[l, kr, sl]
                sums = []
                for h in range(2):
                    here = even_k if h == 0 else jnp.logical_not(even_k)
                    s = scores_at(2 * hp + h)[...] + key_bias
                    top = jnp.max(s, axis=1, keepdims=True)
                    e = jnp.exp2((s - top) * (LOG2E * scale)).astype(BF16)
                    e_s[l, b, hp * 2 + h] = e
                    sums.append(mm(e, jnp.where(here, v, jnp.ones_like(v))))
                top_part = jnp.where(even_q, sums[0], sums[1])
                total = jnp.where(even_q, sums[1], sums[0])
                inv = pltpu.roll(1.0 / total, HD, 1)
                ri_s[l, qr, sl] = inv.astype(BF16)
                o_s[l, qr, sl] = (top_part * inv).astype(BF16)

    def back_half(l, b, hp, part, first):
        at = pl.multiple_of(hp * 2 * HD, 2 * HD)
        sl = pl.ds(at, 2 * HD)
        qr = pl.ds(pl.multiple_of(b * TQ, 16), TQ)
        kr = pl.ds(pl.multiple_of(b * S + part * SH, 16), SH)
        v = v_s[l, kr, sl]
        spare = pl.ds(pl.multiple_of((b * (H // 2) + hp) * S, 128), TQ)
        if first:
            do = x16[qr, sl].astype(F32) * ri_s[l, qr, sl].astype(F32)
            prod = do * o_s[l, qr, sl].astype(F32)
            d0 = jnp.sum(jnp.where(even_q, prod, 0.0), axis=1, keepdims=True)
            d1 = jnp.sum(jnp.where(even_q, 0.0, prod), axis=1, keepdims=True)
            do16 = do.astype(BF16)
            q_t = q_s[l, qr, sl].T
            do_t = do16.T
            x16[qr, sl] = do16
            gp_s[l, 0 : 2 * HD, spare] = q_t
            gp_s[l, 2 * HD : 4 * HD, spare] = do_t
            acc[qr, sl] = jnp.where(even_q, d0, d1)
        else:
            do16 = x16[qr, sl]
            q_t = gp_s[l, 0 : 2 * HD, spare]
            do_t = gp_s[l, 2 * HD : 4 * HD, spare]
            both = acc[qr, sl]
            d0, d1 = both[:, 0:1], both[:, HD : HD + 1]
        zero = jnp.zeros_like(v)
        stacked = jnp.concatenate([jnp.where(even_h, v, zero), jnp.where(even_h, zero, v)], axis=0)
        dp = mm_nt(do16, stacked)
        keys = slice(part * SH, (part + 1) * SH)
        e = jnp.concatenate([e_s[l, b, hp * 2, :, keys], e_s[l, b, hp * 2 + 1, :, keys]], axis=1)
        ds = (e.astype(F32) * (dp - jnp.where(low_lane, d0, d1))).astype(BF16)
        dk = mm(q_t, ds)
        dv = mm(do_t, e)
        dk = jnp.concatenate([dk[:HD, :SH], dk[HD:, SH:]], axis=0) * scale
        dv = jnp.concatenate([dv[:HD, :SH], dv[HD:, SH:]], axis=0)
        wide[kr, pl.ds(pl.multiple_of(D + at, 128), 2 * HD)] = dk.astype(BF16).T
        wide[kr, pl.ds(pl.multiple_of(2 * D + at, 128), 2 * HD)] = dv.astype(BF16).T
        return ds

    def back_queries(l, b, hp, low, high):
        at = pl.multiple_of(hp * 2 * HD, 2 * HD)
        sl = pl.ds(at, 2 * HD)
        kr = pl.ds(pl.multiple_of(b * S, 16), S)
        k = k_s[l, kr, sl]
        zero = jnp.zeros_like(k)
        both = jnp.concatenate([jnp.where(even_k, k, zero), jnp.where(even_k, zero, k)], axis=0)
        dq = mm(jnp.concatenate([low[:, :SH], high[0], low[:, SH:], high[1]], axis=1), both)
        wide[pl.ds(pl.multiple_of(b * S, 16), TQ), sl] = (dq * scale).astype(BF16)

    def pairs_loop(body, lo, hi):
        def one(i, carry):
            body(i // (H // 2), i % (H // 2))
            return carry

        lax.fori_loop(lo, hi, one, 0, unroll=True)

    pairs = B * H // 2

    def send(src, dst, sems, l, device):
        return pltpu.make_async_remote_copy(
            src_ref=src,
            dst_ref=dst,
            send_sem=sems.at[l, 0],
            recv_sem=sems.at[l, 1],
            device_id=device,
            device_id_type=MESH,
        )

    def all_of(slots, l, count, sems):
        view = slots.at[l, 0:count]
        return send(view, view, sems, l, {"mlp": other})

    mine_b = core * G + g

    def reduce_start(l, grad):
        rows = jnp.concatenate([grad, jnp.zeros((G * PB - grad.shape[0], D), F32)], axis=0)
        for j in range(NJ):
            for k in range(G):
                block = rows[k * PB : (k + 1) * PB, 128 * j : 128 * (j + 1)]
                part_h[l, j // HJ * G + k, j % HJ] = block.astype(BF16)
        for k, c in reversed(around):
            to = lax.rem(core + c, 2) * G + member(k)
            send(
                part_h.at[l, to], slot_b.at[l, mine_b], sem_b, l, neighbour(k, c)
            ).start()
        slot_b[l, mine_b] = part_h[l, mine_b]

    def reduce_group(l):
        all_of(slot_b, l, 2 * G - 1, sem_b).wait_recv()
        total = slot_b[l, 0].astype(F32)
        for i in range(1, 2 * G):
            total = total + slot_b[l, i].astype(F32)
        slot_c[l, r] = total.astype(BF16)

        def go(k, carry):
            peer = {"dp": rank(k) * G + g}
            send(slot_c.at[l, r], slot_c.at[l, r], sem_c, l, peer).start()
            return carry

        lax.fori_loop(1, R, go, 0, unroll=R <= 4)
        all_of(part_h, l, 2 * G - 1, sem_b).wait_send()

    def reduce_ranks(l):
        if R > 1:
            all_of(slot_c, l, R - 1, sem_c).wait_recv()

        def add(k, total):
            return total + slot_c[l, k].astype(F32)

        total = lax.fori_loop(0, R, add, jnp.zeros((HJ, PB, 128), F32), unroll=R <= 4)
        fin[l, g] = total.astype(BF16)
        for k in range(1, G):
            peer = {"dp": r * G + member(k)}
            send(fin.at[l, g], fin.at[l, g], sem_d, l, peer).start()
        sq_out[l] = square_of(fin[l, g])
        for k in range(G):
            send(sq_out.at[l], sq_in.at[l, g], sem_e, l, neighbour(k, 1)).start()
        if R > 1:
            all_of(slot_c, l, R - 1, sem_c).wait_send()

    def reduce_end(l):
        all_of(fin, l, G - 1, sem_d).wait()
        all_of(sq_in, l, G, sem_e).wait()

    def mlp_chunk(l, part, j, last_):
        cols = slice(j * C, (j + 1) * C)
        at = slice((part * (FH // C) + j) * C, (part * (FH // C) + j + 1) * C)
        pre = mm(x16[0:M, :], w_up[l, part, :, cols]) + ub[part, pl.ds(l, 1), cols]
        cdf = 0.5 + 0.5 * lax.erf(pre * 0.7071067811865476)
        if last_ != "output":
            bell = jnp.exp2(pre * pre * (-0.5 * LOG2E)) * 0.3989422804014327
            gp_s[l, :, at] = (cdf + pre * bell).astype(BF16)
        if last_ != "slope":
            add = mm((pre * cdf).astype(BF16), w_dn[l, part, cols, :])
            if part == 0 and j == 0:
                acc[0:M, :] = add
            else:
                acc[0:M, :] += add

    chunks = [(part, j) for part in range(2) for j in range(FH // C)]

    def norm_one(l):
        for b in range(B):
            for j in range(NJ):
                seq[b, TK : TK + PN, columns(j)] = prom_v[j, pl.ds(l, PN, stride=L), :]
        gain, shift = norms[l, 0:1, :], norms[l, 1:2, :]
        for b in range(B):
            xh, inv = norm_rows(seq[b])
            at = slice(b * S, (b + 1) * S)
            xh1[l, at, :] = xh.astype(BF16)
            inv_s[l, at, 0:1] = inv
            wide[at, 0:D] = (xh * gain + shift).astype(BF16)

    def attend(l):
        lhs = jnp.concatenate([wide[b * S : b * S + TQ, 0:D] for b in range(B)], axis=0)
        q_s[l] = (mm(lhs, w_qkv[l, :, 0:D]) + bias[l, 0:1, :]).astype(BF16)
        k_s[l] = mm(wide[:, 0:D], w_qkv[l, :, D : 2 * D]).astype(BF16)
        v_s[l] = (mm(wide[:, 0:D], w_qkv[l, :, 2 * D : 3 * D]) + bias[l, 1:2, :]).astype(BF16)
        attend_forward(l)

    def norm_two(l):
        branch = mm(o_s[l], w_out[l]) + bias[l, 2:3, :]
        for b in range(B):
            hid[b * TK : (b + 1) * TK, :] = seq[b, 0:TK, :] + branch[b * TQ : b * TQ + TK]
        gain2, shift2 = norms[l, 2:3, :], norms[l, 3:4, :]
        xh, inv = norm_rows(hid[0:M, :])
        xh2[l] = xh.astype(BF16)
        inv_s[l, 0:M, 1:2] = inv
        x16[0:M, :] = (xh * gain2 + shift2).astype(BF16)

    norm_one(0)
    copy_small(2).start()
    for i in range(1, 4):
        copy_weight(0, i).start()
    for j in range(NJ):
        copy_cot(j).start()
    copy_weight(0, 0).wait()

    def forward(l, carry):
        attend(l)
        for i in range(1, 4):
            copy_weight(l, i).wait()

        @pl.when(l == 0)
        def _():
            for later in range(1, L):
                for i in range(2):
                    push_weight(later, i).start()
                for i in range(4):
                    copy_weight(later, i).start()
            copy_small(2).wait()
            push_ub().wait()

        @pl.when(l < L - 1)
        def _():
            norm_two(l)
            for part, j in chunks:
                if part == 1 and j == 0:
                    push_weight(l, 0).wait()
                    push_weight(l, 1).wait()
                mlp_chunk(l, part, j, "both")
            for b in range(B):
                at = slice(b * TK, (b + 1) * TK)
                seq[b, 0:TK, :] = hid[at, :] + acc[at, :] + bias[l, 3:4, :]
            norm_one(l + 1)
            copy_weight(l + 1, 0).wait()

        return carry

    lax.fori_loop(0, L, forward, 0)
    push_weight(L - 1, 0).wait()
    push_weight(L - 1, 1).wait()
    for j in range(NJ):
        copy_cot(j).wait()
    norm_two(L - 1)
    for part, j in chunks:
        mlp_chunk(L - 1, part, j, "slope")
    for b in range(B):
        seq[b, 0:TK, :] = hid[b * TK : (b + 1) * TK, :] + bias[L - 1, 3:4, :]

    def activations_out():
        for b in range(B):
            seq[b, 0:TK, :] += acc[b * TK : (b + 1) * TK, :]
            for j in range(NJ):
                stage_v[j, pl.ds(b, T, stride=B), :] = seq[b, 0:T, 128 * j : 128 * (j + 1)]
        for j in range(NJ):
            tok_v[j] = stage_v[j].astype(BF16)

    for b in range(B):
        hid[(b + 1) * TK - 8 : (b + 1) * TK, :] = jnp.zeros((8, D), F32)

    def store_cot(b, cols, rows):
        hid[b * TK : b * TK + T, cols] = rows

    spread(cot_v, store_cot)

    def backward(step, carry):
        l = L - 1 - step
        above = l + 1

        def sum_above(phase):
            pl.when(step > 0)(lambda: phase(above))

        sum_above(reduce_group)
        x16[0:M, :] = hid[0:M, :].astype(BF16)
        for part in range(2):
            for j in range(FH // C):
                cols = slice(j * C, (j + 1) * C)
                at = slice((part * (FH // C) + j) * C, (part * (FH // C) + j + 1) * C)
                ga = mm_nt(x16[0:M, :], w_dn[l, part, cols, :])
                gpre = (gp_s[l, :, at].astype(F32) * ga).astype(BF16)
                add = mm_nt(gpre, w_up[l, part, :, cols])
                if part == 0 and j == 0:
                    acc[0:M, :] = add
                else:
                    acc[0:M, :] += add
        gain2 = norms[l, 2:3, :]

        new = hid[0:M, :] + ln_back(
            acc[0:M, :], xh2[l].astype(F32), inv_s[l, 0:M, 1:2], gain2
        )
        hid[0:M, :] = new
        grad_mixed = mm_nt(new.astype(BF16), w_out[l])
        for b in range(B):
            rows = [grad_mixed[b * TK : (b + 1) * TK], jnp.zeros((TQ - TK, D), F32)]
            x16[b * TQ : (b + 1) * TQ, :] = jnp.concatenate(rows, axis=0).astype(BF16)
        gain = norms[l, 0:1, :]

        def high_keys(b, hp):
            ds = back_half(l, b, hp, 1, True)
            e_s[l, b, hp * 2, :, SH:] = ds[:, :SH]
            e_s[l, b, hp * 2 + 1, :, SH:] = ds[:, SH:]

        def low_keys(b, hp):
            ds = back_half(l, b, hp, 0, False)
            back_queries(
                l, b, hp, ds, (e_s[l, b, hp * 2, :, SH:], e_s[l, b, hp * 2 + 1, :, SH:])
            )

        def prompt_gradient():
            base = TK // 16 * 16
            lhs = jnp.concatenate(
                [wide[b * S + base : (b + 1) * S, D : 3 * D] for b in range(B)], axis=0
            )
            full = mm_nt(lhs, w_qkv[l, :, D : 3 * D])
            n = S - base
            dprom = full[TK - base : n]
            for b in range(1, B):
                dprom = dprom + full[b * n + TK - base : (b + 1) * n]
            xh_p = xh1[l, base:S, :].astype(F32)[TK - base :]
            return ln_back(dprom, xh_p, inv_s[l, TK:S, 0:1], gain)

        pairs_loop(high_keys, 0, pairs)
        reduce_start(l, prompt_gradient())
        sum_above(reduce_ranks)
        pairs_loop(low_keys, 0, pairs)
        lhs = jnp.concatenate([wide[b * S : b * S + TQ, :] for b in range(B)], axis=0)
        acc[...] = mm_nt(lhs, w_qkv[l])
        pl.when(l == 0)(lambda: reduce_group(l))
        sum_above(reduce_end)
        for b in range(B):
            at = slice(b * TK, (b + 1) * TK)
            dx = ln_back(
                acc[b * TQ : b * TQ + TK, :],
                xh1[l, b * S : b * S + TQ, :].astype(F32)[:TK],
                inv_s[l, b * S : b * S + TK, 0:1],
                gain,
            )
            hid[at, :] = hid[at, :] + dx
        return carry

    lax.fori_loop(0, L, backward, 0)
    for j in range(HJ):
        copy_moment(0, j).start()
        copy_moment(1, j).start()
    x16[0:M, :] = (xh2[L - 1].astype(F32) * norms[L - 1, 2:3, :] + norms[L - 1, 3:4, :]).astype(BF16)
    for i, (part, j) in enumerate(chunks):
        if i == len(chunks) - 2:
            reduce_ranks(0)
        mlp_chunk(L - 1, part, j, "output")
    activations_out()
    for j in range(NJ):
        for b in range(B):
            stage_v[j, pl.ds(b, T, stride=B), :] = hid[
                b * TK : b * TK + T, 128 * j : 128 * (j + 1)
            ]
    for j in range(HJ):
        prompt_nat[j] = prom_nat[core * HJ + j]
        copy_moment(0, j).wait()
        copy_moment(1, j).wait()
    reduce_end(0)
    sums_out[...] = fin[...]
    squares_out[...] = sq_in[...]


def finish_kernel(
    act, igrad, sums, theirs, first, second, prompt,
    act_hbm, igrad_hbm, grad_hbm, norm_hbm, first_hbm, second_hbm, prompt_hbm,
    grad, norm, new_first, new_second, new_prompt, sem,
):
    leaving = []

    def leave(src, dst):
        copy = pltpu.make_async_copy(src, dst, sem.at[len(leaving)])
        copy.start()
        leaving.append(copy)

    def columns_out(src, dst, j):
        leave(src.at[j, 0 : dst.shape[0]], dst.at[:, :, 128 * j : 128 * (j + 1)])

    for src, dst in ((igrad, igrad_hbm), (act, act_hbm)):
        for j in range(src.shape[0]):
            columns_out(src, dst, j)
    L, G, HJ, PB, _ = sums.shape
    PP = grad.shape[1]
    n = grad_hbm.shape[0] * L
    flat = (HJ, PP * L, 128)
    grad_v = grad.reshape(*flat)
    for l in range(L):
        for k in range(G):
            rows = min(PB, n // L - k * PB)
            for j in range(HJ):
                grad_v[j, pl.ds(k * PB * L + l, rows, stride=L), :] = sums[l, k, j].astype(F32)[
                    :rows
                ]
    for j in range(HJ):
        columns_out(grad, grad_hbm, j)
    own_sum, other_sum = jnp.zeros((PB, 128), F32), jnp.zeros((PB, 128), F32)
    for l in range(L):
        for k in range(G):
            own_sum += square_of(sums[l, k])
            other_sum += theirs[l, k]
    grad_norm = jnp.sqrt(jnp.sum(own_sum + other_sum, axis=(0, 1), keepdims=True))
    norm[...] = grad_norm
    leave(norm, norm_hbm)
    factor = jnp.minimum(1.0, clip_limit / (grad_norm + 1e-06))
    fix_first = 1.0 - beta_one**STEP
    fix_second = 1.0 - beta_two**STEP
    for j in range(HJ):
        clipped = grad_v[j, 0:n, :] * factor
        up_first = beta_one * first.reshape(*flat)[j, 0:n, :] + (1.0 - beta_one) * clipped
        up_second = (
            beta_two * second.reshape(*flat)[j, 0:n, :] + (1.0 - beta_two) * clipped * clipped
        )
        new_first.reshape(*flat)[j, 0:n, :] = up_first
        new_second.reshape(*flat)[j, 0:n, :] = up_second
        old = prompt.reshape(*flat)[j, 0:n, :]
        new_prompt.reshape(*flat)[j, 0:n, :] = old - learn_rate * (
            up_first / fix_first / (jnp.sqrt(up_second / fix_second) + adam_eps)
            + weight_decay * old
        )
        columns_out(new_first, first_hbm, j)
        columns_out(new_second, second_hbm, j)
        columns_out(new_prompt, prompt_hbm, j)
    for copy in leaving:
        copy.wait()


def finish(arrays, T, PN):
    act, igrad, _, _, first, _, _ = arrays
    HJ, PP, L, _ = first.shape
    small = jax.ShapeDtypeStruct((PN, L, HJ * 128), F32)
    big = (T, act.shape[2], act.shape[0] * 128)
    return pl.pallas_call(
        finish_kernel,
        out_shape=(
            jax.ShapeDtypeStruct(big, act.dtype),
            jax.ShapeDtypeStruct(big, igrad.dtype),
            small,
            jax.ShapeDtypeStruct((1, 1), F32),
            small,
            small,
            small,
        ),
        in_specs=[pl.BlockSpec(memory_space=VMEM)] * len(arrays),
        out_specs=(pl.BlockSpec(memory_space=pl.ANY),) * 7,
        scratch_shapes=[
            VMEM(first.shape, F32),
            VMEM((1, 1), F32),
            VMEM(first.shape, F32),
            VMEM(first.shape, F32),
            VMEM(first.shape, F32),
            DMA((2 * act.shape[0] + 4 * HJ + 1,)),
        ],
        compiler_params=pltpu.CompilerParams(vmem_limit_bytes=2 * 2**20),
    )(*arrays)


def native(x):
    return x.transpose(1, 0, 2)


def local(
    ndp, tokens, cotangent, prompts, first_moment, second_moment, norm_params, bias_rows,
    qkv_weight, out_weight, up_weight, up_bias, down_weight,
):
    B, T, D = tokens.shape
    L, PN, _ = prompts.shape
    FH = down_weight.shape[1]
    TK = up_to(T, 8)
    PP = up_to(PN, 8)
    S = up_to(TK + PP, 128)
    TQ = up_to(T, 16)
    G = 4
    R = ndp // G
    NJ, HJ, PB = D // 128, D // 256, 16
    dims = (B, T, D, L, PN, TK, PP, S, TQ, FH, G, R)
    H = HEADS
    n_local = 2 * NJ + 3 * HJ + 3
    scratch = [
        VMEM((NJ, TK, B, 128), BF16),
        VMEM((NJ, PP, L, 128), F32),
        VMEM((L, 4, D), F32),
        VMEM((L, 4, D), F32),
        VMEM((L, D, 3 * D), BF16),
        VMEM((L, D, D), BF16),
        VMEM((L, 2, D, FH), BF16),
        VMEM((2, L, FH), F32),
        VMEM((L, 2, FH, D), BF16),
        VMEM((B, S, D), F32),
        VMEM((B * TQ, D), F32),
        VMEM((B * TQ, D), F32),
        VMEM((B * S, 3 * D), BF16),
        VMEM((B * TQ, D), BF16),
        VMEM((L, B * S, D), BF16),
        VMEM((L, B * TK, D), BF16),
        VMEM((L, B * S, 2), F32),
        VMEM((L, B * TQ, D), BF16),
        VMEM((L, B * S, D), BF16),
        VMEM((L, B * S, D), BF16),
        VMEM((L, B, H, TQ, S), BF16),
        VMEM((L, B * TQ, D), BF16),
        VMEM((L, B * TQ, D), BF16),
        VMEM((L, B * TK, 2 * FH), BF16),
        VMEM((L, 2 * G, HJ, PB, 128), BF16),
        VMEM((L, 2 * G, HJ, PB, 128), BF16),
        VMEM((L, R, HJ, PB, 128), BF16),
        VMEM((L, G, HJ, PB, 128), BF16),
        VMEM((L, PB, 128), F32),
        VMEM((L, G, PB, 128), F32),
        DMA((n_local,)),
        DMA((L, 4)),
        DMA((2, HJ + 1)),
        DMA((L, 2, 2)),
        DMA((L, 2)),
        DMA((L, 2)),
        DMA((L, 2)),
        DMA((L, 2)),
    ]
    any_spec = pl.BlockSpec(memory_space=pl.ANY)
    small = VMEM((HJ, PP, L, 128), F32)
    results = pl.pallas_call(
        functools.partial(main_kernel, dims),
        out_shape=(
            VMEM((NJ, TK, B, 128), BF16),
            VMEM((NJ, TK, B, 128), F32),
            VMEM((L, G, HJ, PB, 128), BF16),
            VMEM((L, G, PB, 128), F32),
            small,
            small,
            small,
        ),
        in_specs=[any_spec] * 12,
        scratch_shapes=scratch,
        compiler_params=pltpu.CompilerParams(
            collective_id=0, has_side_effects=True, vmem_limit_bytes=61 * 2**20
        ),
    )(
        native(tokens), native(cotangent), native(prompts), native(first_moment),
        native(second_moment), norm_params, bias_rows, qkv_weight, out_weight,
        up_weight, up_bias, down_weight,
    )
    act, igrad, grad, norm, new_first, new_second, new_prompts = finish(results, T, PN)
    return (
        native(act), native(igrad), native(grad), norm.reshape(()),
        native(new_first), native(new_second), native(new_prompts),
    )


def solution(mesh):
    ndp = mesh.shape["dp"]
    return jax.shard_map(
        functools.partial(local, ndp),
        mesh=mesh,
        in_specs=(
            P(("dp", "mlp"), None, None),
            P(("dp", "mlp"), None, None),
            P(None, None, "mlp"),
            P(None, None, "mlp"),
            P(None, None, "mlp"),
            P(),
            P(),
            P(),
            P(),
            P(None, None, "mlp"),
            P(None, "mlp"),
            P(None, "mlp", None),
        ),
        out_specs=(
            P(("dp", "mlp"), None, None),
            P(("dp", "mlp"), None, None),
            P(None, None, "mlp"),
            P(),
            P(None, None, "mlp"),
            P(None, None, "mlp"),
            P(None, None, "mlp"),
        ),
        check_vma=False,
    )
```
